512 devices in a mesh: line: 64 (over y, z_lo, core), bus: 8 (over x, z_hi).
Axes of the slice: x: 4, y: 8, z: 8 (z_hi: 2, z_lo: 4; z = z_hi * 4 + z_lo), core: 2. Of those that a mesh axis runs over, the one named last changes fastest.
Arguments:
- shift_factors: float32 [8192, 60416], P('line', 'bus'), may hold values from -2 to 2
- injection: float32 [32, 60416], P(None, 'bus'), may hold values from -0.046875 to 0.046875
- rating: float32 [8192], P('line'), may hold values from 0.5 to 4
- monitored: int32 [4096, 8], P('line'), may hold values from 0 to 63, all different within a row; in each aligned block of 64 rows (0 to 63, 64 to 127, ...) at most 12 rows name the same one
- live_count: int32 [4096], P('line'), may hold values from 4 to 8
- outage_offset: int32 [4096], P('line'), may hold values from 0 to 127
- outage_ends: int32 [4096, 2], P('line'), may hold values from 0 to 60415
Outputs:
- loading: float32 [4096, 8, 128], P('line', None, 'bus')
The draws below stay inside these ranges and needn't reach their ends.
Inputs may be any that keep to these rules, and one draw needn't show every extreme that they name: `monitored`: each row names 8 different blocks; among the 64 outages of one index of line (aligned blocks of rows) no block is named in more than 12 rows, and some block in exactly 12.
All inputs are finite; a program needn't handle non-finite values.
Results may differ from the reference program's by a relative error of at most 0.0003.
Values sent between devices are 32-bit elements; how exact they have to be, the bound alone decides.
No kernel may reach another device: no remote copies, remote signals or barrier semaphores. Data moves between devices by JAX's collectives and lax.ppermute only.
A program may use at most 64 MiB of HBM per device.

```python
import math
import jax
import jax.numpy as jnp
import numpy as np
from jax import lax

B = 60416
BLOCK = 128
HOURS = 32
OUT_DEV = 64
MB = 8
LINES = 8192
OUTAGES = 4096
MOST = 12
N_LINE = 64


def set_ends(drawn, rng, smallest, top_value):
    dims = drawn.shape
    index_at = [jax.random.randint(jax.random.fold_in(rng, axis), (), 0, dims[axis]) for axis in range(len(dims))]
    drawn = drawn.at[tuple(index_at)].set(smallest)
    longest = dims.index(max(dims))
    index_at[longest] = (index_at[longest] + 1) % dims[longest]
    return drawn.at[tuple(index_at)].set(top_value)


def level_of(key, shape, split, low, top_value):
    loudness = 1.0
    for axis_at, blocks in split:
        steps = jax.random.uniform(jax.random.fold_in(jax.random.fold_in(key, 6), axis_at), (blocks,), jnp.float32, low / len(split), top_value / len(split))
        loudness = loudness * jnp.repeat(jnp.exp(steps), shape[axis_at] // blocks).reshape((-1,) + (1,) * (len(shape) - 1 - axis_at))
    return loudness


def routed_block(rng, own, number, rows, amount, top, limit, lean):
    ranking = jax.random.permutation(rng, amount)
    heavy_load, common = portions_of(amount, rows * top, limit, lean, True), portions_of(amount, rows * top, limit, lean, False)
    places = jnp.arange(amount)

    def named(tallies, turn):
        used = int((tallies > 0).sum())
        fixed = max(1, used // 4)
        passed = fixed + (places - fixed + turn * (used - fixed)) % max(1, amount - fixed)
        return jnp.zeros((amount,), jnp.int32).at[ranking[jnp.where(places < fixed, places, passed)]].set(jnp.asarray(tallies, jnp.int32))

    tallies = jnp.where(number % 4 == 0, named(heavy_load, number // 4), named(common, number - number // 4 - 1))
    mixed = jax.random.permutation(jax.random.fold_in(own, 3), amount)
    giver, sink = mixed[0:amount // 2 * 2:2], mixed[1:amount // 2 * 2:2]
    room = jnp.minimum(tallies[giver] - 1, limit - tallies[sink]) // 2
    room = jnp.where((giver == ranking[0]) | (sink == ranking[0]) | (tallies[sink] == 0), 0, jnp.maximum(room, 0))
    passed = jax.random.randint(jax.random.fold_in(own, 4), (amount // 2,), 0, 1 << 20) % (room + 1)
    tallies = tallies.at[giver].add(-passed).at[sink].add(passed)
    items = jnp.searchsorted(jnp.cumsum(tallies), jnp.arange(rows * top), side="right").astype(jnp.int32)
    grid = items.reshape(top, rows).T
    grid = grid[jax.random.permutation(jax.random.fold_in(own, 1), rows)]
    turn = jax.random.randint(jax.random.fold_in(own, 2), (rows, 1), 0, top)
    return jnp.take_along_axis(grid, (jnp.arange(top)[None, :] + turn) % top, axis=1)


def portions_of(number_of, total, reach, skew, full):
    portions = [(1 << 20) // math.isqrt(standing ** skew) + 1 for standing in range(1, number_of + 1)]
    largest = reach if full else min(reach, max(-(-total // number_of), total * portions[0] // sum(portions)))
    least = 1 if total - largest >= number_of - 1 else 0
    counts, surplus = [largest] + [least] * (number_of - 1), total - largest - least * (number_of - 1)
    while surplus > 0:
        candidates = [i for i in range(1, number_of) if counts[i] < largest] or [i for i in range(1, number_of) if counts[i] < reach]
        mass, budget = sum([portions[i] for i in candidates]), surplus
        for i in candidates:
            more = min(reach - counts[i], max(1, budget * portions[i] // mass), surplus)
            counts[i] = counts[i] + more
            surplus = surplus - more
    return np.array(counts)


def normal_values(own_key, dims, width, bound, cuts=(), kind=jnp.bfloat16):
    array = width * jax.random.normal(own_key, dims, jnp.float32)
    if cuts:
        array = array * level_of(own_key, dims, cuts, -0.22, 0.18)
    return jnp.clip(array, -bound, bound).astype(kind)


def setup_inputs(seed: int = 0) -> dict:
    key_list = jax.random.split(jax.random.key(seed), 8)
    shift_factors = normal_values(key_list[0], (LINES, B), 0.5, 2.0, ((0, 64), (1, 8)), jnp.float32)
    injection = normal_values(key_list[1], (HOURS, B), (B // 4) ** -0.5, 0.046875, ((1, 8),), jnp.float32)
    rating = jnp.clip(jnp.exp(math.log(4.0) - 2.0794415 * jax.random.uniform(key_list[2], (LINES,), jnp.float32) ** level_of(key_list[2], (LINES,), ((0, 64),), -0.2, 0.2)), 0.5, 4.0)
    monitored_keys = jax.random.split(jax.random.fold_in(key_list[3], 1), OUTAGES // OUT_DEV)
    monitored_turns = jax.random.permutation(jax.random.fold_in(key_list[3], 3), OUTAGES // OUT_DEV)
    monitored = jax.vmap(lambda own, number: routed_block(jax.random.fold_in(key_list[3], 2), own, number, OUT_DEV, N_LINE, MB, MOST, 2))(monitored_keys, monitored_turns).reshape((OUTAGES, MB))
    live_count = set_ends(jax.random.randint(key_list[4], (OUTAGES,), MB // 2, MB + 1), jax.random.fold_in(key_list[4], 1), MB // 2, MB).astype(jnp.int32)
    outage_offset = set_ends(jax.random.randint(key_list[5], (OUTAGES,), 0, BLOCK), jax.random.fold_in(key_list[5], 1), 0, BLOCK - 1).astype(jnp.int32)
    outage_ends = set_ends(jax.random.randint(key_list[6], (OUTAGES, 2), 0, B), jax.random.fold_in(key_list[6], 1), 0, B - 1).astype(jnp.int32)
    return {"shift_factors": shift_factors, "injection": injection, "rating": rating, "monitored": monitored, "live_count": live_count, "outage_offset": outage_offset, "outage_ends": outage_ends}


floor_value = 0.25


def reference(shift_factors, injection, rating, monitored, live_count, outage_offset, outage_ends):
    flows = lax.dot_general(shift_factors, injection, (((1,), (1,)), ((), ())), precision=lax.Precision.HIGHEST, preferred_element_type=jnp.float32)
    outaged = (monitored[:, 0] * BLOCK + outage_offset).astype(jnp.int32)
    from_bus = outage_ends[:, 0]
    to_bus = outage_ends[:, 1]
    self_sens = shift_factors[outaged, from_bus] - shift_factors[outaged, to_bus]
    divisor_all = jnp.maximum(1.0 - self_sens, floor_value)
    lost_all = flows[outaged]
    offsets = jnp.arange(BLOCK, dtype=jnp.int32)
    slot_index = jnp.arange(MB, dtype=jnp.int32)

    def screen_outage(packed):
        block_ids, live_slots, line_lost, from_one, to_one, divisor, lost_flow = packed
        line_rows = (block_ids[:, None] * BLOCK + offsets[None, :]).astype(jnp.int32)
        sensitivity = shift_factors[line_rows, from_one] - shift_factors[line_rows, to_one]
        post_flow = flows[line_rows] + (sensitivity / divisor)[:, :, None] * lost_flow[None, None, :]
        post_flow = jnp.where((line_rows == line_lost)[:, :, None], 0.0, post_flow)
        loading = jnp.max(jnp.abs(post_flow), axis=2) / rating[line_rows]
        return jnp.where((slot_index < live_slots)[:, None], loading, 0.0)

    return lax.map(screen_outage, (monitored, live_count, outaged, from_bus, to_bus, divisor_all, lost_all))
```

```python
import functools

import jax
import jax.numpy as jnp
from jax import lax
from jax.experimental import pallas as pl
from jax.experimental.pallas import tpu as pltpu
from jax.sharding import PartitionSpec as P

floor_value = 0.25
F32 = jnp.float32
BF16 = jnp.bfloat16
NT = (((1,), (1,)), ((), ()))
TN = (((0,), (0,)), ((), ()))
HOURS = 32
CAP = 12
CHUNK = 512


def iota(shape, axis):
    return lax.broadcasted_iota(jnp.int32, shape, axis)


def split2(value):
    high = value.astype(BF16)
    return high, (value - high.astype(F32)).astype(BF16)


def request_kernel(mon_ref, ends_ref, off_ref, out_ref):
    outages, slots = mon_ref.shape
    lane = iota((outages, 128), 1)
    names = jnp.zeros((outages, 128), F32)
    for s in range(slots):
        names = jnp.where(mon_ref[:, s : s + 1] == lane, 1.0, names)
    before = jnp.where(iota((outages, outages), 1) < iota((outages, outages), 0), 1.0, 0.0)
    rank = lax.dot_general(
        before.astype(BF16), names.astype(BF16), (((1,), (0,)), ((), ())), preferred_element_type=F32
    )
    square_row, square_lane = iota((outages, outages), 0), iota((outages, outages), 1)
    off = jnp.sum(jnp.where(square_row == square_lane, off_ref[...], 0), axis=1, keepdims=True)
    ones = jnp.ones((outages, 128), jnp.int32)
    start = (ends_ref[:, 0:1] + 1) * ones
    end = (ends_ref[:, 1:2] + 1) * ones
    place = (off + 1) * ones
    chosen, values = [], []
    for c in range(CAP):
        chosen.append(jnp.where(rank == float(c), names, 0.0).astype(BF16))
        value = jnp.where(lane == c, start, jnp.where(lane == 16 + c, end, jnp.where(lane == 32 + c, place, 0)))
        values.append(
            jnp.concatenate([(value >> 8).astype(F32), (value & 255).astype(F32)], axis=1).astype(BF16)
        )
    both = lax.dot_general(
        jnp.concatenate(chosen, axis=0), jnp.concatenate(values, axis=0), TN, preferred_element_type=F32
    )
    packed = 256.0 * both[:, :128] + both[:, 128:]
    out_ref[...] = packed[: out_ref.shape[0]]


def flow_kernel(s_ref, inj_ref, split_ref, part_ref):
    rows, width = s_ref.shape
    total = jnp.zeros((2 * HOURS, 2 * rows), F32)

    def step(at, size, total):
        cols = pl.ds(at, size)
        s_high, s_low = split2(s_ref[:, cols])
        both = jnp.concatenate([s_high, s_low], axis=0)
        split_ref[:, cols] = both
        i_high, i_low = split2(inj_ref[:, cols])
        return total + lax.dot_general(
            jnp.concatenate([i_high, i_low], axis=0), both, NT, preferred_element_type=F32
        )

    whole = width // CHUNK
    total = lax.fori_loop(0, whole, lambda q, t: step(pl.multiple_of(q * CHUNK, CHUNK), CHUNK, t), total)
    if width % CHUNK:
        total = step(whole * CHUNK, width % CHUNK, total)
    part_ref[...] = (
        total[:HOURS, :rows] + (total[:HOURS, rows:] + total[HOURS:, :rows]) + total[HOURS:, rows:]
    )


def pick_kernel(req_ref, split_ref, part_ref, out_ref, from_ref, to_ref, sum_ref):
    lines = req_ref.shape[0]
    both_rows, width = split_ref.shape
    rows = both_rows // 2
    buses, _, entries = out_ref.shape
    sub = rows // buses
    base = lax.axis_index("bus") * width + 1
    req = req_ref[...]
    lane = iota((lines, 128), 1)
    for c in range(CAP):
        first = req[:, c : c + 1].astype(jnp.int32) - base
        second = req[:, 16 + c : 17 + c].astype(jnp.int32) - base
        same = first == second
        first = jnp.where(same, -1, first)
        second = jnp.where(same, -1, second)
        from_ref[c * lines : (c + 1) * lines, :] = jnp.broadcast_to(first, (lines, 128))
        to_ref[c * lines : (c + 1) * lines, :] = jnp.broadcast_to(second, (lines, 128))
    sum_ref[...] = jnp.zeros_like(sum_ref)

    def step(at, size):
        columns = []
        for t in range(size // 128):
            spot = iota((entries, 128), 1) + (at + t * 128)
            hot = jnp.where(from_ref[...] == spot, 1.0, jnp.where(to_ref[...] == spot, -1.0, 0.0))
            columns.append(hot.astype(BF16))
        sum_ref[...] += lax.dot_general(
            jnp.concatenate(columns, axis=1), split_ref[:, pl.ds(at, size)], NT, preferred_element_type=F32
        )

    whole = width // CHUNK

    def body(q, carry):
        step(pl.multiple_of(q * CHUNK, CHUNK), CHUNK)
        return carry

    lax.fori_loop(0, whole, body, 0)
    if width % CHUNK:
        step(whole * CHUNK, width % CHUNK)
    picked = sum_ref[:, :rows] + sum_ref[:, rows:]
    own = jnp.zeros((lines, 128), F32)
    for c in range(CAP):
        off = req[:, 32 + c : 33 + c].astype(jnp.int32) - 1
        value = jnp.sum(
            jnp.where(lane == off, picked[c * lines : (c + 1) * lines], 0.0), axis=1, keepdims=True
        )
        own = jnp.where(lane == c, value, own)
    turned = jnp.transpose(picked)
    own_turned = jnp.transpose(jnp.concatenate([own, jnp.zeros((128 - lines, 128), F32)], axis=0))
    part = part_ref[...]
    extra = jnp.concatenate(
        [part[8 * t : 8 * t + 8] for t in range(4)] + [own_turned[0:8], own_turned[8:16]], axis=1
    )
    for b in range(buses):
        out_ref[b, :sub, :] = turned[b * sub : (b + 1) * sub]
        out_ref[b, sub:, :] = extra


def reply_kernel(got_ref, req_ref, rate_ref, out_ref, rate_scratch):
    buses, _, _ = got_ref.shape
    lines = req_ref.shape[0]
    rows = rate_ref.shape[1]
    sub = rows // buses
    place = lax.axis_index("bus")
    total = got_ref[0]
    for b in range(1, buses):
        total = total + got_ref[b]
    flows = jnp.concatenate([total[sub : sub + 8, 128 * t : 128 * t + 128] for t in range(4)], axis=0)
    lane = iota((HOURS, 128), 1)
    hour = iota((HOURS, 128), 0)
    wanted = iota((128, 128), 0) == place * sub + iota((128, 128), 1) % sub
    select = jnp.where(wanted, 1.0, 0.0).astype(BF16)
    f_high, f_low = split2(flows)
    f_rest = (flows - f_high.astype(F32) - f_low.astype(F32)).astype(BF16)
    spread = lax.dot_general(
        jnp.concatenate([f_high, f_low, f_rest], axis=0),
        select,
        (((1,), (0,)), ((), ())),
        preferred_element_type=F32,
    )
    spread = spread[:HOURS] + spread[HOURS : 2 * HOURS] + spread[2 * HOURS :]
    spread = jnp.where(lane // sub == hour % 8, spread, 0.0)
    for t in range(4):
        row = jnp.sum(spread[8 * t : 8 * t + 8], axis=0, keepdims=True)
        out_ref[:, 128 * t : 128 * t + 128] = jnp.broadcast_to(row, (lines, 128))
    req = req_ref[...]
    lane_line = iota((lines, 128), 1)
    hots = [
        jnp.where(lane_line == req[:, 32 + c : 33 + c].astype(jnp.int32) - 1, 1.0, 0.0).astype(BF16)
        for c in range(CAP)
    ]
    left = jnp.concatenate([jnp.concatenate(hots[4 * q : 4 * q + 4], axis=1) for q in range(3)], axis=0)

    def diagonal(block):
        blank = jnp.zeros_like(block)
        return jnp.concatenate(
            [jnp.concatenate([block if v == u else blank for v in range(4)], axis=1) for u in range(4)], axis=0
        )

    lost = lax.dot_general(
        left, diagonal(f_high), NT, preferred_element_type=F32
    ) + lax.dot_general(left, diagonal(f_low), NT, preferred_element_type=F32)
    for q in range(3):
        out_ref[:, 512 + 128 * q : 640 + 128 * q] = lost[q * lines : (q + 1) * lines]
    rate_scratch[...] = jnp.transpose(jnp.broadcast_to(rate_ref[...], (128, 128)))
    rate = rate_scratch[pl.ds(pl.multiple_of(place * sub, sub), sub), :]
    sens = total[:sub]

    def wide(block):
        return jnp.concatenate([block, jnp.zeros((block.shape[0], 128 - lines), F32)], axis=1)

    blocks = [wide(sens[:, c * lines : (c + 1) * lines]) for c in range(CAP)]
    one = jnp.concatenate(blocks[:8], axis=0)
    two = jnp.concatenate(
        blocks[8:] + [total[sub : sub + 8, 512:640], total[sub : sub + 8, 640:768], rate, jnp.zeros((32, 128), F32)],
        axis=0,
    )
    out_ref[:, 896:1024] = jnp.transpose(one)[:lines]
    out_ref[:, 1024:1152] = jnp.transpose(two)[:lines]


def screen_kernel(got_ref, mon_ref, off_ref, live_ref, out_ref):
    lines = got_ref.shape[0]
    outages, slots = mon_ref.shape
    sub = out_ref.shape[1]
    place = lax.axis_index("bus")
    pieces = []
    for t in range(9):
        block = got_ref[:, 128 * t : 128 * t + 128]
        high = block.astype(BF16).astype(F32)
        low = (block - high).astype(BF16).astype(F32)
        pieces.append(jnp.transpose(jnp.concatenate([high, low], axis=0)).astype(BF16))
    shared = jnp.concatenate(pieces[:4] + pieces[7:], axis=0)
    own = jnp.concatenate(pieces[4:7] + pieces[8:], axis=0)
    mon = jnp.concatenate([mon_ref[...].astype(F32), jnp.zeros((outages, 128 - slots), F32)], axis=1)
    named = jnp.transpose(jnp.concatenate([mon, mon], axis=0))[:slots].astype(jnp.int32)
    line_row = iota((lines, 128), 0)
    lane = iota((1, 128), 1)
    outage = lane % outages
    names = jnp.zeros((lines, 128), F32)
    for s in range(slots):
        names = jnp.where(named[s : s + 1] == line_row, 1.0, names)
    earlier = iota((128, 128), 0) < iota((128, 128), 1) % outages
    rank = lax.dot_general(
        names.astype(BF16),
        jnp.where(earlier, 1.0, 0.0).astype(BF16),
        (((1,), (0,)), ((), ())),
        preferred_element_type=F32,
    )

    def hot_of(target):
        hot = jnp.where(line_row == target, 1.0, 0.0)
        turn = jnp.sum(hot * rank, axis=0, keepdims=True)
        hot = hot.astype(BF16)
        return jnp.concatenate([hot, hot], axis=0), turn

    plain = (((1,), (0,)), ((), ()))
    hot_own, turn_own = hot_of(named[0:1])
    got_own = lax.dot_general(own, hot_own, plain, preferred_element_type=F32)
    lost = jnp.zeros((HOURS, 128), F32)
    self_sens = jnp.zeros((1, 128), F32)
    for c in range(CAP):
        mine = turn_own == float(c)
        lost = jnp.where(mine, got_own[HOURS * c : HOURS * c + HOURS], lost)
        self_sens = jnp.where(mine, got_own[448 + c : 449 + c], self_sens)
    divisor = jnp.maximum(1.0 - self_sens, floor_value)
    off = jnp.concatenate([off_ref[...], off_ref[...]], axis=1)
    live = jnp.concatenate([live_ref[...], live_ref[...]], axis=1)
    lost_scaled = lost
    row = iota((sub, 128), 0)
    for t in range(slots // 2):
        target = jnp.where(lane < outages, named[2 * t : 2 * t + 1], named[2 * t + 1 : 2 * t + 2])
        hot, turn = hot_of(target)
        got = lax.dot_general(shared, hot, plain, preferred_element_type=F32)
        sens = jnp.zeros((sub, 128), F32)
        for c in range(CAP):
            sens = jnp.where(turn == float(c), got[512 + sub * c : 512 + sub * c + sub], sens)
        factor = sens / divisor
        worst = jnp.zeros((sub, 128), F32)
        for h in range(HOURS):
            worst = jnp.maximum(worst, jnp.abs(got[sub * h : sub * h + sub] + factor * lost_scaled[h : h + 1]))
        result = worst / got[720:736]
        slot = 2 * t + jnp.where(lane < outages, 0, 1)
        keep = slot < live
        if t == 0:
            keep = keep & ~((slot == 0) & (row == off - place * sub))
        result = jnp.where(keep, result, 0.0)
        turned = jnp.transpose(jnp.concatenate([result, jnp.zeros((128 - sub, 128), F32)], axis=0))
        out_ref[pl.ds(2 * t, outages, stride=slots), :] = turned[:outages, :sub]
        out_ref[pl.ds(2 * t + 1, outages, stride=slots), :] = turned[outages:, :sub]


def call(kernel, out_shape, scratch=(), flops=0, moved=0):
    single = not isinstance(out_shape, (tuple, list))
    spec = pl.BlockSpec(memory_space=pltpu.VMEM)
    return pl.pallas_call(
        kernel,
        out_shape=out_shape,
        out_specs=spec if single else tuple(spec for _ in out_shape),
        scratch_shapes=list(scratch),
        compiler_params=pltpu.CompilerParams(vmem_limit_bytes=32 * 1024 * 1024),
        cost_estimate=pl.CostEstimate(flops=flops, bytes_accessed=moved, transcendentals=0),
    )


def local(shift_factors, injection, rating, monitored, live_count, outage_offset, outage_ends):
    bus_count = lax.axis_size("bus")
    line_count = lax.axis_size("line")
    block_rows, bus_width = shift_factors.shape
    sub_rows = block_rows // bus_count
    outages, slot_count = monitored.shape
    entries = CAP * line_count
    shape = jax.ShapeDtypeStruct
    off_row = outage_offset.reshape(1, outages)
    live_row = live_count.reshape(1, outages)
    rate_row = rating.reshape(1, block_rows)
    with jax.named_scope("requests"):
        requests = call(request_kernel, shape((line_count, 128), F32))(monitored, outage_ends, off_row)
        asked = lax.all_to_all(requests, "line", split_axis=0, concat_axis=0, tiled=True)
    with jax.named_scope("flows"):
        split, part = call(
            flow_kernel,
            (shape((2 * block_rows, bus_width), BF16), shape((HOURS, block_rows), F32)),
            flops=8 * HOURS * block_rows * bus_width,
            moved=3 * 4 * block_rows * bus_width,
        )(shift_factors, injection)
    with jax.named_scope("picks"):
        partial_sens = call(
            pick_kernel,
            shape((bus_count, sub_rows + 8, entries), F32),
            scratch=(
                pltpu.VMEM((entries, 128), jnp.int32),
                pltpu.VMEM((entries, 128), jnp.int32),
                pltpu.VMEM((entries, 2 * block_rows), F32),
            ),
            flops=4 * entries * block_rows * bus_width,
            moved=4 * block_rows * bus_width,
        )(asked, split, part)
        sens = lax.all_to_all(partial_sens, "bus", split_axis=0, concat_axis=0, tiled=True)
    with jax.named_scope("reply"):
        reply = call(reply_kernel, shape((line_count, 1152), F32), scratch=(pltpu.VMEM((128, 128), F32),))(
            sens, asked, rate_row
        )
        got = lax.all_to_all(reply, "line", split_axis=0, concat_axis=0, tiled=True)
    with jax.named_scope("screen"):
        loading = call(screen_kernel, shape((outages * slot_count, sub_rows), F32))(
            got, monitored, off_row, live_row
        )
    return loading.reshape(outages, slot_count, sub_rows)


def solution(mesh):
    return jax.shard_map(
        local,
        mesh=mesh,
        in_specs=(
            P("line", "bus"),
            P(None, "bus"),
            P("line"),
            P("line", None),
            P("line"),
            P("line"),
            P("line", None),
        ),
        out_specs=P("line", None, "bus"),
        check_vma=False,
    )
```

```python
import jax
import jax.numpy as jnp
from jax import lax
from jax.experimental import pallas as pl
from jax.experimental.pallas import tpu as pltpu
from jax.sharding import PartitionSpec as P

floor_value = 0.25
F32 = jnp.float32
BF16 = jnp.bfloat16
NT = (((1,), (1,)), ((), ()))
NN = (((1,), (0,)), ((), ()))
HOURS = 32
CAP = 12
CHUNK = 1920
PEERS = 4
PASS = 2


def iota(shape, axis):
    return lax.broadcasted_iota(jnp.int32, shape, axis)


def split2(value):
    high = value.astype(BF16)
    return high, (value - high.astype(F32)).astype(BF16)


def request_kernel(mon_ref, ends_ref, off_ref, out_ref):
    slots, outages = mon_ref.shape
    lines = out_ref.shape[0]

    def twice(row):
        return jnp.concatenate([row, row], axis=1)

    named = twice(mon_ref[...])
    line_row = iota((lines, 128), 0)
    names = jnp.zeros((lines, 128), F32)
    for s in range(slots):
        names = jnp.where(named[s : s + 1] == line_row, 1.0, names)
    earlier = iota((128, 128), 0) < iota((128, 128), 1) % outages
    rank = lax.dot_general(
        names.astype(BF16), jnp.where(earlier, 1.0, 0.0).astype(BF16), NN, preferred_element_type=F32
    )
    rank = jnp.where(names > 0.0, rank, -1.0)
    start = twice(ends_ref[0:1, :]) + 1
    end = twice(ends_ref[1:2, :]) + 1
    place = twice(off_ref[...]) + 1
    second = iota((1, 128), 1) // outages
    spot = iota((128, 128), 0)
    chosen, high, low = [], [], []
    for t in range(CAP // 2):
        turn = 2 * t + second
        chosen.append(jnp.where(rank == turn.astype(F32), 1.0, 0.0).astype(BF16))
        value = jnp.where(
            spot == turn, start, jnp.where(spot == 16 + turn, end, jnp.where(spot == 32 + turn, place, 0))
        )
        high.append((value >> 8).astype(F32).astype(BF16))
        low.append((value & 255).astype(F32).astype(BF16))
    chosen = jnp.concatenate(chosen, axis=1)
    high = lax.dot_general(chosen, jnp.concatenate(high, axis=1), NT, preferred_element_type=F32)
    low = lax.dot_general(chosen, jnp.concatenate(low, axis=1), NT, preferred_element_type=F32)
    out_ref[...] = 256.0 * high + low


def pick_kernel(req_ref, s_ref, inj_ref, out_ref, from_ref, to_ref, sum_ref, flow_ref):
    lines = req_ref.shape[0]
    rows, width = s_ref.shape
    peers, _, entries = out_ref.shape
    deep = rows // peers
    base = lax.axis_index("bus") * width + 1
    req = req_ref[...]
    lane = iota((lines, 128), 1)
    for c in range(CAP):
        first = req[:, c : c + 1].astype(jnp.int32) - base
        second = req[:, 16 + c : 17 + c].astype(jnp.int32) - base
        same = first == second
        first = jnp.where(same | (first < 0) | (first >= width), -1, first)
        second = jnp.where(same | (second < 0) | (second >= width), -1, second)
        from_ref[c * lines : (c + 1) * lines, :] = jnp.broadcast_to(first, (lines, 128)).astype(jnp.int16)
        to_ref[c * lines : (c + 1) * lines, :] = jnp.broadcast_to(second, (lines, 128)).astype(jnp.int16)
    sum_ref[...] = jnp.zeros_like(sum_ref)
    flow_ref[...] = jnp.zeros_like(flow_ref)
    one, minus, zero = jnp.asarray(1, BF16), jnp.asarray(-1, BF16), jnp.asarray(0, BF16)

    def step(at, size):
        columns = []
        for t in range(size // 128):
            spot = (iota((16, 128), 1) + (at + t * 128)).astype(jnp.int16)
            spot = jnp.broadcast_to(spot[None], (entries // 16, 16, 128)).reshape(entries, 128)
            columns.append(
                jnp.where(from_ref[...] == spot, one, jnp.where(to_ref[...] == spot, minus, zero))
            )
        cols = pl.ds(at, size)
        s_high, s_low = split2(s_ref[:, cols])
        both = jnp.concatenate([s_high, s_low], axis=0)
        i_high, i_low = split2(inj_ref[:, cols])
        sum_ref[...] += lax.dot_general(
            jnp.concatenate(columns, axis=1), both, NT, preferred_element_type=F32
        )
        flow_ref[...] += lax.dot_general(
            jnp.concatenate([i_high, i_low], axis=0), both, NT, preferred_element_type=F32
        )

    whole = width // CHUNK

    def body(q, carry):
        step(pl.multiple_of(q * CHUNK, CHUNK), CHUNK)
        return carry

    lax.fori_loop(0, whole, body, 0)
    if width % CHUNK:
        step(whole * CHUNK, width % CHUNK)
    part = (
        flow_ref[:HOURS, :rows]
        + (flow_ref[:HOURS, rows:] + flow_ref[HOURS:, :rows])
        + flow_ref[HOURS:, rows:]
    )
    picked = sum_ref[:, :rows] + sum_ref[:, rows:]
    own = jnp.zeros((lines, 128), F32)
    for c in range(CAP):
        off = req[:, 32 + c : 33 + c].astype(jnp.int32) - 1
        value = jnp.sum(
            jnp.where(lane == off, picked[c * lines : (c + 1) * lines], 0.0), axis=1, keepdims=True
        )
        own = jnp.where(lane == c, value, own)
    turned = jnp.transpose(picked)
    own_turned = jnp.transpose(jnp.concatenate([own, jnp.zeros((128 - lines, 128), F32)], axis=0))
    extra = jnp.concatenate(
        [part[8 * t : 8 * t + 8] for t in range(4)] + [own_turned[0:8], own_turned[8:16]], axis=1
    )
    for b in range(peers):
        out_ref[b, :deep, :] = turned[b * deep : (b + 1) * deep]
        out_ref[b, deep:, :] = extra


def sum_kernel(got_ref, out_ref):
    peers, deep, _ = out_ref.shape
    rows = deep - 8
    total = got_ref[0]
    for b in range(1, got_ref.shape[0]):
        total = total + got_ref[b]
    for b in range(peers):
        out_ref[b, :rows, :] = total[b * rows : (b + 1) * rows]
        out_ref[b, rows:, :] = total[peers * rows :]


def reply_kernel(got_ref, req_ref, rate_ref, out_ref, rate_scratch):
    sub = got_ref.shape[1] - 8
    lines = req_ref.shape[0]
    place = lax.axis_index("bus")
    total = got_ref[0]
    for b in range(1, got_ref.shape[0]):
        total = total + got_ref[b]
    flows = jnp.concatenate([total[sub : sub + 8, 128 * t : 128 * t + 128] for t in range(4)], axis=0)
    lane = iota((HOURS, 128), 1)
    hour = iota((HOURS, 128), 0)
    wanted = iota((128, 128), 0) == place * sub + iota((128, 128), 1) % sub
    select = jnp.where(wanted, 1.0, 0.0).astype(BF16)
    f_high, f_low = split2(flows)
    f_rest = (flows - f_high.astype(F32) - f_low.astype(F32)).astype(BF16)
    spread = lax.dot_general(
        jnp.concatenate([f_high, f_low, f_rest], axis=0),
        select,
        (((1,), (0,)), ((), ())),
        preferred_element_type=F32,
    )
    spread = spread[:HOURS] + spread[HOURS : 2 * HOURS] + spread[2 * HOURS :]
    spread = jnp.where(lane // sub == hour % 8, spread, 0.0)
    for t in range(4):
        row = jnp.sum(spread[8 * t : 8 * t + 8], axis=0, keepdims=True)
        out_ref[:, 128 * t : 128 * t + 128] = jnp.broadcast_to(row, (lines, 128))
    req = req_ref[...]
    lane_line = iota((lines, 128), 1)
    hots = [
        jnp.where(lane_line == req[:, 32 + c : 33 + c].astype(jnp.int32) - 1, 1.0, 0.0).astype(BF16)
        for c in range(CAP)
    ]
    left = jnp.concatenate([jnp.concatenate(hots[4 * q : 4 * q + 4], axis=1) for q in range(3)], axis=0)

    def diagonal(block):
        blank = jnp.zeros_like(block)
        return jnp.concatenate(
            [jnp.concatenate([block if v == u else blank for v in range(4)], axis=1) for u in range(4)], axis=0
        )

    lost = lax.dot_general(
        left, diagonal(f_high), NT, preferred_element_type=F32
    ) + lax.dot_general(left, diagonal(f_low), NT, preferred_element_type=F32)
    for q in range(3):
        out_ref[:, 512 + 128 * q : 640 + 128 * q] = lost[q * lines : (q + 1) * lines]
    rate_scratch[...] = jnp.transpose(jnp.broadcast_to(rate_ref[...], (128, 128)))
    rate = rate_scratch[pl.ds(pl.multiple_of(place * sub, sub), sub), :]
    sens = total[:sub]

    def wide(block):
        return jnp.concatenate([block, jnp.zeros((block.shape[0], 128 - lines), F32)], axis=1)

    blocks = [wide(sens[:, c * lines : (c + 1) * lines]) for c in range(CAP)]
    one = jnp.concatenate(blocks[:8], axis=0)
    two = jnp.concatenate(
        blocks[8:] + [total[sub : sub + 8, 512:640], total[sub : sub + 8, 640:768], rate, jnp.zeros((32, 128), F32)],
        axis=0,
    )
    out_ref[:, 896:1024] = jnp.transpose(one)[:lines]
    out_ref[:, 1024:1152] = jnp.transpose(two)[:lines]


def screen_kernel(got_ref, mon_ref, off_ref, live_ref, out_ref):
    lines = got_ref.shape[0]
    slots, outages = mon_ref.shape
    sub = out_ref.shape[1]
    place = lax.axis_index("bus")
    pieces = []
    for t in range(9):
        block = got_ref[:, 128 * t : 128 * t + 128]
        high = block.astype(BF16).astype(F32)
        low = (block - high).astype(BF16).astype(F32)
        pieces.append(jnp.transpose(jnp.concatenate([high, low], axis=0)).astype(BF16))
    shared = jnp.concatenate(pieces[:4] + pieces[7:], axis=0)
    own = jnp.concatenate(pieces[4:7] + pieces[8:], axis=0)
    named = jnp.concatenate([mon_ref[...], mon_ref[...]], axis=1)
    line_row = iota((lines, 128), 0)
    lane = iota((1, 128), 1)
    outage = lane % outages
    names = jnp.zeros((lines, 128), F32)
    for s in range(slots):
        names = jnp.where(named[s : s + 1] == line_row, 1.0, names)
    earlier = iota((128, 128), 0) < iota((128, 128), 1) % outages
    rank = lax.dot_general(
        names.astype(BF16),
        jnp.where(earlier, 1.0, 0.0).astype(BF16),
        (((1,), (0,)), ((), ())),
        preferred_element_type=F32,
    )

    def hot_of(target):
        hot = jnp.where(line_row == target, 1.0, 0.0)
        turn = jnp.sum(hot * rank, axis=0, keepdims=True)
        hot = hot.astype(BF16)
        return jnp.concatenate([hot, hot], axis=0), turn

    plain = (((1,), (0,)), ((), ()))
    hot_own, turn_own = hot_of(named[0:1])
    got_own = lax.dot_general(own, hot_own, plain, preferred_element_type=F32)
    lost = jnp.zeros((HOURS, 128), F32)
    self_sens = jnp.zeros((1, 128), F32)
    for c in range(CAP):
        mine = turn_own == float(c)
        lost = jnp.where(mine, got_own[HOURS * c : HOURS * c + HOURS], lost)
        self_sens = jnp.where(mine, got_own[448 + c : 449 + c], self_sens)
    divisor = jnp.maximum(1.0 - self_sens, floor_value)
    off = jnp.concatenate([off_ref[...], off_ref[...]], axis=1)
    live = jnp.concatenate([live_ref[...], live_ref[...]], axis=1)
    lost_scaled = lost
    row = iota((sub, 128), 0)
    for t in range(slots // 2):
        target = jnp.where(lane < outages, named[2 * t : 2 * t + 1], named[2 * t + 1 : 2 * t + 2])
        hot, turn = hot_of(target)
        got = lax.dot_general(shared, hot, plain, preferred_element_type=F32)
        sens = jnp.zeros((sub, 128), F32)
        for c in range(CAP):
            sens = jnp.where(turn == float(c), got[512 + sub * c : 512 + sub * c + sub], sens)
        factor = sens / divisor
        worst = jnp.zeros((sub, 128), F32)
        for h in range(HOURS):
            worst = jnp.maximum(worst, jnp.abs(got[sub * h : sub * h + sub] + factor * lost_scaled[h : h + 1]))
        result = worst / got[720:736]
        slot = 2 * t + jnp.where(lane < outages, 0, 1)
        keep = slot < live
        if t == 0:
            keep = keep & ~((slot == 0) & (row == off - place * sub))
        result = jnp.where(keep, result, 0.0)
        out_ref[2 * t] = result[:, :outages]
        out_ref[2 * t + 1] = result[:, outages:]


def call(kernel, out_shape, scratch=(), flops=0, moved=0):
    single = not isinstance(out_shape, (tuple, list))
    spec = pl.BlockSpec(memory_space=pltpu.VMEM)
    return pl.pallas_call(
        kernel,
        out_shape=out_shape,
        out_specs=spec if single else tuple(spec for _ in out_shape),
        scratch_shapes=list(scratch),
        compiler_params=pltpu.CompilerParams(vmem_limit_bytes=32 * 1024 * 1024),
        cost_estimate=pl.CostEstimate(flops=flops, bytes_accessed=moved, transcendentals=0),
    )


def local(shift_factors, injection, rating, monitored, live_count, outage_offset, outage_ends):
    bus_count = lax.axis_size("bus")
    line_count = lax.axis_size("line")
    block_rows, bus_width = shift_factors.shape
    sub_rows = block_rows // bus_count
    outages, slot_count = monitored.shape
    entries = CAP * line_count
    shape = jax.ShapeDtypeStruct
    groups_x = [[first + other * PASS for other in range(PEERS)] for first in range(PASS)]
    groups_z = [[PASS * first + other for other in range(PASS)] for first in range(PEERS)]
    off_row = outage_offset.reshape(1, outages)
    live_row = live_count.reshape(1, outages)
    rate_row = rating.reshape(1, block_rows)
    named = monitored.T
    with jax.named_scope("requests"):
        requests = call(request_kernel, shape((line_count, 128), F32))(named, outage_ends.T, off_row)
        asked = lax.all_to_all(requests, "line", split_axis=0, concat_axis=0, tiled=True)
    with jax.named_scope("picks"):
        partial_sens = call(
            pick_kernel,
            shape((PEERS, PASS * sub_rows + 8, entries), F32),
            scratch=(
                pltpu.VMEM((entries, 128), jnp.int16),
                pltpu.VMEM((entries, 128), jnp.int16),
                pltpu.VMEM((entries, 2 * block_rows), F32),
                pltpu.VMEM((2 * HOURS, 2 * block_rows), F32),
            ),
            flops=4 * entries * block_rows * bus_width,
            moved=4 * block_rows * bus_width,
        )(asked, shift_factors, injection)
        partial_sens = lax.all_to_all(
            partial_sens, "bus", split_axis=0, concat_axis=0, tiled=True, axis_index_groups=groups_x
        )
    with jax.named_scope("sums"):
        half = call(sum_kernel, shape((PASS, sub_rows + 8, entries), F32))(partial_sens)
        sens = lax.all_to_all(half, "bus", split_axis=0, concat_axis=0, tiled=True, axis_index_groups=groups_z)
    with jax.named_scope("reply"):
        reply = call(reply_kernel, shape((line_count, 1152), F32), scratch=(pltpu.VMEM((128, 128), F32),))(
            sens, asked, rate_row
        )
        got = lax.all_to_all(reply, "line", split_axis=0, concat_axis=0, tiled=True)
    with jax.named_scope("screen"):
        loading = call(screen_kernel, shape((slot_count, sub_rows, outages), F32))(got, named, off_row, live_row)
    return jnp.transpose(loading, (2, 0, 1))


def solution(mesh):
    return jax.shard_map(
        local,
        mesh=mesh,
        in_specs=(
            P("line", "bus"),
            P(None, "bus"),
            P("line"),
            P("line", None),
            P("line"),
            P("line"),
            P("line", None),
        ),
        out_specs=P("line", None, "bus"),
        check_vma=False,
    )
```

```python
import jax
import jax.numpy as jnp
from jax import lax
from jax.experimental import pallas as pl
from jax.experimental.pallas import tpu as pltpu
from jax.sharding import PartitionSpec as P

floor_value = 0.25
F32 = jnp.float32
BF16 = jnp.bfloat16
NT = (((1,), (1,)), ((), ()))
NN = (((1,), (0,)), ((), ()))
HOURS = 32
CAP = 12
CHUNK = 1920
PASS = 2
IN_VMEM = pl.BlockSpec(memory_space=pltpu.VMEM)
IN_PLACE = pl.BlockSpec(memory_space=pl.ANY)


def iota(shape, axis):
    return lax.broadcasted_iota(jnp.int32, shape, axis)


def split2(value):
    high = value.astype(BF16)
    return high, (value - high.astype(F32)).astype(BF16)


def request_kernel(mon_ref, ends_ref, off_ref, out_ref):
    slots, outages = mon_ref.shape
    lines = out_ref.shape[0]

    def twice(row):
        return jnp.concatenate([row, row], axis=1)

    named = twice(mon_ref[...])
    line_row = iota((lines, 128), 0)
    names = jnp.zeros((lines, 128), F32)
    for s in range(slots):
        names = jnp.where(named[s : s + 1] == line_row, 1.0, names)
    earlier = iota((128, 128), 0) < iota((128, 128), 1) % outages
    rank = lax.dot_general(
        names.astype(BF16), jnp.where(earlier, 1.0, 0.0).astype(BF16), NN, preferred_element_type=F32
    )
    rank = jnp.where(names > 0.0, rank, -1.0)
    start = twice(ends_ref[0:1, :]) + 1
    end = twice(ends_ref[1:2, :]) + 1
    place = twice(off_ref[...]) + 1
    second = iota((1, 128), 1) // outages
    spot = iota((128, 128), 0)
    chosen, high, low = [], [], []
    for t in range(CAP // 2):
        turn = 2 * t + second
        chosen.append(jnp.where(rank == turn.astype(F32), 1.0, 0.0).astype(BF16))
        value = jnp.where(
            spot == turn, start, jnp.where(spot == 16 + turn, end, jnp.where(spot == 32 + turn, place, 0))
        )
        high.append((value >> 8).astype(F32).astype(BF16))
        low.append((value & 255).astype(F32).astype(BF16))
    chosen = jnp.concatenate(chosen, axis=1)
    high = lax.dot_general(chosen, jnp.concatenate(high, axis=1), NT, preferred_element_type=F32)
    low = lax.dot_general(chosen, jnp.concatenate(low, axis=1), NT, preferred_element_type=F32)
    out_ref[...] = 256.0 * high + low


def pick_kernel(
    req_ref, s_hbm, inj_hbm, out_ref, s_ref, inj_ref, from_ref, to_ref, sum_ref, flow_ref, s_sems, inj_sem
):
    lines = req_ref.shape[0]
    rows, width = s_ref.shape
    peers, _, entries = out_ref.shape
    deep = rows // peers
    whole, rest = width // CHUNK, width % CHUNK

    def copy(at, size, q):
        cols = pl.ds(at, size)
        return pltpu.make_async_copy(s_hbm.at[:, cols], s_ref.at[:, cols], s_sems.at[q])

    inj_copy = pltpu.make_async_copy(inj_hbm, inj_ref, inj_sem)
    for q in range(whole):
        copy(q * CHUNK, CHUNK, q).start()
        if q == 0:
            inj_copy.start()
    if rest:
        copy(whole * CHUNK, rest, whole).start()
    bus = lax.axis_index("bus_x") * lax.axis_size("bus_z") + lax.axis_index("bus_z")
    base = bus * width + 1
    req = req_ref[...]
    lane = iota((lines, 128), 1)
    for c in range(CAP):
        first = req[:, c : c + 1].astype(jnp.int32) - base
        second = req[:, 16 + c : 17 + c].astype(jnp.int32) - base
        same = first == second
        first = jnp.where(same | (first < 0) | (first >= width), -1, first)
        second = jnp.where(same | (second < 0) | (second >= width), -1, second)
        from_ref[c * lines : (c + 1) * lines, :] = jnp.broadcast_to(first, (lines, 128)).astype(jnp.int16)
        to_ref[c * lines : (c + 1) * lines, :] = jnp.broadcast_to(second, (lines, 128)).astype(jnp.int16)
    sum_ref[...] = jnp.zeros_like(sum_ref)
    flow_ref[...] = jnp.zeros_like(flow_ref)
    one, minus, zero = jnp.asarray(1, BF16), jnp.asarray(-1, BF16), jnp.asarray(0, BF16)

    def step(at, size):
        columns = []
        for t in range(size // 128):
            spot = (iota((16, 128), 1) + (at + t * 128)).astype(jnp.int16)
            spot = jnp.broadcast_to(spot[None], (entries // 16, 16, 128)).reshape(entries, 128)
            columns.append(
                jnp.where(from_ref[...] == spot, one, jnp.where(to_ref[...] == spot, minus, zero))
            )
        cols = pl.ds(at, size)
        s_high, s_low = split2(s_ref[:, cols])
        both = jnp.concatenate([s_high, s_low], axis=0)
        i_high, i_low = split2(inj_ref[:, cols])
        sum_ref[...] += lax.dot_general(
            jnp.concatenate(columns, axis=1), both, NT, preferred_element_type=F32
        )
        flow_ref[...] += lax.dot_general(
            jnp.concatenate([i_high, i_low], axis=0), both, NT, preferred_element_type=F32
        )

    inj_copy.wait()

    def body(q, carry):
        at = pl.multiple_of(q * CHUNK, CHUNK)
        copy(at, CHUNK, q).wait()
        step(at, CHUNK)
        return carry

    lax.fori_loop(0, whole, body, 0)
    if rest:
        copy(whole * CHUNK, rest, whole).wait()
        step(whole * CHUNK, rest)
    part = (
        flow_ref[:HOURS, :rows]
        + (flow_ref[:HOURS, rows:] + flow_ref[HOURS:, :rows])
        + flow_ref[HOURS:, rows:]
    )
    picked = sum_ref[:, :rows] + sum_ref[:, rows:]
    own = jnp.zeros((lines, 128), F32)
    for c in range(CAP):
        off = req[:, 32 + c : 33 + c].astype(jnp.int32) - 1
        value = jnp.sum(
            jnp.where(lane == off, picked[c * lines : (c + 1) * lines], 0.0), axis=1, keepdims=True
        )
        own = jnp.where(lane == c, value, own)
    turned = jnp.transpose(picked)
    own_turned = jnp.transpose(jnp.concatenate([own, jnp.zeros((128 - lines, 128), F32)], axis=0))
    extra = jnp.concatenate(
        [part[8 * t : 8 * t + 8] for t in range(4)] + [own_turned[0:8], own_turned[8:16]], axis=1
    )
    for b in range(peers):
        out_ref[b, :deep, :] = turned[b * deep : (b + 1) * deep]
        out_ref[b, deep:, :] = extra


def reply_kernel(got_ref, req_ref, rate_ref, out_ref, rate_scratch):
    peers = got_ref.shape[0]
    lines = req_ref.shape[0]
    rows = rate_ref.shape[1]
    passes = out_ref.shape[0] // lines
    sub = (got_ref.shape[1] - 8) // passes
    place = lax.axis_index("bus_x") * passes
    total = got_ref[0]
    for b in range(1, peers):
        total = total + got_ref[b]
    sens, rest = total[: passes * sub], total[passes * sub :]
    flows = jnp.concatenate([rest[:, 128 * t : 128 * t + 128] for t in range(4)], axis=0)
    lane = iota((HOURS, 128), 1)
    hour = iota((HOURS, 128), 0)
    f_high, f_low = split2(flows)
    f_rest = (flows - f_high.astype(F32) - f_low.astype(F32)).astype(BF16)
    f_all = jnp.concatenate([f_high, f_low, f_rest], axis=0)
    req = req_ref[...]
    lane_line = iota((lines, 128), 1)
    hots = [
        jnp.where(lane_line == req[:, 32 + c : 33 + c].astype(jnp.int32) - 1, 1.0, 0.0).astype(BF16)
        for c in range(CAP)
    ]
    left = jnp.concatenate([jnp.concatenate(hots[4 * q : 4 * q + 4], axis=1) for q in range(3)], axis=0)

    def diagonal(block):
        blank = jnp.zeros_like(block)
        return jnp.concatenate(
            [jnp.concatenate([block if v == u else blank for v in range(4)], axis=1) for u in range(4)], axis=0
        )

    lost = lax.dot_general(
        left, diagonal(f_high), NT, preferred_element_type=F32
    ) + lax.dot_general(left, diagonal(f_low), NT, preferred_element_type=F32)
    rate_scratch[...] = 0.5 * jnp.transpose(jnp.broadcast_to(rate_ref[...], (rows, 128)))

    def wide(block):
        return jnp.concatenate([block, jnp.zeros((block.shape[0], 128 - lines), F32)], axis=1)

    for p in range(passes):
        at = slice(p * lines, (p + 1) * lines)
        wanted = iota((128, 128), 0) == (place + p) * sub + iota((128, 128), 1) % sub
        spread = lax.dot_general(f_all, jnp.where(wanted, 1.0, 0.0).astype(BF16), NN, preferred_element_type=F32)
        spread = spread[:HOURS] + spread[HOURS : 2 * HOURS] + spread[2 * HOURS :]
        spread = jnp.where(lane // sub == hour % 8, spread, 0.0)
        for t in range(4):
            row = jnp.sum(spread[8 * t : 8 * t + 8], axis=0, keepdims=True)
            out_ref[at, 128 * t : 128 * t + 128] = jnp.broadcast_to(row, (lines, 128))
        for q in range(3):
            out_ref[at, 512 + 128 * q : 640 + 128 * q] = lost[q * lines : (q + 1) * lines]
        rate = rate_scratch[pl.ds(pl.multiple_of((place + p) * sub, sub), sub), :]
        part = sens[p * sub : (p + 1) * sub]
        blocks = [wide(part[:, c * lines : (c + 1) * lines]) for c in range(CAP)]
        one = jnp.concatenate(blocks[:8], axis=0)
        two = jnp.concatenate(
            blocks[8:] + [rest[:, 512:640], rest[:, 640:768], rate, jnp.zeros((32, 128), F32)], axis=0
        )
        out_ref[at, 896:1024] = jnp.transpose(one)[:lines]
        out_ref[at, 1024:1152] = jnp.transpose(two)[:lines]


def screen_kernel(got_ref, mon_ref, off_ref, live_ref, out_ref):
    slots, outages = mon_ref.shape
    sub = out_ref.shape[1]
    passes = lax.axis_size("bus_z")
    lines = got_ref.shape[0] // passes
    place = lax.axis_index("bus_x") * passes + lax.axis_index("bus_z")
    pieces = []
    for t in range(9):
        block = got_ref[:lines, 128 * t : 128 * t + 128]
        for p in range(1, passes):
            block = block + got_ref[p * lines : (p + 1) * lines, 128 * t : 128 * t + 128]
        high = block.astype(BF16).astype(F32)
        low = (block - high).astype(BF16).astype(F32)
        pieces.append(jnp.transpose(jnp.concatenate([high, low], axis=0)).astype(BF16))
    shared = jnp.concatenate(pieces[:4] + pieces[7:], axis=0)
    own = jnp.concatenate(pieces[4:7] + pieces[8:], axis=0)
    named = jnp.concatenate([mon_ref[...], mon_ref[...]], axis=1)
    line_row = iota((lines, 128), 0)
    lane = iota((1, 128), 1)
    outage = lane % outages
    names = jnp.zeros((lines, 128), F32)
    for s in range(slots):
        names = jnp.where(named[s : s + 1] == line_row, 1.0, names)
    earlier = iota((128, 128), 0) < iota((128, 128), 1) % outages
    rank = lax.dot_general(
        names.astype(BF16),
        jnp.where(earlier, 1.0, 0.0).astype(BF16),
        (((1,), (0,)), ((), ())),
        preferred_element_type=F32,
    )

    def hot_of(target):
        hot = jnp.where(line_row == target, 1.0, 0.0)
        turn = jnp.sum(hot * rank, axis=0, keepdims=True)
        hot = hot.astype(BF16)
        return jnp.concatenate([hot, hot], axis=0), turn

    plain = (((1,), (0,)), ((), ()))
    hot_own, turn_own = hot_of(named[0:1])
    got_own = lax.dot_general(own, hot_own, plain, preferred_element_type=F32)
    lost = jnp.zeros((HOURS, 128), F32)
    self_sens = jnp.zeros((1, 128), F32)
    for c in range(CAP):
        mine = turn_own == float(c)
        lost = jnp.where(mine, got_own[HOURS * c : HOURS * c + HOURS], lost)
        self_sens = jnp.where(mine, got_own[448 + c : 449 + c], self_sens)
    divisor = jnp.maximum(1.0 - self_sens, floor_value)
    off = jnp.concatenate([off_ref[...], off_ref[...]], axis=1)
    live = jnp.concatenate([live_ref[...], live_ref[...]], axis=1)
    lost_scaled = lost
    row = iota((sub, 128), 0)
    for t in range(slots // 2):
        target = jnp.where(lane < outages, named[2 * t : 2 * t + 1], named[2 * t + 1 : 2 * t + 2])
        hot, turn = hot_of(target)
        got = lax.dot_general(shared, hot, plain, preferred_element_type=F32)
        sens = jnp.zeros((sub, 128), F32)
        for c in range(CAP):
            sens = jnp.where(turn == float(c), got[512 + sub * c : 512 + sub * c + sub], sens)
        factor = sens / divisor
        worst = jnp.zeros((sub, 128), F32)
        for h in range(HOURS):
            worst = jnp.maximum(worst, jnp.abs(got[sub * h : sub * h + sub] + factor * lost_scaled[h : h + 1]))
        result = worst / got[720:736]
        slot = 2 * t + jnp.where(lane < outages, 0, 1)
        keep = slot < live
        if t == 0:
            keep = keep & ~((slot == 0) & (row == off - place * sub))
        result = jnp.where(keep, result, 0.0)
        out_ref[2 * t] = result[:, :outages]
        out_ref[2 * t + 1] = result[:, outages:]


def call(kernel, out_shape, in_specs, scratch=(), flops=0, moved=0, limit=16):
    return pl.pallas_call(
        kernel,
        out_shape=out_shape,
        in_specs=in_specs,
        out_specs=IN_VMEM,
        scratch_shapes=list(scratch),
        compiler_params=pltpu.CompilerParams(vmem_limit_bytes=limit * 1024 * 1024),
        cost_estimate=pl.CostEstimate(flops=flops, bytes_accessed=moved, transcendentals=0),
    )


def local(shift_factors, injection, rating, monitored, live_count, outage_offset, outage_ends):
    peers = lax.axis_size("bus_x")
    passes = lax.axis_size("bus_z")
    line_count = lax.axis_size("line")
    block_rows, bus_width = shift_factors.shape
    sub_rows = block_rows // (peers * passes)
    outages, slot_count = monitored.shape
    entries = CAP * line_count
    shape = jax.ShapeDtypeStruct
    off_row = outage_offset.reshape(1, outages)
    live_row = live_count.reshape(1, outages)
    rate_row = rating.reshape(1, block_rows)
    named = monitored.T
    with jax.named_scope("requests"):
        requests = call(request_kernel, shape((line_count, 128), F32), [IN_VMEM] * 3, limit=56)(
            named, outage_ends.T, off_row
        )
        asked = lax.all_to_all(requests, "line", split_axis=0, concat_axis=0, tiled=True)
    with jax.named_scope("picks"):
        partial_sens = call(
            pick_kernel,
            shape((peers, passes * sub_rows + 8, entries), F32),
            [IN_VMEM, IN_PLACE, IN_PLACE],
            scratch=(
                pltpu.VMEM((block_rows, bus_width), F32),
                pltpu.VMEM((HOURS, bus_width), F32),
                pltpu.VMEM((entries, 128), jnp.int16),
                pltpu.VMEM((entries, 128), jnp.int16),
                pltpu.VMEM((entries, 2 * block_rows), F32),
                pltpu.VMEM((2 * HOURS, 2 * block_rows), F32),
                pltpu.SemaphoreType.DMA((-(-bus_width // CHUNK),)),
                pltpu.SemaphoreType.DMA,
            ),
            flops=4 * entries * block_rows * bus_width,
            moved=4 * block_rows * bus_width,
            limit=56,
        )(asked, shift_factors, injection)
        half_sens = lax.all_to_all(partial_sens, "bus_x", split_axis=0, concat_axis=0, tiled=True)
    with jax.named_scope("reply"):
        reply = call(
            reply_kernel,
            shape((passes * line_count, 1152), F32),
            [IN_VMEM] * 3,
            scratch=(pltpu.VMEM((block_rows, block_rows), F32),),
        )(half_sens, asked, rate_row)
        got = lax.all_to_all(reply, ("bus_z", "line"), split_axis=0, concat_axis=0, tiled=True)
    with jax.named_scope("screen"):
        loading = call(screen_kernel, shape((slot_count, sub_rows, outages), F32), [IN_VMEM] * 4)(
            got, named, off_row, live_row
        )
    return jnp.transpose(loading, (2, 0, 1))


def solution(mesh):
    lines, buses = mesh.devices.shape
    bus = ("bus_x", "bus_z")
    return jax.shard_map(
        local,
        mesh=jax.sharding.Mesh(mesh.devices.reshape(lines, buses // PASS, PASS), ("line",) + bus),
        in_specs=(
            P("line", bus),
            P(None, bus),
            P("line"),
            P("line", None),
            P("line"),
            P("line"),
            P("line", None),
        ),
        out_specs=P("line", None, bus),
        check_vma=False,
    )
```

```python
import jax
import jax.numpy as jnp
from jax import lax
from jax.experimental import pallas as pl
from jax.experimental.pallas import tpu as pltpu
from jax.sharding import PartitionSpec as P

floor_value = 0.25
F32 = jnp.float32
BF16 = jnp.bfloat16
NT = (((1,), (1,)), ((), ()))
NN = (((1,), (0,)), ((), ()))
HOURS = 32
CAP = 12
CHUNK = 2304
PASS = 2
TILES = 9
IN_VMEM = pl.BlockSpec(memory_space=pltpu.VMEM)
IN_HBM = pl.BlockSpec(memory_space=pltpu.HBM)


def iota(shape, axis):
    return lax.broadcasted_iota(jnp.int32, shape, axis)


def split2(value):
    high = value.astype(BF16)
    return high, (value - high.astype(F32)).astype(BF16)


def request_kernel(mon_ref, ends_ref, off_ref, out_ref):
    slots, outages = mon_ref.shape
    lines = out_ref.shape[0]

    def twice(row):
        return jnp.concatenate([row, row], axis=1)

    named = twice(mon_ref[...])
    line_row = iota((lines, 128), 0)
    names = jnp.zeros((lines, 128), F32)
    for s in range(slots):
        names = jnp.where(named[s : s + 1] == line_row, 1.0, names)
    earlier = iota((128, 128), 0) < iota((128, 128), 1) % outages
    rank = lax.dot_general(
        names.astype(BF16), jnp.where(earlier, 1.0, 0.0).astype(BF16), NN, preferred_element_type=F32
    )
    rank = jnp.where(names > 0.0, rank, -1.0)
    start = twice(ends_ref[0:1, :]) + 1
    end = twice(ends_ref[1:2, :]) + 1
    place = twice(off_ref[...]) + 1
    second = iota((1, 128), 1) // outages
    spot = iota((128, 128), 0)
    chosen, high, low = [], [], []
    for t in range(CAP // 2):
        turn = 2 * t + second
        chosen.append(jnp.where(rank == turn.astype(F32), 1.0, 0.0).astype(BF16))
        value = jnp.where(
            spot == turn, start, jnp.where(spot == 16 + turn, end, jnp.where(spot == 32 + turn, place, 0))
        )
        high.append((value >> 8).astype(F32).astype(BF16))
        low.append((value & 255).astype(F32).astype(BF16))
    chosen = jnp.concatenate(chosen, axis=1)
    high = lax.dot_general(chosen, jnp.concatenate(high, axis=1), NT, preferred_element_type=F32)
    low = lax.dot_general(chosen, jnp.concatenate(low, axis=1), NT, preferred_element_type=F32)
    out_ref[...] = 256.0 * high + low


def pick_kernel(
    req_ref, s_hbm, inj_hbm, out_ref, s_ref, inj_ref, from_ref, to_ref, sum_ref, flow_ref, s_sems, inj_sems
):
    lines = req_ref.shape[0]
    rows, width = s_ref.shape
    peers, _, entries = out_ref.shape
    deep = rows // peers
    whole, rest = width // CHUNK, width % CHUNK

    def copies(at, size, q):
        cols = pl.ds(at, size)
        return (
            pltpu.make_async_copy(s_hbm.at[:, cols], s_ref.at[:, cols], s_sems.at[q]),
            pltpu.make_async_copy(inj_hbm.at[:, cols], inj_ref.at[:, cols], inj_sems.at[q]),
        )

    def fetch(at, size, q):
        for copy in copies(at, size, q):
            copy.start()

    def arrive(at, size, q):
        for copy in copies(at, size, q):
            copy.wait()

    fetch(whole * CHUNK, rest, whole)
    for q in range(whole):
        fetch(q * CHUNK, CHUNK, q)
    bus = lax.axis_index("bus_x") * lax.axis_size("bus_z") + lax.axis_index("bus_z")
    base = bus * width + 1
    req = req_ref[...]
    lane = iota((lines, 128), 1)
    for c in range(CAP):
        first = req[:, c : c + 1].astype(jnp.int32) - base
        second = req[:, 16 + c : 17 + c].astype(jnp.int32) - base
        same = first == second
        first = jnp.where(same | (first < 0) | (first >= width), -1, first)
        second = jnp.where(same | (second < 0) | (second >= width), -1, second)
        from_ref[c * lines : (c + 1) * lines, :] = jnp.broadcast_to(first, (lines, 128)).astype(jnp.int16)
        to_ref[c * lines : (c + 1) * lines, :] = jnp.broadcast_to(second, (lines, 128)).astype(jnp.int16)
    sum_ref[...] = jnp.zeros_like(sum_ref)
    flow_ref[...] = jnp.zeros_like(flow_ref)
    one, minus, zero = jnp.asarray(1, BF16), jnp.asarray(-1, BF16), jnp.asarray(0, BF16)

    def step(at, size):
        columns = []
        for t in range(size // 128):
            spot = (iota((16, 128), 1) + (at + t * 128)).astype(jnp.int16)
            spot = jnp.broadcast_to(spot[None], (entries // 16, 16, 128)).reshape(entries, 128)
            columns.append(
                jnp.where(from_ref[...] == spot, one, jnp.where(to_ref[...] == spot, minus, zero))
            )
        cols = pl.ds(at, size)
        s_high, s_low = split2(s_ref[:, cols])
        both = jnp.concatenate([s_high, s_low], axis=0)
        i_high, i_low = split2(inj_ref[:, cols])
        sum_ref[...] += lax.dot_general(
            jnp.concatenate(columns, axis=1), both, NT, preferred_element_type=F32
        )
        flow_ref[...] += lax.dot_general(
            jnp.concatenate([i_high, i_low], axis=0), both, NT, preferred_element_type=F32
        )

    arrive(whole * CHUNK, rest, whole)
    step(whole * CHUNK, rest)

    def body(q, carry):
        at = pl.multiple_of(q * CHUNK, CHUNK)
        arrive(at, CHUNK, q)
        step(at, CHUNK)
        return carry

    lax.fori_loop(0, whole, body, 0)
    part = (
        flow_ref[:HOURS, :rows]
        + (flow_ref[:HOURS, rows:] + flow_ref[HOURS:, :rows])
        + flow_ref[HOURS:, rows:]
    )
    picked = sum_ref[:, :rows] + sum_ref[:, rows:]
    own = jnp.zeros((lines, 128), F32)
    for c in range(CAP):
        off = req[:, 32 + c : 33 + c].astype(jnp.int32) - 1
        value = jnp.sum(
            jnp.where(lane == off, picked[c * lines : (c + 1) * lines], 0.0), axis=1, keepdims=True
        )
        own = jnp.where(lane == c, value, own)
    turned = jnp.transpose(picked)
    own_turned = jnp.transpose(jnp.concatenate([own, jnp.zeros((128 - lines, 128), F32)], axis=0))
    extra = jnp.concatenate(
        [part[8 * t : 8 * t + 8] for t in range(4)] + [own_turned[0:8], own_turned[8:16]], axis=1
    )
    for b in range(peers):
        out_ref[b, :deep, :] = turned[b * deep : (b + 1) * deep]
        out_ref[b, deep:, :] = extra


def reply_kernel(got_ref, req_ref, rate_ref, out_ref, rate_scratch):
    peers = got_ref.shape[0]
    lines = req_ref.shape[0]
    rows = rate_ref.shape[1]
    passes = out_ref.shape[0] // (lines * TILES)
    sub = (got_ref.shape[1] - 8) // passes
    place = lax.axis_index("bus_x") * passes
    total = got_ref[0]
    for b in range(1, peers):
        total = total + got_ref[b]
    sens, rest = total[: passes * sub], total[passes * sub :]
    flows = jnp.concatenate([rest[:, 128 * t : 128 * t + 128] for t in range(4)], axis=0)
    lane = iota((HOURS, 128), 1)
    hour = iota((HOURS, 128), 0)
    f_high, f_low = split2(flows)
    f_rest = (flows - f_high.astype(F32) - f_low.astype(F32)).astype(BF16)
    f_all = jnp.concatenate([f_high, f_low, f_rest], axis=0)
    req = req_ref[...]
    lane_line = iota((lines, 128), 1)
    hots = [
        jnp.where(lane_line == req[:, 32 + c : 33 + c].astype(jnp.int32) - 1, 1.0, 0.0).astype(BF16)
        for c in range(CAP)
    ]
    left = jnp.concatenate([jnp.concatenate(hots[4 * q : 4 * q + 4], axis=1) for q in range(3)], axis=0)

    def diagonal(block):
        blank = jnp.zeros_like(block)
        return jnp.concatenate(
            [jnp.concatenate([block if v == u else blank for v in range(4)], axis=1) for u in range(4)], axis=0
        )

    lost = lax.dot_general(
        left, diagonal(f_high), NT, preferred_element_type=F32
    ) + lax.dot_general(left, diagonal(f_low), NT, preferred_element_type=F32)
    rate_scratch[...] = 0.5 * jnp.transpose(jnp.broadcast_to(rate_ref[...], (rows, 128)))

    def wide(block):
        return jnp.concatenate([block, jnp.zeros((block.shape[0], 128 - lines), F32)], axis=1)

    def put(p, q, block):
        out_ref[pl.ds(p * lines * TILES + q, lines, stride=TILES), :] = block

    for p in range(passes):
        wanted = iota((128, 128), 0) == (place + p) * sub + iota((128, 128), 1) % sub
        spread = lax.dot_general(f_all, jnp.where(wanted, 1.0, 0.0).astype(BF16), NN, preferred_element_type=F32)
        spread = spread[:HOURS] + spread[HOURS : 2 * HOURS] + spread[2 * HOURS :]
        spread = jnp.where(lane // sub == hour % 8, spread, 0.0)
        for t in range(4):
            row = jnp.sum(spread[8 * t : 8 * t + 8], axis=0, keepdims=True)
            put(p, t, jnp.broadcast_to(row, (lines, 128)))
        for q in range(3):
            put(p, 4 + q, lost[q * lines : (q + 1) * lines])
        rate = rate_scratch[pl.ds(pl.multiple_of((place + p) * sub, sub), sub), :]
        part = sens[p * sub : (p + 1) * sub]
        blocks = [wide(part[:, c * lines : (c + 1) * lines]) for c in range(CAP)]
        one = jnp.concatenate(blocks[:8], axis=0)
        two = jnp.concatenate(
            blocks[8:] + [rest[:, 512:640], rest[:, 640:768], rate, jnp.zeros((32, 128), F32)], axis=0
        )
        put(p, 7, jnp.transpose(one)[:lines])
        put(p, 8, jnp.transpose(two)[:lines])


def screen_kernel(got_ref, mon_ref, off_ref, live_ref, out_ref):
    slots, outages = mon_ref.shape
    sub = out_ref.shape[1]
    passes = lax.axis_size("bus_z")
    lines = got_ref.shape[0] // (passes * TILES)
    place = lax.axis_index("bus_x") * passes + lax.axis_index("bus_z")
    pieces = []
    for t in range(TILES):
        block = got_ref[pl.ds(t, lines, stride=TILES), :]
        for p in range(1, passes):
            block = block + got_ref[pl.ds(p * lines * TILES + t, lines, stride=TILES), :]
        high = block.astype(BF16).astype(F32)
        low = (block - high).astype(BF16).astype(F32)
        pieces.append(jnp.transpose(jnp.concatenate([high, low], axis=0)).astype(BF16))
    shared = jnp.concatenate(pieces[:4] + pieces[7:], axis=0)
    own = jnp.concatenate(pieces[4:7] + pieces[8:], axis=0)
    named = jnp.concatenate([mon_ref[...], mon_ref[...]], axis=1)
    line_row = iota((lines, 128), 0)
    lane = iota((1, 128), 1)
    outage = lane % outages
    names = jnp.zeros((lines, 128), F32)
    for s in range(slots):
        names = jnp.where(named[s : s + 1] == line_row, 1.0, names)
    earlier = iota((128, 128), 0) < iota((128, 128), 1) % outages
    rank = lax.dot_general(
        names.astype(BF16),
        jnp.where(earlier, 1.0, 0.0).astype(BF16),
        (((1,), (0,)), ((), ())),
        preferred_element_type=F32,
    )

    def hot_of(target):
        hot = jnp.where(line_row == target, 1.0, 0.0)
        turn = jnp.sum(hot * rank, axis=0, keepdims=True)
        hot = hot.astype(BF16)
        return jnp.concatenate([hot, hot], axis=0), turn

    plain = (((1,), (0,)), ((), ()))
    hot_own, turn_own = hot_of(named[0:1])
    got_own = lax.dot_general(own, hot_own, plain, preferred_element_type=F32)
    lost = jnp.zeros((HOURS, 128), F32)
    self_sens = jnp.zeros((1, 128), F32)
    for c in range(CAP):
        mine = turn_own == float(c)
        lost = jnp.where(mine, got_own[HOURS * c : HOURS * c + HOURS], lost)
        self_sens = jnp.where(mine, got_own[448 + c : 449 + c], self_sens)
    divisor = jnp.maximum(1.0 - self_sens, floor_value)
    off = jnp.concatenate([off_ref[...], off_ref[...]], axis=1)
    live = jnp.concatenate([live_ref[...], live_ref[...]], axis=1)
    lost_scaled = lost
    row = iota((sub, 128), 0)
    for t in range(slots // 2):
        target = jnp.where(lane < outages, named[2 * t : 2 * t + 1], named[2 * t + 1 : 2 * t + 2])
        hot, turn = hot_of(target)
        got = lax.dot_general(shared, hot, plain, preferred_element_type=F32)
        sens = jnp.zeros((sub, 128), F32)
        for c in range(CAP):
            sens = jnp.where(turn == float(c), got[512 + sub * c : 512 + sub * c + sub], sens)
        factor = sens / divisor
        worst = jnp.zeros((sub, 128), F32)
        for h in range(HOURS):
            worst = jnp.maximum(worst, jnp.abs(got[sub * h : sub * h + sub] + factor * lost_scaled[h : h + 1]))
        result = worst / got[720:736]
        slot = 2 * t + jnp.where(lane < outages, 0, 1)
        keep = slot < live
        if t == 0:
            keep = keep & ~((slot == 0) & (row == off - place * sub))
        result = jnp.where(keep, result, 0.0)
        out_ref[2 * t] = result[:, :outages]
        out_ref[2 * t + 1] = result[:, outages:]


def call(kernel, out_shape, in_specs, scratch=(), flops=0, moved=0, limit=16):
    return pl.pallas_call(
        kernel,
        out_shape=out_shape,
        in_specs=in_specs,
        out_specs=IN_VMEM,
        scratch_shapes=list(scratch),
        compiler_params=pltpu.CompilerParams(vmem_limit_bytes=limit * 1024 * 1024),
        cost_estimate=pl.CostEstimate(flops=flops, bytes_accessed=moved, transcendentals=0),
    )


def local(shift_factors, injection, rating, monitored, live_count, outage_offset, outage_ends):
    peers = lax.axis_size("bus_x")
    passes = lax.axis_size("bus_z")
    line_count = lax.axis_size("line")
    block_rows, bus_width = shift_factors.shape
    sub_rows = block_rows // (peers * passes)
    outages, slot_count = monitored.shape
    entries = CAP * line_count
    shape = jax.ShapeDtypeStruct
    off_row = outage_offset.reshape(1, outages)
    live_row = live_count.reshape(1, outages)
    rate_row = rating.reshape(1, block_rows)
    named = monitored.T
    with jax.named_scope("requests"):
        requests = call(request_kernel, shape((line_count, 128), F32), [IN_VMEM] * 3, limit=56)(
            named, outage_ends.T, off_row
        )
        asked = lax.all_to_all(requests, "line", split_axis=0, concat_axis=0, tiled=True)
    with jax.named_scope("picks"):
        partial_sens = call(
            pick_kernel,
            shape((peers, passes * sub_rows + 8, entries), F32),
            [IN_VMEM, IN_HBM, IN_HBM],
            scratch=(
                pltpu.VMEM((block_rows, bus_width), F32),
                pltpu.VMEM((HOURS, bus_width), F32),
                pltpu.VMEM((entries, 128), jnp.int16),
                pltpu.VMEM((entries, 128), jnp.int16),
                pltpu.VMEM((entries, 2 * block_rows), F32),
                pltpu.VMEM((2 * HOURS, 2 * block_rows), F32),
                pltpu.SemaphoreType.DMA((bus_width // CHUNK + 1,)),
                pltpu.SemaphoreType.DMA((bus_width // CHUNK + 1,)),
            ),
            flops=4 * entries * block_rows * bus_width,
            moved=4 * block_rows * bus_width,
            limit=53,
        )(asked, shift_factors, injection)
        half_sens = lax.all_to_all(partial_sens, "bus_x", split_axis=0, concat_axis=0, tiled=True)
    with jax.named_scope("reply"):
        reply = call(
            reply_kernel,
            shape((passes * line_count * TILES, 128), F32),
            [IN_VMEM] * 3,
            scratch=(pltpu.VMEM((block_rows, block_rows), F32),),
        )(half_sens, asked, rate_row)
        reply = reply.reshape(passes * line_count, TILES * 128)
        got = lax.all_to_all(reply, ("bus_z", "line"), split_axis=0, concat_axis=0, tiled=True)
    with jax.named_scope("screen"):
        loading = call(screen_kernel, shape((slot_count, sub_rows, outages), F32), [IN_VMEM] * 4)(
            got.reshape(-1, 128), named, off_row, live_row
        )
    return jnp.transpose(loading, (2, 0, 1))


def solution(mesh):
    lines, buses = mesh.devices.shape
    bus = ("bus_x", "bus_z")
    return jax.shard_map(
        local,
        mesh=jax.sharding.Mesh(mesh.devices.reshape(lines, buses // PASS, PASS), ("line",) + bus),
        in_specs=(
            P("line", bus),
            P(None, bus),
            P("line"),
            P("line", None),
            P("line"),
            P("line"),
            P("line", None),
        ),
        out_specs=P("line", None, bus),
        check_vma=False,
    )
```

```python
import jax
import jax.numpy as jnp
from jax import lax
from jax.experimental import pallas as pl
from jax.experimental.pallas import tpu as pltpu
from jax.sharding import PartitionSpec as P

floor_value = 0.25
F32 = jnp.float32
BF16 = jnp.bfloat16
NT = (((1,), (1,)), ((), ()))
NN = (((1,), (0,)), ((), ()))
HOURS = 32
CAP = 12
CHUNK = 2304
PASS = 2
TILES = 9
PACKED = 256
IN_VMEM = pl.BlockSpec(memory_space=pltpu.VMEM)
IN_HBM = pl.BlockSpec(memory_space=pltpu.HBM)


def iota(shape, axis):
    return lax.broadcasted_iota(jnp.int32, shape, axis)


def split2(value):
    high = value.astype(BF16)
    return high, (value - high.astype(F32)).astype(BF16)


def request_kernel(mon_ref, ends_ref, off_ref, live_ref, out_ref):
    slots, outages = mon_ref.shape
    lines = out_ref.shape[0]

    def twice(row):
        return jnp.concatenate([row, row], axis=1)

    named = twice(mon_ref[...])
    line_row = iota((lines, 128), 0)
    live = twice(live_ref[...])
    names = jnp.zeros((lines, 128), F32)
    asks = jnp.zeros((lines, 128), F32)
    for s in range(slots):
        same = named[s : s + 1] == line_row
        names = jnp.where(same, 1.0, names)
        asks = jnp.where(same & (s < live), 1.0, asks)
    earlier = iota((128, 128), 0) < iota((128, 128), 1) % outages
    rank = lax.dot_general(
        names.astype(BF16), jnp.where(earlier, 1.0, 0.0).astype(BF16), NN, preferred_element_type=F32
    )
    rank = jnp.where(asks > 0.0, rank, -1.0)
    start = twice(ends_ref[0:1, :]) + 1
    end = twice(ends_ref[1:2, :]) + 1
    place = twice(off_ref[...]) + 1
    second = iota((1, 128), 1) // outages
    spot = iota((128, 128), 0)
    chosen, high, low = [], [], []
    for t in range(CAP // 2):
        turn = 2 * t + second
        chosen.append(jnp.where(rank == turn.astype(F32), 1.0, 0.0).astype(BF16))
        value = jnp.where(
            spot == turn, start, jnp.where(spot == 16 + turn, end, jnp.where(spot == 32 + turn, place, 0))
        )
        high.append((value >> 8).astype(F32).astype(BF16))
        low.append((value & 255).astype(F32).astype(BF16))
    chosen = jnp.concatenate(chosen, axis=1)
    high = lax.dot_general(chosen, jnp.concatenate(high, axis=1), NT, preferred_element_type=F32)
    low = lax.dot_general(chosen, jnp.concatenate(low, axis=1), NT, preferred_element_type=F32)
    out_ref[...] = 256.0 * high + low


def pick_kernel(
    req_ref,
    s_hbm,
    inj_hbm,
    out_ref,
    s_ref,
    inj_ref,
    split_ref,
    turn_ref,
    perm_ref,
    from_ref,
    to_ref,
    sum_ref,
    flow_ref,
    total_ref,
    s_sems,
    inj_sems,
):
    lines = req_ref.shape[0]
    rows, width = s_ref.shape
    peers, _, entries = out_ref.shape
    packed = from_ref.shape[0]
    deep = rows // peers
    whole, rest = width // CHUNK, width % CHUNK

    def copies(at, size, q):
        cols = pl.ds(at, size)
        return (
            pltpu.make_async_copy(s_hbm.at[:, cols], s_ref.at[:, cols], s_sems.at[q]),
            pltpu.make_async_copy(inj_hbm.at[:, cols], inj_ref.at[:, cols], inj_sems.at[q]),
        )

    def fetch(at, size, q):
        for copy in copies(at, size, q):
            copy.start()

    def arrive(at, size, q):
        for copy in copies(at, size, q):
            copy.wait()

    fetch(whole * CHUNK, rest, whole)
    for q in range(whole):
        fetch(q * CHUNK, CHUNK, q)
    bus = lax.axis_index("bus_x") * lax.axis_size("bus_z") + lax.axis_index("bus_z")
    base = (bus * width + 1).astype(F32)
    req = req_ref[...]
    lane = iota((lines, 128), 1)
    first = req - base
    second = pltpu.roll(req, 112, 1) - base
    has_first = (first >= 0.0) & (first < float(width))
    has_second = (second >= 0.0) & (second < float(width))
    used = (has_first | has_second) & (first != second) & (lane < CAP)
    mask = jnp.where(used, 1.0, 0.0)
    hits = mask.astype(BF16)
    above = jnp.where(iota((lines, lines), 1) < iota((lines, lines), 0), 1.0, 0.0).astype(BF16)
    ahead = jnp.where(iota((128, 128), 0) < iota((128, 128), 1), 1.0, 0.0).astype(BF16)
    ones = jnp.ones((lines, lines), BF16)
    in_lane = lax.dot_general(ones, hits, NN, preferred_element_type=F32)
    rank = lax.dot_general(above, hits, NN, preferred_element_type=F32) + lax.dot_general(
        in_lane.astype(BF16), ahead, NN, preferred_element_type=F32
    )
    rank = jnp.where(used, rank, -1.0)
    count = jnp.sum(mask).astype(jnp.int32)
    blocks = (count + (packed - 1)) // packed
    first = jnp.where(has_first & used, first + 1.0, 0.0)
    second = jnp.where(has_second & used, second + 1.0, 0.0)
    first_high = jnp.floor(first * (1.0 / 128.0))
    second_high = jnp.floor(second * (1.0 / 128.0))
    fields = (first_high, first - 128.0 * first_high, second_high, second - 128.0 * second_high, rank)
    mixed = pltpu.roll(req, 48, 1)
    for q in reversed(range(5)):
        field = pltpu.roll(fields[q], 16 * q, 1) if q else fields[q]
        mixed = jnp.where(lane < 16 * (q + 1), field, mixed) if q < 4 else jnp.where(lane < 80, field, mixed)
    turn_ref[...] = jnp.transpose(jnp.concatenate([mixed, jnp.zeros((128 - lines, 128), F32)], axis=0))
    pairs = []
    lane_row = iota((8, 128), 1)
    for t in range(CAP // 2):
        even = turn_ref[pl.ds(2 * t, 8, stride=16), :]
        odd = turn_ref[pl.ds(2 * t + 1, 8, stride=16), :]
        pairs.append(jnp.where(lane_row < lines, even, pltpu.roll(odd, lines, 1)))
    table = jnp.concatenate(pairs, axis=1)
    ranks = table[4:5].astype(jnp.int32)
    offs = table[5:6].astype(jnp.int32) - 1
    table_low = table.astype(BF16)
    one, minus, zero = jnp.asarray(1, BF16), jnp.asarray(-1, BF16), jnp.asarray(0, BF16)
    flow_ref[...] = jnp.zeros_like(flow_ref)
    total_ref[...] = jnp.zeros_like(total_ref)

    def open_block(block):
        perm = jnp.where(iota((packed, entries), 0) + block * packed == ranks, 1.0, 0.0).astype(BF16)
        perm_ref[...] = perm
        ends = lax.dot_general(perm, table_low, NT, preferred_element_type=F32)
        start = (128.0 * ends[:, 0:1] + ends[:, 1:2] - 1.0).astype(jnp.int32)
        end = (128.0 * ends[:, 2:3] + ends[:, 3:4] - 1.0).astype(jnp.int32)
        from_ref[...] = jnp.broadcast_to(start, (packed, 128)).astype(jnp.int16)
        to_ref[...] = jnp.broadcast_to(end, (packed, 128)).astype(jnp.int16)
        sum_ref[...] = jnp.zeros_like(sum_ref)

    def pick(at, size):
        columns = []
        for t in range(size // 128):
            spot = (iota((16, 128), 1) + (at + t * 128)).astype(jnp.int16)
            spot = jnp.broadcast_to(spot[None], (packed // 16, 16, 128)).reshape(packed, 128)
            columns.append(
                jnp.where(from_ref[...] == spot, one, jnp.where(to_ref[...] == spot, minus, zero))
            )
        sum_ref[...] += lax.dot_general(
            jnp.concatenate(columns, axis=1), split_ref[:, pl.ds(at, size)], NT, preferred_element_type=F32
        )

    def close_block():
        turned = jnp.transpose(sum_ref[:, :rows] + sum_ref[:, rows:])
        both = lax.dot_general(
            jnp.concatenate(split2(turned), axis=0), perm_ref[...], NN, preferred_element_type=F32
        )
        total_ref[...] += both[:rows] + both[rows:]

    def step(at, size):
        cols = pl.ds(at, size)
        both = jnp.concatenate(split2(s_ref[:, cols]), axis=0)
        split_ref[:, cols] = both
        flow_ref[...] += lax.dot_general(
            jnp.concatenate(split2(inj_ref[:, cols]), axis=0), both, NT, preferred_element_type=F32
        )
        pick(at, size)

    open_block(0)
    arrive(whole * CHUNK, rest, whole)
    step(whole * CHUNK, rest)

    def first_block(q, carry):
        at = pl.multiple_of(q * CHUNK, CHUNK)
        arrive(at, CHUNK, q)
        step(at, CHUNK)
        return carry

    lax.fori_loop(0, whole, first_block, 0)
    close_block()

    def other_block(block, carry):
        open_block(block)
        pick(whole * CHUNK, rest)

        def piece(q, carry):
            pick(pl.multiple_of(q * CHUNK, CHUNK), CHUNK)
            return carry

        lax.fori_loop(0, whole, piece, 0)
        close_block()
        return carry

    lax.fori_loop(1, blocks, other_block, 0)
    part = (
        flow_ref[:HOURS, :rows]
        + (flow_ref[:HOURS, rows:] + flow_ref[HOURS:, :rows])
        + flow_ref[HOURS:, rows:]
    )
    total = total_ref[...]
    own = jnp.sum(jnp.where(iota((rows, entries), 0) == offs, total, 0.0), axis=0, keepdims=True)
    own = [own[:, 128 * t : 128 * t + 128] for t in range(CAP // 2)] + [jnp.zeros((2, 128), F32)]
    extra = jnp.concatenate(
        [part[8 * t : 8 * t + 8] for t in range(4)] + [jnp.concatenate(own, axis=0), jnp.zeros((8, 128), F32)],
        axis=1,
    )
    for b in range(peers):
        out_ref[b, :deep, :] = total[b * deep : (b + 1) * deep]
        out_ref[b, deep:, :] = extra


def reply_kernel(got_ref, req_ref, rate_ref, out_ref, rate_scratch):
    peers = got_ref.shape[0]
    lines = req_ref.shape[0]
    rows = rate_ref.shape[1]
    passes = out_ref.shape[0] // (lines * TILES)
    sub = (got_ref.shape[1] - 8) // passes
    place = lax.axis_index("bus_x") * passes
    total = got_ref[0]
    for b in range(1, peers):
        total = total + got_ref[b]
    sens, rest = total[: passes * sub], total[passes * sub :]
    flows = jnp.concatenate([rest[:, 128 * t : 128 * t + 128] for t in range(4)], axis=0)
    lane = iota((HOURS, 128), 1)
    hour = iota((HOURS, 128), 0)
    f_high, f_low = split2(flows)
    f_rest = (flows - f_high.astype(F32) - f_low.astype(F32)).astype(BF16)
    f_all = jnp.concatenate([f_high, f_low, f_rest], axis=0)
    req = req_ref[...]
    lane_line = iota((lines, 128), 1)
    hots = [
        jnp.where(lane_line == req[:, 32 + c : 33 + c].astype(jnp.int32) - 1, 1.0, 0.0).astype(BF16)
        for c in range(CAP)
    ]
    left = jnp.concatenate([jnp.concatenate(hots[4 * q : 4 * q + 4], axis=1) for q in range(3)], axis=0)

    def diagonal(block):
        blank = jnp.zeros_like(block)
        return jnp.concatenate(
            [jnp.concatenate([block if v == u else blank for v in range(4)], axis=1) for u in range(4)], axis=0
        )

    lost = lax.dot_general(
        left, diagonal(f_high), NT, preferred_element_type=F32
    ) + lax.dot_general(left, diagonal(f_low), NT, preferred_element_type=F32)
    rate_scratch[...] = 0.5 * jnp.transpose(jnp.broadcast_to(rate_ref[...], (rows, 128)))

    def wide(block):
        return jnp.concatenate([block, jnp.zeros((block.shape[0], 128 - lines), F32)], axis=1)

    def put(p, q, block):
        out_ref[pl.ds(p * lines * TILES + q, lines, stride=TILES), :] = block

    for p in range(passes):
        wanted = iota((128, 128), 0) == (place + p) * sub + iota((128, 128), 1) % sub
        spread = lax.dot_general(f_all, jnp.where(wanted, 1.0, 0.0).astype(BF16), NN, preferred_element_type=F32)
        spread = spread[:HOURS] + spread[HOURS : 2 * HOURS] + spread[2 * HOURS :]
        spread = jnp.where(lane // sub == hour % 8, spread, 0.0)
        for t in range(4):
            row = jnp.sum(spread[8 * t : 8 * t + 8], axis=0, keepdims=True)
            put(p, t, jnp.broadcast_to(row, (lines, 128)))
        for q in range(3):
            put(p, 4 + q, lost[q * lines : (q + 1) * lines])
        rate = rate_scratch[pl.ds(pl.multiple_of((place + p) * sub, sub), sub), :]
        part = sens[p * sub : (p + 1) * sub]
        blocks = [wide(part[:, c * lines : (c + 1) * lines]) for c in range(CAP)]
        one = jnp.concatenate(blocks[:8], axis=0)
        two = jnp.concatenate(
            blocks[8:]
            + [rest[:, 512:640], pltpu.roll(rest[:, 512:640], lines, 1), rate, jnp.zeros((32, 128), F32)],
            axis=0,
        )
        put(p, 7, jnp.transpose(one)[:lines])
        put(p, 8, jnp.transpose(two)[:lines])


def screen_kernel(got_ref, mon_ref, off_ref, live_ref, out_ref):
    slots, outages = mon_ref.shape
    sub = out_ref.shape[1]
    passes = lax.axis_size("bus_z")
    lines = got_ref.shape[0] // (passes * TILES)
    place = lax.axis_index("bus_x") * passes + lax.axis_index("bus_z")
    pieces = []
    for t in range(TILES):
        block = got_ref[pl.ds(t, lines, stride=TILES), :]
        for p in range(1, passes):
            block = block + got_ref[pl.ds(p * lines * TILES + t, lines, stride=TILES), :]
        high = block.astype(BF16).astype(F32)
        low = (block - high).astype(BF16).astype(F32)
        pieces.append(jnp.transpose(jnp.concatenate([high, low], axis=0)).astype(BF16))
    shared = jnp.concatenate(pieces[:4] + pieces[7:], axis=0)
    own = jnp.concatenate(pieces[4:7] + pieces[8:], axis=0)
    named = jnp.concatenate([mon_ref[...], mon_ref[...]], axis=1)
    line_row = iota((lines, 128), 0)
    lane = iota((1, 128), 1)
    outage = lane % outages
    names = jnp.zeros((lines, 128), F32)
    for s in range(slots):
        names = jnp.where(named[s : s + 1] == line_row, 1.0, names)
    earlier = iota((128, 128), 0) < iota((128, 128), 1) % outages
    rank = lax.dot_general(
        names.astype(BF16),
        jnp.where(earlier, 1.0, 0.0).astype(BF16),
        (((1,), (0,)), ((), ())),
        preferred_element_type=F32,
    )

    def hot_of(target):
        hot = jnp.where(line_row == target, 1.0, 0.0)
        turn = jnp.sum(hot * rank, axis=0, keepdims=True)
        hot = hot.astype(BF16)
        return jnp.concatenate([hot, hot], axis=0), turn

    plain = (((1,), (0,)), ((), ()))
    hot_own, turn_own = hot_of(named[0:1])
    got_own = lax.dot_general(own, hot_own, plain, preferred_element_type=F32)
    lost = jnp.zeros((HOURS, 128), F32)
    self_sens = jnp.zeros((1, 128), F32)
    for c in range(CAP):
        mine = turn_own == float(c)
        lost = jnp.where(mine, got_own[HOURS * c : HOURS * c + HOURS], lost)
        at = 448 + 8 * (c % 2) + c // 2
        self_sens = jnp.where(mine, got_own[at : at + 1], self_sens)
    divisor = jnp.maximum(1.0 - self_sens, floor_value)
    off = jnp.concatenate([off_ref[...], off_ref[...]], axis=1)
    live = jnp.concatenate([live_ref[...], live_ref[...]], axis=1)
    lost_scaled = lost
    row = iota((sub, 128), 0)
    for t in range(slots // 2):
        target = jnp.where(lane < outages, named[2 * t : 2 * t + 1], named[2 * t + 1 : 2 * t + 2])
        hot, turn = hot_of(target)
        got = lax.dot_general(shared, hot, plain, preferred_element_type=F32)
        sens = jnp.zeros((sub, 128), F32)
        for c in range(CAP):
            sens = jnp.where(turn == float(c), got[512 + sub * c : 512 + sub * c + sub], sens)
        factor = sens / divisor
        worst = jnp.zeros((sub, 128), F32)
        for h in range(HOURS):
            worst = jnp.maximum(worst, jnp.abs(got[sub * h : sub * h + sub] + factor * lost_scaled[h : h + 1]))
        result = worst / got[720:736]
        slot = 2 * t + jnp.where(lane < outages, 0, 1)
        keep = slot < live
        if t == 0:
            keep = keep & ~((slot == 0) & (row == off - place * sub))
        result = jnp.where(keep, result, 0.0)
        out_ref[2 * t] = result[:, :outages]
        out_ref[2 * t + 1] = result[:, outages:]


def call(kernel, out_shape, in_specs, scratch=(), flops=0, moved=0, limit=16):
    return pl.pallas_call(
        kernel,
        out_shape=out_shape,
        in_specs=in_specs,
        out_specs=IN_VMEM,
        scratch_shapes=list(scratch),
        compiler_params=pltpu.CompilerParams(vmem_limit_bytes=limit * 1024 * 1024),
        cost_estimate=pl.CostEstimate(flops=flops, bytes_accessed=moved, transcendentals=0),
    )


def local(shift_factors, injection, rating, monitored, live_count, outage_offset, outage_ends):
    peers = lax.axis_size("bus_x")
    passes = lax.axis_size("bus_z")
    line_count = lax.axis_size("line")
    block_rows, bus_width = shift_factors.shape
    sub_rows = block_rows // (peers * passes)
    outages, slot_count = monitored.shape
    entries = CAP * line_count
    shape = jax.ShapeDtypeStruct
    off_row = outage_offset.reshape(1, outages)
    live_row = live_count.reshape(1, outages)
    rate_row = rating.reshape(1, block_rows)
    named = monitored.T
    with jax.named_scope("requests"):
        requests = call(request_kernel, shape((line_count, 128), F32), [IN_VMEM] * 4, limit=56)(
            named, outage_ends.T, off_row, live_row
        )
        asked = lax.all_to_all(requests, "line", split_axis=0, concat_axis=0, tiled=True)
    with jax.named_scope("picks"):
        partial_sens = call(
            pick_kernel,
            shape((peers, passes * sub_rows + 8, entries), F32),
            [IN_VMEM, IN_HBM, IN_HBM],
            scratch=(
                pltpu.VMEM((block_rows, bus_width), F32),
                pltpu.VMEM((HOURS, bus_width), F32),
                pltpu.VMEM((2 * block_rows, bus_width), BF16),
                pltpu.VMEM((128, 128), F32),
                pltpu.VMEM((PACKED, entries), BF16),
                pltpu.VMEM((PACKED, 128), jnp.int16),
                pltpu.VMEM((PACKED, 128), jnp.int16),
                pltpu.VMEM((PACKED, 2 * block_rows), F32),
                pltpu.VMEM((2 * HOURS, 2 * block_rows), F32),
                pltpu.VMEM((block_rows, entries), F32),
                pltpu.SemaphoreType.DMA((bus_width // CHUNK + 1,)),
                pltpu.SemaphoreType.DMA((bus_width // CHUNK + 1,)),
            ),
            flops=4 * entries * block_rows * bus_width,
            moved=4 * block_rows * bus_width,
            limit=53,
        )(asked, shift_factors, injection)
        half_sens = lax.all_to_all(partial_sens, "bus_x", split_axis=0, concat_axis=0, tiled=True)
    with jax.named_scope("reply"):
        reply = call(
            reply_kernel,
            shape((passes * line_count * TILES, 128), F32),
            [IN_VMEM] * 3,
            scratch=(pltpu.VMEM((block_rows, block_rows), F32),),
        )(half_sens, asked, rate_row)
        reply = reply.reshape(passes * line_count, TILES * 128)
        got = lax.all_to_all(reply, ("bus_z", "line"), split_axis=0, concat_axis=0, tiled=True)
    with jax.named_scope("screen"):
        loading = call(screen_kernel, shape((slot_count, sub_rows, outages), F32), [IN_VMEM] * 4)(
            got.reshape(-1, 128), named, off_row, live_row
        )
    return jnp.transpose(loading, (2, 0, 1))


def solution(mesh):
    lines, buses = mesh.devices.shape
    bus = ("bus_x", "bus_z")
    return jax.shard_map(
        local,
        mesh=jax.sharding.Mesh(mesh.devices.reshape(lines, buses // PASS, PASS), ("line",) + bus),
        in_specs=(
            P("line", bus),
            P(None, bus),
            P("line"),
            P("line", None),
            P("line"),
            P("line"),
            P("line", None),
        ),
        out_specs=P("line", None, bus),
        check_vma=False,
    )
```

```python
import jax
import jax.numpy as jnp
from jax import lax
from jax.experimental import pallas as pl
from jax.experimental.pallas import tpu as pltpu
from jax.sharding import PartitionSpec as P

floor_value = 0.25
F32 = jnp.float32
BF16 = jnp.bfloat16
NT = (((1,), (1,)), ((), ()))
NN = (((1,), (0,)), ((), ()))
HOURS = 32
CAP = 12
CHUNK = 2304
PASS = 2
TILES = 6
PACKED = 256
IN_VMEM = pl.BlockSpec(memory_space=pltpu.VMEM)
IN_HBM = pl.BlockSpec(memory_space=pltpu.HBM)


def iota(shape, axis):
    return lax.broadcasted_iota(jnp.int32, shape, axis)


def split2(value):
    high = value.astype(BF16)
    return high, (value - high.astype(F32)).astype(BF16)


def request_kernel(mon_ref, ends_ref, off_ref, live_ref, out_ref):
    slots, outages = mon_ref.shape
    lines = out_ref.shape[0]

    def twice(row):
        return jnp.concatenate([row, row], axis=1)

    named = twice(mon_ref[...])
    line_row = iota((lines, 128), 0)
    live = twice(live_ref[...])
    names = jnp.zeros((lines, 128), F32)
    asks = jnp.zeros((lines, 128), F32)
    for s in range(slots):
        same = named[s : s + 1] == line_row
        names = jnp.where(same, 1.0, names)
        asks = jnp.where(same & (s < live), 1.0, asks)
    earlier = iota((128, 128), 0) < iota((128, 128), 1) % outages
    rank = lax.dot_general(
        names.astype(BF16), jnp.where(earlier, 1.0, 0.0).astype(BF16), NN, preferred_element_type=F32
    )
    rank = jnp.where(asks > 0.0, rank, -1.0)
    start = twice(ends_ref[0:1, :]) + 1
    end = twice(ends_ref[1:2, :]) + 1
    place = twice(off_ref[...]) + 1
    second = iota((1, 128), 1) // outages
    spot = iota((128, 128), 0)
    chosen, high, low = [], [], []
    for t in range(CAP // 2):
        turn = 2 * t + second
        chosen.append(jnp.where(rank == turn.astype(F32), 1.0, 0.0).astype(BF16))
        value = jnp.where(
            spot == turn, start, jnp.where(spot == 16 + turn, end, jnp.where(spot == 32 + turn, place, 0))
        )
        high.append((value >> 8).astype(F32).astype(BF16))
        low.append((value & 255).astype(F32).astype(BF16))
    chosen = jnp.concatenate(chosen, axis=1)
    high = lax.dot_general(chosen, jnp.concatenate(high, axis=1), NT, preferred_element_type=F32)
    low = lax.dot_general(chosen, jnp.concatenate(low, axis=1), NT, preferred_element_type=F32)
    out_ref[...] = 256.0 * high + low


def flow_kernel(s_hbm, inj_hbm, part_ref, s_ref, inj_ref, flow_ref, s_sems, inj_sems):
    rows, width = s_ref.shape
    whole, rest = width // CHUNK, width % CHUNK

    def copies(at, size, q):
        cols = pl.ds(at, size)
        return (
            pltpu.make_async_copy(s_hbm.at[:, cols], s_ref.at[:, cols], s_sems.at[q]),
            pltpu.make_async_copy(inj_hbm.at[:, cols], inj_ref.at[:, cols], inj_sems.at[q]),
        )

    def fetch(at, size, q):
        for copy in copies(at, size, q):
            copy.start()

    def step(at, size, q):
        for copy in copies(at, size, q):
            copy.wait()
        cols = pl.ds(at, size)
        flow_ref[...] += lax.dot_general(
            jnp.concatenate(split2(inj_ref[:, cols]), axis=0),
            jnp.concatenate(split2(s_ref[:, cols]), axis=0),
            NT,
            preferred_element_type=F32,
        )

    for q in range(whole):
        fetch(q * CHUNK, CHUNK, q)
    fetch(whole * CHUNK, rest, whole)
    flow_ref[...] = jnp.zeros_like(flow_ref)

    def body(q, carry):
        step(pl.multiple_of(q * CHUNK, CHUNK), CHUNK, q)
        return carry

    lax.fori_loop(0, whole, body, 0)
    step(whole * CHUNK, rest, whole)
    part_ref[...] = (
        flow_ref[:HOURS, :rows]
        + (flow_ref[:HOURS, rows:] + flow_ref[HOURS:, :rows])
        + flow_ref[HOURS:, rows:]
    )


def pick_kernel(
    req_ref,
    s_hbm,
    out_ref,
    s_ref,
    split_ref,
    turn_ref,
    perm_ref,
    from_ref,
    to_ref,
    sum_ref,
    total_ref,
    s_sems,
):
    lines = req_ref.shape[0]
    rows, width = s_ref.shape
    peers, _, entries = out_ref.shape
    packed = from_ref.shape[0]
    deep = rows // peers
    whole, rest = width // CHUNK, width % CHUNK

    def copy(at, size, q):
        cols = pl.ds(at, size)
        return pltpu.make_async_copy(s_hbm.at[:, cols], s_ref.at[:, cols], s_sems.at[q])

    copy(whole * CHUNK, rest, whole).start()
    for q in range(whole):
        copy(q * CHUNK, CHUNK, q).start()
    bus = lax.axis_index("bus_x") * lax.axis_size("bus_z") + lax.axis_index("bus_z")
    base = (bus * width + 1).astype(F32)
    req = req_ref[...]
    lane = iota((lines, 128), 1)
    first = req - base
    second = pltpu.roll(req, 112, 1) - base
    has_first = (first >= 0.0) & (first < float(width))
    has_second = (second >= 0.0) & (second < float(width))
    used = (has_first | has_second) & (first != second) & (lane < CAP)
    mask = jnp.where(used, 1.0, 0.0)
    hits = mask.astype(BF16)
    above = jnp.where(iota((lines, lines), 1) < iota((lines, lines), 0), 1.0, 0.0).astype(BF16)
    ahead = jnp.where(iota((128, 128), 0) < iota((128, 128), 1), 1.0, 0.0).astype(BF16)
    ones = jnp.ones((lines, lines), BF16)
    in_lane = lax.dot_general(ones, hits, NN, preferred_element_type=F32)
    rank = lax.dot_general(above, hits, NN, preferred_element_type=F32) + lax.dot_general(
        in_lane.astype(BF16), ahead, NN, preferred_element_type=F32
    )
    rank = jnp.where(used, rank, -1.0)
    count = jnp.sum(mask).astype(jnp.int32)
    blocks = (count + (packed - 1)) // packed
    first = jnp.where(has_first & used, first + 1.0, 0.0)
    second = jnp.where(has_second & used, second + 1.0, 0.0)
    first_high = jnp.floor(first * (1.0 / 128.0))
    second_high = jnp.floor(second * (1.0 / 128.0))
    fields = (first_high, first - 128.0 * first_high, second_high, second - 128.0 * second_high, rank)
    mixed = pltpu.roll(req, 48, 1)
    for q in reversed(range(5)):
        field = pltpu.roll(fields[q], 16 * q, 1) if q else fields[q]
        mixed = jnp.where(lane < 16 * (q + 1), field, mixed) if q < 4 else jnp.where(lane < 80, field, mixed)
    turn_ref[...] = jnp.transpose(jnp.concatenate([mixed, jnp.zeros((128 - lines, 128), F32)], axis=0))
    pairs = []
    lane_row = iota((8, 128), 1)
    for t in range(CAP // 2):
        even = turn_ref[pl.ds(2 * t, 8, stride=16), :]
        odd = turn_ref[pl.ds(2 * t + 1, 8, stride=16), :]
        pairs.append(jnp.where(lane_row < lines, even, pltpu.roll(odd, lines, 1)))
    table = jnp.concatenate(pairs, axis=1)
    ranks = table[4:5].astype(jnp.int32)
    offs = table[5:6].astype(jnp.int32) - 1
    table_low = table.astype(BF16)
    one, minus, zero = jnp.asarray(1, BF16), jnp.asarray(-1, BF16), jnp.asarray(0, BF16)
    total_ref[...] = jnp.zeros_like(total_ref)

    def open_block(block):
        perm = jnp.where(iota((packed, entries), 0) + block * packed == ranks, 1.0, 0.0).astype(BF16)
        perm_ref[...] = perm
        ends = lax.dot_general(perm, table_low, NT, preferred_element_type=F32)
        start = (128.0 * ends[:, 0:1] + ends[:, 1:2] - 1.0).astype(jnp.int32)
        end = (128.0 * ends[:, 2:3] + ends[:, 3:4] - 1.0).astype(jnp.int32)
        from_ref[...] = jnp.broadcast_to(start, (packed, 128)).astype(jnp.int16)
        to_ref[...] = jnp.broadcast_to(end, (packed, 128)).astype(jnp.int16)
        sum_ref[...] = jnp.zeros_like(sum_ref)

    def pick(at, size):
        columns = []
        for t in range(size // 128):
            spot = (iota((16, 128), 1) + (at + t * 128)).astype(jnp.int16)
            spot = jnp.broadcast_to(spot[None], (packed // 16, 16, 128)).reshape(packed, 128)
            columns.append(
                jnp.where(from_ref[...] == spot, one, jnp.where(to_ref[...] == spot, minus, zero))
            )
        sum_ref[...] += lax.dot_general(
            jnp.concatenate(columns, axis=1), split_ref[:, pl.ds(at, size)], NT, preferred_element_type=F32
        )

    def close_block():
        turned = jnp.transpose(sum_ref[:, :rows] + sum_ref[:, rows:])
        both = lax.dot_general(
            jnp.concatenate(split2(turned), axis=0), perm_ref[...], NN, preferred_element_type=F32
        )
        total_ref[...] += both[:rows] + both[rows:]

    def step(at, size):
        cols = pl.ds(at, size)
        both = jnp.concatenate(split2(s_ref[:, cols]), axis=0)
        split_ref[:, cols] = both
        pick(at, size)

    open_block(0)
    copy(whole * CHUNK, rest, whole).wait()
    step(whole * CHUNK, rest)

    def first_block(q, carry):
        at = pl.multiple_of(q * CHUNK, CHUNK)
        copy(at, CHUNK, q).wait()
        step(at, CHUNK)
        return carry

    lax.fori_loop(0, whole, first_block, 0)
    close_block()

    def other_block(block, carry):
        open_block(block)
        pick(whole * CHUNK, rest)

        def piece(q, carry):
            pick(pl.multiple_of(q * CHUNK, CHUNK), CHUNK)
            return carry

        lax.fori_loop(0, whole, piece, 0)
        close_block()
        return carry

    lax.fori_loop(1, blocks, other_block, 0)
    total = total_ref[...]
    own = jnp.sum(jnp.where(iota((rows, entries), 0) == offs, total, 0.0), axis=0, keepdims=True)
    own = [own[:, 128 * t : 128 * t + 128] for t in range(CAP // 2)] + [jnp.zeros((2, 128), F32)]
    own = jnp.concatenate(own, axis=0)
    for b in range(peers):
        out_ref[b, :deep, :] = total[b * deep : (b + 1) * deep]
        out_ref[b, deep:, :512] = jnp.zeros((8, 512), F32)
        out_ref[b, deep:, 512:640] = own
        out_ref[b, deep:, 640:] = jnp.zeros((8, 128), F32)


def merge_kernel(message_ref, mine_ref, other_ref, out_ref):
    flows = mine_ref[...] + other_ref[...]
    flows = jnp.concatenate([flows[8 * t : 8 * t + 8] for t in range(4)], axis=1)
    deep = out_ref.shape[1] - 8
    for b in range(out_ref.shape[0]):
        out_ref[b, :deep, :] = message_ref[b, :deep, :]
        out_ref[b, deep:, :512] = flows
        out_ref[b, deep:, 512:] = message_ref[b, deep:, 512:]


def reply_kernel(got_ref, req_ref, rate_ref, out_ref, rate_scratch):
    peers = got_ref.shape[0]
    lines = req_ref.shape[0]
    rows = rate_ref.shape[1]
    passes = out_ref.shape[0] // (lines * TILES)
    sub = (got_ref.shape[1] - 8) // passes
    half = HOURS // passes
    place = lax.axis_index("bus_x") * passes
    total = got_ref[0]
    for b in range(1, peers):
        total = total + got_ref[b]
    sens, rest = total[: passes * sub], total[passes * sub :]
    flows = jnp.where(
        lax.axis_index("bus_z") == 0,
        jnp.concatenate([rest[:, 0:128], rest[:, 128:256]], axis=0),
        jnp.concatenate([rest[:, 256:384], rest[:, 384:512]], axis=0),
    )
    lane = iota((half, 128), 1)
    hour = iota((half, 128), 0)
    f_high, f_low = split2(flows)
    f_rest = (flows - f_high.astype(F32) - f_low.astype(F32)).astype(BF16)
    f_all = jnp.concatenate([f_high, f_low, f_rest], axis=0)
    req = req_ref[...]
    lane_line = iota((lines, 128), 1)
    hots = [
        jnp.where(lane_line == req[:, 32 + c : 33 + c].astype(jnp.int32) - 1, 1.0, 0.0).astype(BF16)
        for c in range(CAP)
    ] + [jnp.zeros((lines, 128), BF16)] * 4
    left = jnp.concatenate([jnp.concatenate(hots[8 * q : 8 * q + 8], axis=1) for q in range(2)], axis=0)

    def diagonal(block):
        blank = jnp.zeros_like(block)
        return jnp.concatenate(
            [jnp.concatenate([block if v == u else blank for v in range(8)], axis=1) for u in range(8)], axis=0
        )

    lost = lax.dot_general(
        left, diagonal(f_high), NT, preferred_element_type=F32
    ) + lax.dot_general(left, diagonal(f_low), NT, preferred_element_type=F32)
    rate_scratch[...] = 0.5 * jnp.transpose(jnp.broadcast_to(rate_ref[...], (rows, 128)))

    def wide(block):
        return jnp.concatenate([block, jnp.zeros((block.shape[0], 128 - lines), F32)], axis=1)

    def put(p, q, block):
        out_ref[pl.ds(p * lines * TILES + q, lines, stride=TILES), :] = block

    for p in range(passes):
        wanted = iota((128, 128), 0) == (place + p) * sub + iota((128, 128), 1) % sub
        spread = lax.dot_general(f_all, jnp.where(wanted, 1.0, 0.0).astype(BF16), NN, preferred_element_type=F32)
        spread = spread[:half] + spread[half : 2 * half] + spread[2 * half :]
        spread = jnp.where(lane // sub == hour % 8, spread, 0.0)
        for t in range(2):
            row = jnp.sum(spread[8 * t : 8 * t + 8], axis=0, keepdims=True)
            put(p, t, jnp.broadcast_to(row, (lines, 128)))
        rate = rate_scratch[pl.ds(pl.multiple_of((place + p) * sub, sub), sub), :]
        part = sens[p * sub : (p + 1) * sub]
        blocks = [wide(part[:, c * lines : (c + 1) * lines]) for c in range(CAP)]
        one = jnp.concatenate(blocks[:8], axis=0)
        two = jnp.concatenate([jnp.zeros((64, 128), F32)] + blocks[8:], axis=0)
        three = jnp.concatenate(
            [rest[:, 512:640], pltpu.roll(rest[:, 512:640], lines, 1), rate, jnp.zeros((96, 128), F32)], axis=0
        )
        put(p, 2, lost[:lines])
        put(p, 3, jnp.where(lane_line < 64, lost[lines:], jnp.transpose(two)[:lines]))
        put(p, 4, jnp.transpose(one)[:lines])
        put(p, 5, jnp.transpose(three)[:lines])


def screen_kernel(got_ref, mon_ref, off_ref, live_ref, out_ref):
    slots, outages = mon_ref.shape
    sub = out_ref.shape[1]
    passes = lax.axis_size("bus_z")
    lines = got_ref.shape[0] // (passes * TILES)
    place = lax.axis_index("bus_x") * passes + lax.axis_index("bus_z")
    half = HOURS // passes

    def tile(p, t):
        return got_ref[pl.ds(p * lines * TILES + t, lines, stride=TILES), :]

    def piece(block):
        high = block.astype(BF16).astype(F32)
        low = (block - high).astype(BF16).astype(F32)
        return jnp.transpose(jnp.concatenate([high, low], axis=0)).astype(BF16)

    sums = [piece(tile(0, t) + tile(1, t)) for t in (4, 3, 5)]
    shared = jnp.concatenate([piece(tile(p, t)) for p in range(passes) for t in range(2)] + sums, axis=0)
    own = jnp.concatenate([piece(tile(p, t)) for p in range(passes) for t in range(2, 4)] + sums[2:], axis=0)
    named = jnp.concatenate([mon_ref[...], mon_ref[...]], axis=1)
    line_row = iota((lines, 128), 0)
    lane = iota((1, 128), 1)
    outage = lane % outages
    names = jnp.zeros((lines, 128), F32)
    for s in range(slots):
        names = jnp.where(named[s : s + 1] == line_row, 1.0, names)
    earlier = iota((128, 128), 0) < iota((128, 128), 1) % outages
    rank = lax.dot_general(
        names.astype(BF16),
        jnp.where(earlier, 1.0, 0.0).astype(BF16),
        (((1,), (0,)), ((), ())),
        preferred_element_type=F32,
    )

    def hot_of(target):
        hot = jnp.where(line_row == target, 1.0, 0.0)
        turn = jnp.sum(hot * rank, axis=0, keepdims=True)
        hot = hot.astype(BF16)
        return jnp.concatenate([hot, hot], axis=0), turn

    plain = (((1,), (0,)), ((), ()))
    hot_own, turn_own = hot_of(named[0:1])
    got_own = lax.dot_general(own, hot_own, plain, preferred_element_type=F32)
    lost = [jnp.zeros((half, 128), F32)] * passes
    self_sens = jnp.zeros((1, 128), F32)
    for c in range(CAP):
        mine = turn_own == float(c)
        for p in range(passes):
            at = 256 * p + half * c
            lost[p] = jnp.where(mine, got_own[at : at + half], lost[p])
        at = 512 + 8 * (c % 2) + c // 2
        self_sens = jnp.where(mine, got_own[at : at + 1], self_sens)
    lost = jnp.concatenate(lost, axis=0)
    divisor = jnp.maximum(1.0 - self_sens, floor_value)
    off = jnp.concatenate([off_ref[...], off_ref[...]], axis=1)
    live = jnp.concatenate([live_ref[...], live_ref[...]], axis=1)
    row = iota((sub, 128), 0)
    for t in range(slots // 2):
        target = jnp.where(lane < outages, named[2 * t : 2 * t + 1], named[2 * t + 1 : 2 * t + 2])
        hot, turn = hot_of(target)
        got = lax.dot_general(shared, hot, plain, preferred_element_type=F32)
        sens = jnp.zeros((sub, 128), F32)
        for c in range(CAP):
            at = 512 + sub * c + (64 if c >= 8 else 0)
            sens = jnp.where(turn == float(c), got[at : at + sub], sens)
        factor = sens / divisor
        worst = jnp.zeros((sub, 128), F32)
        for h in range(HOURS):
            worst = jnp.maximum(worst, jnp.abs(got[sub * h : sub * h + sub] + factor * lost[h : h + 1]))
        result = worst / got[784:800]
        slot = 2 * t + jnp.where(lane < outages, 0, 1)
        keep = slot < live
        if t == 0:
            keep = keep & ~((slot == 0) & (row == off - place * sub))
        result = jnp.where(keep, result, 0.0)
        out_ref[2 * t] = result[:, :outages]
        out_ref[2 * t + 1] = result[:, outages:]


def call(kernel, out_shape, in_specs, scratch=(), flops=0, moved=0, limit=16):
    return pl.pallas_call(
        kernel,
        out_shape=out_shape,
        in_specs=in_specs,
        out_specs=IN_VMEM,
        scratch_shapes=list(scratch),
        compiler_params=pltpu.CompilerParams(vmem_limit_bytes=limit * 1024 * 1024),
        cost_estimate=pl.CostEstimate(flops=flops, bytes_accessed=moved, transcendentals=0),
    )


def local(shift_factors, injection, rating, monitored, live_count, outage_offset, outage_ends):
    peers = lax.axis_size("bus_x")
    passes = lax.axis_size("bus_z")
    line_count = lax.axis_size("line")
    block_rows, bus_width = shift_factors.shape
    sub_rows = block_rows // (peers * passes)
    outages, slot_count = monitored.shape
    entries = CAP * line_count
    shape = jax.ShapeDtypeStruct
    off_row = outage_offset.reshape(1, outages)
    live_row = live_count.reshape(1, outages)
    rate_row = rating.reshape(1, block_rows)
    named = monitored.T
    with jax.named_scope("requests"):
        requests = call(request_kernel, shape((line_count, 128), F32), [IN_VMEM] * 4, limit=56)(
            named, outage_ends.T, off_row, live_row
        )
        asked = lax.all_to_all(requests, "line", split_axis=0, concat_axis=0, tiled=True)
    pieces = bus_width // CHUNK + 1
    with jax.named_scope("flows"):
        mine = call(
            flow_kernel,
            shape((HOURS, block_rows), F32),
            [IN_HBM, IN_HBM],
            scratch=(
                pltpu.VMEM((block_rows, bus_width), F32),
                pltpu.VMEM((HOURS, bus_width), F32),
                pltpu.VMEM((2 * HOURS, 2 * block_rows), F32),
                pltpu.SemaphoreType.DMA((pieces,)),
                pltpu.SemaphoreType.DMA((pieces,)),
            ),
            flops=8 * HOURS * block_rows * bus_width,
            moved=4 * block_rows * bus_width,
            limit=54,
        )(shift_factors, injection)
        other = lax.ppermute(mine, "bus_z", [(p, (p + 1) % passes) for p in range(passes)])
    with jax.named_scope("picks"):
        partial_sens = call(
            pick_kernel,
            shape((peers, passes * sub_rows + 8, entries), F32),
            [IN_VMEM, IN_HBM],
            scratch=(
                pltpu.VMEM((block_rows, bus_width), F32),
                pltpu.VMEM((2 * block_rows, bus_width), BF16),
                pltpu.VMEM((128, 128), F32),
                pltpu.VMEM((PACKED, entries), BF16),
                pltpu.VMEM((PACKED, 128), jnp.int16),
                pltpu.VMEM((PACKED, 128), jnp.int16),
                pltpu.VMEM((PACKED, 2 * block_rows), F32),
                pltpu.VMEM((block_rows, entries), F32),
                pltpu.SemaphoreType.DMA((pieces,)),
            ),
            flops=4 * entries * block_rows * bus_width,
            moved=4 * block_rows * bus_width,
            limit=53,
        )(asked, shift_factors)
        partial_sens = call(merge_kernel, shape((peers, passes * sub_rows + 8, entries), F32), [IN_VMEM] * 3)(
            partial_sens, mine, other
        )
        half_sens = lax.all_to_all(partial_sens, "bus_x", split_axis=0, concat_axis=0, tiled=True)
    with jax.named_scope("reply"):
        reply = call(
            reply_kernel,
            shape((passes * line_count * TILES, 128), F32),
            [IN_VMEM] * 3,
            scratch=(pltpu.VMEM((block_rows, block_rows), F32),),
        )(half_sens, asked, rate_row)
        reply = reply.reshape(passes * line_count, TILES * 128)
        got = lax.all_to_all(reply, ("bus_z", "line"), split_axis=0, concat_axis=0, tiled=True)
    with jax.named_scope("screen"):
        loading = call(screen_kernel, shape((slot_count, sub_rows, outages), F32), [IN_VMEM] * 4)(
            got.reshape(-1, 128), named, off_row, live_row
        )
    return jnp.transpose(loading, (2, 0, 1))


def solution(mesh):
    lines, buses = mesh.devices.shape
    bus = ("bus_x", "bus_z")
    return jax.shard_map(
        local,
        mesh=jax.sharding.Mesh(mesh.devices.reshape(lines, buses // PASS, PASS), ("line",) + bus),
        in_specs=(
            P("line", bus),
            P(None, bus),
            P("line"),
            P("line", None),
            P("line"),
            P("line"),
            P("line", None),
        ),
        out_specs=P("line", None, bus),
        check_vma=False,
    )
```

```python
import jax
import jax.numpy as jnp
from jax import lax
from jax.experimental import pallas as pl
from jax.experimental.pallas import tpu as pltpu
from jax.sharding import PartitionSpec as P

floor_value = 0.25
F32 = jnp.float32
BF16 = jnp.bfloat16
NT = (((1,), (1,)), ((), ()))
NN = (((1,), (0,)), ((), ()))
HOURS = 32
CAP = 12
CHUNK = 2304
PASS = 2
TILES = 9
PACKED = 256
IN_VMEM = pl.BlockSpec(memory_space=pltpu.VMEM)


def iota(shape, axis):
    return lax.broadcasted_iota(jnp.int32, shape, axis)


def split2(value):
    high = value.astype(BF16)
    return high, (value - high.astype(F32)).astype(BF16)


def request_kernel(table_ref, out_ref):
    outages = table_ref.shape[1]
    slots = table_ref.shape[0] - 4
    lines = out_ref.shape[0]
    table = table_ref[...]
    table = jnp.concatenate([table, table], axis=1)
    named = table[:slots]
    line_row = iota((lines, 128), 0)
    live = table[slots + 3 : slots + 4]
    names = jnp.zeros((lines, 128), F32)
    asks = jnp.zeros((lines, 128), F32)
    for s in range(slots):
        same = named[s : s + 1] == line_row
        names = jnp.where(same, 1.0, names)
        asks = jnp.where(same & (s < live), 1.0, asks)
    earlier = iota((128, 128), 0) < iota((128, 128), 1) % outages
    rank = lax.dot_general(
        names.astype(BF16), jnp.where(earlier, 1.0, 0.0).astype(BF16), NN, preferred_element_type=F32
    )
    rank = jnp.where(asks > 0.0, rank, -1.0)
    start = table[slots : slots + 1] + 1
    end = table[slots + 1 : slots + 2] + 1
    place = table[slots + 2 : slots + 3] + 1
    second = iota((1, 128), 1) // outages
    spot = iota((128, 128), 0)
    chosen, high, low = [], [], []
    for t in range(CAP // 2):
        turn = 2 * t + second
        chosen.append(jnp.where(rank == turn.astype(F32), 1.0, 0.0).astype(BF16))
        value = jnp.where(
            spot == turn, start, jnp.where(spot == 16 + turn, end, jnp.where(spot == 32 + turn, place, 0))
        )
        high.append((value >> 8).astype(F32).astype(BF16))
        low.append((value & 255).astype(F32).astype(BF16))
    chosen = jnp.concatenate(chosen, axis=1)
    high = lax.dot_general(chosen, jnp.concatenate(high, axis=1), NT, preferred_element_type=F32)
    low = lax.dot_general(chosen, jnp.concatenate(low, axis=1), NT, preferred_element_type=F32)
    out_ref[...] = 256.0 * high + low


def pick_kernel(
    req_ref,
    s_ref,
    inj_ref,
    out_ref,
    split_ref,
    turn_ref,
    perm_ref,
    from_ref,
    to_ref,
    sum_ref,
    flow_ref,
    total_ref,
):
    lines = req_ref.shape[0]
    rows, width = s_ref.shape
    peers, _, entries = out_ref.shape
    packed = from_ref.shape[0]
    deep = rows // peers
    whole, rest = width // CHUNK, width % CHUNK

    bus = lax.axis_index("bus_x") * lax.axis_size("bus_z") + lax.axis_index("bus_z")
    base = (bus * width + 1).astype(F32)
    req = req_ref[...]
    lane = iota((lines, 128), 1)
    first = req - base
    second = pltpu.roll(req, 112, 1) - base
    has_first = (first >= 0.0) & (first < float(width))
    has_second = (second >= 0.0) & (second < float(width))
    used = (has_first | has_second) & (first != second) & (lane < CAP)
    mask = jnp.where(used, 1.0, 0.0)
    hits = mask.astype(BF16)
    above = jnp.where(iota((lines, lines), 1) < iota((lines, lines), 0), 1.0, 0.0).astype(BF16)
    ahead = jnp.where(iota((128, 128), 0) < iota((128, 128), 1), 1.0, 0.0).astype(BF16)
    ones = jnp.ones((lines, lines), BF16)
    in_lane = lax.dot_general(ones, hits, NN, preferred_element_type=F32)
    rank = lax.dot_general(above, hits, NN, preferred_element_type=F32) + lax.dot_general(
        in_lane.astype(BF16), ahead, NN, preferred_element_type=F32
    )
    rank = jnp.where(used, rank, -1.0)
    count = jnp.sum(mask).astype(jnp.int32)
    blocks = (count + (packed - 1)) // packed
    first = jnp.where(has_first & used, first + 1.0, 0.0)
    second = jnp.where(has_second & used, second + 1.0, 0.0)
    first_high = jnp.floor(first * (1.0 / 128.0))
    second_high = jnp.floor(second * (1.0 / 128.0))
    fields = (first_high, first - 128.0 * first_high, second_high, second - 128.0 * second_high, rank)
    mixed = pltpu.roll(req, 48, 1)
    for q in reversed(range(5)):
        field = pltpu.roll(fields[q], 16 * q, 1) if q else fields[q]
        mixed = jnp.where(lane < 16 * (q + 1), field, mixed) if q < 4 else jnp.where(lane < 80, field, mixed)
    turn_ref[...] = jnp.transpose(jnp.concatenate([mixed, jnp.zeros((128 - lines, 128), F32)], axis=0))
    pairs = []
    lane_row = iota((8, 128), 1)
    for t in range(CAP // 2):
        even = turn_ref[pl.ds(2 * t, 8, stride=16), :]
        odd = turn_ref[pl.ds(2 * t + 1, 8, stride=16), :]
        pairs.append(jnp.where(lane_row < lines, even, pltpu.roll(odd, lines, 1)))
    table = jnp.concatenate(pairs, axis=1)
    ranks = table[4:5].astype(jnp.int32)
    offs = table[5:6].astype(jnp.int32) - 1
    table_low = table.astype(BF16)
    one, minus, zero = jnp.asarray(1, BF16), jnp.asarray(-1, BF16), jnp.asarray(0, BF16)
    flow_ref[...] = jnp.zeros_like(flow_ref)
    total_ref[...] = jnp.zeros_like(total_ref)

    def open_block(block):
        perm = jnp.where(iota((packed, entries), 0) + block * packed == ranks, 1.0, 0.0).astype(BF16)
        perm_ref[...] = perm
        ends = lax.dot_general(perm, table_low, NT, preferred_element_type=F32)
        start = (128.0 * ends[:, 0:1] + ends[:, 1:2] - 1.0).astype(jnp.int32)
        end = (128.0 * ends[:, 2:3] + ends[:, 3:4] - 1.0).astype(jnp.int32)
        from_ref[...] = jnp.broadcast_to(start, (packed, 128)).astype(jnp.int16)
        to_ref[...] = jnp.broadcast_to(end, (packed, 128)).astype(jnp.int16)
        sum_ref[...] = jnp.zeros_like(sum_ref)

    def pick(at, size):
        columns = []
        for t in range(size // 128):
            spot = (iota((16, 128), 1) + (at + t * 128)).astype(jnp.int16)
            spot = jnp.broadcast_to(spot[None], (packed // 16, 16, 128)).reshape(packed, 128)
            columns.append(
                jnp.where(from_ref[...] == spot, one, jnp.where(to_ref[...] == spot, minus, zero))
            )
        sum_ref[...] += lax.dot_general(
            jnp.concatenate(columns, axis=1), split_ref[:, pl.ds(at, size)], NT, preferred_element_type=F32
        )

    def close_block():
        turned = jnp.transpose(sum_ref[:, :rows] + sum_ref[:, rows:])
        both = lax.dot_general(
            jnp.concatenate(split2(turned), axis=0), perm_ref[...], NN, preferred_element_type=F32
        )
        total_ref[...] += both[:rows] + both[rows:]

    def step(at, size):
        cols = pl.ds(at, size)
        both = jnp.concatenate(split2(s_ref[:, cols]), axis=0)
        split_ref[:, cols] = both
        flow_ref[...] += lax.dot_general(
            jnp.concatenate(split2(inj_ref[:, cols]), axis=0), both, NT, preferred_element_type=F32
        )
        pick(at, size)

    open_block(0)
    step(whole * CHUNK, rest)

    def first_block(q, carry):
        at = pl.multiple_of(q * CHUNK, CHUNK)
        step(at, CHUNK)
        return carry

    lax.fori_loop(0, whole, first_block, 0)
    close_block()

    def other_block(block, carry):
        open_block(block)
        pick(whole * CHUNK, rest)

        def piece(q, carry):
            pick(pl.multiple_of(q * CHUNK, CHUNK), CHUNK)
            return carry

        lax.fori_loop(0, whole, piece, 0)
        close_block()
        return carry

    lax.fori_loop(1, blocks, other_block, 0)
    part = (
        flow_ref[:HOURS, :rows]
        + (flow_ref[:HOURS, rows:] + flow_ref[HOURS:, :rows])
        + flow_ref[HOURS:, rows:]
    )
    total = total_ref[...]
    own = jnp.sum(jnp.where(iota((rows, entries), 0) == offs, total, 0.0), axis=0, keepdims=True)
    own = [own[:, 128 * t : 128 * t + 128] for t in range(CAP // 2)] + [jnp.zeros((2, 128), F32)]
    extra = jnp.concatenate(
        [part[8 * t : 8 * t + 8] for t in range(4)] + [jnp.concatenate(own, axis=0), jnp.zeros((8, 128), F32)],
        axis=1,
    )
    for b in range(peers):
        out_ref[b, :deep, :] = total[b * deep : (b + 1) * deep]
        out_ref[b, deep:, :] = extra


def reply_kernel(got_ref, req_ref, rate_ref, out_ref, rate_scratch):
    peers = got_ref.shape[0]
    lines = req_ref.shape[0]
    rows = rate_ref.shape[1]
    passes = out_ref.shape[0] // (lines * TILES)
    sub = (got_ref.shape[1] - 8) // passes
    place = lax.axis_index("bus_x") * passes
    total = got_ref[0]
    for b in range(1, peers):
        total = total + got_ref[b]
    sens, rest = total[: passes * sub], total[passes * sub :]
    flows = jnp.concatenate([rest[:, 128 * t : 128 * t + 128] for t in range(4)], axis=0)
    lane = iota((HOURS, 128), 1)
    hour = iota((HOURS, 128), 0)
    f_high, f_low = split2(flows)
    f_rest = (flows - f_high.astype(F32) - f_low.astype(F32)).astype(BF16)
    f_all = jnp.concatenate([f_high, f_low, f_rest], axis=0)
    req = req_ref[...]
    lane_line = iota((lines, 128), 1)
    hots = [
        jnp.where(lane_line == req[:, 32 + c : 33 + c].astype(jnp.int32) - 1, 1.0, 0.0).astype(BF16)
        for c in range(CAP)
    ]
    left = jnp.concatenate([jnp.concatenate(hots[4 * q : 4 * q + 4], axis=1) for q in range(3)], axis=0)

    def diagonal(block):
        blank = jnp.zeros_like(block)
        return jnp.concatenate(
            [jnp.concatenate([block if v == u else blank for v in range(4)], axis=1) for u in range(4)], axis=0
        )

    lost = lax.dot_general(
        left, diagonal(f_high), NT, preferred_element_type=F32
    ) + lax.dot_general(left, diagonal(f_low), NT, preferred_element_type=F32)
    rate_scratch[...] = 0.5 * jnp.transpose(jnp.broadcast_to(rate_ref[...], (rows, 128)))

    def wide(block):
        return jnp.concatenate([block, jnp.zeros((block.shape[0], 128 - lines), F32)], axis=1)

    def put(p, q, block):
        out_ref[pl.ds(p * TILES + q, lines, stride=passes * TILES), :] = block

    for p in range(passes):
        wanted = iota((128, 128), 0) == (place + p) * sub + iota((128, 128), 1) % sub
        spread = lax.dot_general(f_all, jnp.where(wanted, 1.0, 0.0).astype(BF16), NN, preferred_element_type=F32)
        spread = spread[:HOURS] + spread[HOURS : 2 * HOURS] + spread[2 * HOURS :]
        spread = jnp.where(lane // sub == hour % 8, spread, 0.0)
        for t in range(4):
            row = jnp.sum(spread[8 * t : 8 * t + 8], axis=0, keepdims=True)
            put(p, t, jnp.broadcast_to(row, (lines, 128)))
        for q in range(3):
            put(p, 4 + q, lost[q * lines : (q + 1) * lines])
        rate = rate_scratch[pl.ds(pl.multiple_of((place + p) * sub, sub), sub), :]
        part = sens[p * sub : (p + 1) * sub]
        blocks = [wide(part[:, c * lines : (c + 1) * lines]) for c in range(CAP)]
        one = jnp.concatenate(blocks[:8], axis=0)
        two = jnp.concatenate(
            blocks[8:]
            + [rest[:, 512:640], pltpu.roll(rest[:, 512:640], lines, 1), rate, jnp.zeros((32, 128), F32)],
            axis=0,
        )
        put(p, 7, jnp.transpose(one)[:lines])
        put(p, 8, jnp.transpose(two)[:lines])


def screen_kernel(got_ref, table_ref, out_ref):
    slots, sub, outages = out_ref.shape
    passes = lax.axis_size("bus_z")
    lines = got_ref.shape[0] // (passes * TILES)
    place = lax.axis_index("bus_x") * passes + lax.axis_index("bus_z")
    pieces = []
    for t in range(TILES):
        block = got_ref[pl.ds(t, lines, stride=passes * TILES), :]
        for p in range(1, passes):
            block = block + got_ref[pl.ds(p * TILES + t, lines, stride=passes * TILES), :]
        high = block.astype(BF16).astype(F32)
        low = (block - high).astype(BF16).astype(F32)
        pieces.append(jnp.transpose(jnp.concatenate([high, low], axis=0)).astype(BF16))
    shared = jnp.concatenate(pieces[:4] + pieces[7:], axis=0)
    own = jnp.concatenate(pieces[4:7] + pieces[8:], axis=0)
    table = jnp.concatenate([table_ref[...], table_ref[...]], axis=1)
    named = table[:slots]
    line_row = iota((lines, 128), 0)
    lane = iota((1, 128), 1)
    outage = lane % outages
    names = jnp.zeros((lines, 128), F32)
    for s in range(slots):
        names = jnp.where(named[s : s + 1] == line_row, 1.0, names)
    earlier = iota((128, 128), 0) < iota((128, 128), 1) % outages
    rank = lax.dot_general(
        names.astype(BF16),
        jnp.where(earlier, 1.0, 0.0).astype(BF16),
        (((1,), (0,)), ((), ())),
        preferred_element_type=F32,
    )

    def hot_of(target):
        hot = jnp.where(line_row == target, 1.0, 0.0)
        turn = jnp.sum(hot * rank, axis=0, keepdims=True)
        hot = hot.astype(BF16)
        return jnp.concatenate([hot, hot], axis=0), turn

    plain = (((1,), (0,)), ((), ()))
    hot_own, turn_own = hot_of(named[0:1])
    got_own = lax.dot_general(own, hot_own, plain, preferred_element_type=F32)
    lost = jnp.zeros((HOURS, 128), F32)
    self_sens = jnp.zeros((1, 128), F32)
    for c in range(CAP):
        mine = turn_own == float(c)
        lost = jnp.where(mine, got_own[HOURS * c : HOURS * c + HOURS], lost)
        at = 448 + 8 * (c % 2) + c // 2
        self_sens = jnp.where(mine, got_own[at : at + 1], self_sens)
    divisor = jnp.maximum(1.0 - self_sens, floor_value)
    off = table[slots + 2 : slots + 3]
    live = table[slots + 3 : slots + 4]
    lost_scaled = lost
    row = iota((sub, 128), 0)
    for t in range(slots // 2):
        target = jnp.where(lane < outages, named[2 * t : 2 * t + 1], named[2 * t + 1 : 2 * t + 2])
        hot, turn = hot_of(target)
        got = lax.dot_general(shared, hot, plain, preferred_element_type=F32)
        sens = jnp.zeros((sub, 128), F32)
        for c in range(CAP):
            sens = jnp.where(turn == float(c), got[512 + sub * c : 512 + sub * c + sub], sens)
        factor = sens / divisor
        worst = jnp.zeros((sub, 128), F32)
        for h in range(HOURS):
            worst = jnp.maximum(worst, jnp.abs(got[sub * h : sub * h + sub] + factor * lost_scaled[h : h + 1]))
        result = worst / got[720:736]
        slot = 2 * t + jnp.where(lane < outages, 0, 1)
        keep = slot < live
        if t == 0:
            keep = keep & ~((slot == 0) & (row == off - place * sub))
        result = jnp.where(keep, result, 0.0)
        out_ref[2 * t] = result[:, :outages]
        out_ref[2 * t + 1] = result[:, outages:]


def call(kernel, out_shape, in_specs, scratch=(), flops=0, moved=0, limit=16):
    return pl.pallas_call(
        kernel,
        out_shape=out_shape,
        in_specs=in_specs,
        out_specs=IN_VMEM,
        scratch_shapes=list(scratch),
        compiler_params=pltpu.CompilerParams(vmem_limit_bytes=limit * 1024 * 1024),
        cost_estimate=pl.CostEstimate(flops=flops, bytes_accessed=moved, transcendentals=0),
    )


def local(shift_factors, injection, rating, monitored, live_count, outage_offset, outage_ends):
    peers = lax.axis_size("bus_x")
    passes = lax.axis_size("bus_z")
    line_count = lax.axis_size("line")
    block_rows, bus_width = shift_factors.shape
    sub_rows = block_rows // (peers * passes)
    outages, slot_count = monitored.shape
    entries = CAP * line_count
    shape = jax.ShapeDtypeStruct
    rate_row = rating.reshape(1, block_rows)
    table = jnp.concatenate(
        [monitored.T, outage_ends.T, outage_offset.reshape(1, outages), live_count.reshape(1, outages)], axis=0
    )
    with jax.named_scope("requests"):
        requests = call(request_kernel, shape((line_count, 128), F32), [IN_VMEM], flops=10**10, moved=10**7)(
            table
        )
        asked = lax.all_to_all(requests, "line", split_axis=0, concat_axis=0, tiled=True)
    with jax.named_scope("picks"):
        partial_sens = call(
            pick_kernel,
            shape((peers, passes * sub_rows + 8, entries), F32),
            [IN_VMEM] * 3,
            scratch=(
                pltpu.VMEM((2 * block_rows, bus_width), BF16),
                pltpu.VMEM((128, 128), F32),
                pltpu.VMEM((PACKED, entries), BF16),
                pltpu.VMEM((PACKED, 128), jnp.int16),
                pltpu.VMEM((PACKED, 128), jnp.int16),
                pltpu.VMEM((PACKED, 2 * block_rows), F32),
                pltpu.VMEM((2 * HOURS, 2 * block_rows), F32),
                pltpu.VMEM((block_rows, entries), F32),
            ),
            flops=4 * entries * block_rows * bus_width,
            moved=4 * block_rows * bus_width,
            limit=24,
        )(asked, shift_factors, injection)
        half_sens = lax.all_to_all(partial_sens, "bus_x", split_axis=0, concat_axis=0, tiled=True)
    with jax.named_scope("reply"):
        reply = call(
            reply_kernel,
            shape((passes * line_count * TILES, 128), F32),
            [IN_VMEM] * 3,
            scratch=(pltpu.VMEM((block_rows, block_rows), F32),),
        )(half_sens, asked, rate_row)
        reply = reply.reshape(passes * line_count, TILES * 128)
        got = lax.all_to_all(reply, ("line", "bus_z"), split_axis=0, concat_axis=0, tiled=True)
    with jax.named_scope("screen"):
        loading = call(screen_kernel, shape((slot_count, sub_rows, outages), F32), [IN_VMEM] * 2)(
            got.reshape(-1, 128), table
        )
    return jnp.transpose(loading, (2, 0, 1))


def solution(mesh):
    lines, buses = mesh.devices.shape
    bus = ("bus_x", "bus_z")
    return jax.shard_map(
        local,
        mesh=jax.sharding.Mesh(mesh.devices.reshape(lines, buses // PASS, PASS), ("line",) + bus),
        in_specs=(
            P("line", bus),
            P(None, bus),
            P("line"),
            P("line", None),
            P("line"),
            P("line"),
            P("line", None),
        ),
        out_specs=P("line", None, bus),
        check_vma=False,
    )
```

```python
import jax
import jax.numpy as jnp
from jax import lax
from jax.experimental import pallas as pl
from jax.experimental.pallas import tpu as pltpu
from jax.sharding import PartitionSpec as P

floor_value = 0.25
F32 = jnp.float32
BF16 = jnp.bfloat16
NT = (((1,), (1,)), ((), ()))
NN = (((1,), (0,)), ((), ()))
HOURS = 32
CAP = 12
CHUNK = 2304
PASS = 2
TILES = 9
PACKED = 160
IN_VMEM = pl.BlockSpec(memory_space=pltpu.VMEM)


def iota(shape, axis):
    return lax.broadcasted_iota(jnp.int32, shape, axis)


def split2(value):
    high = value.astype(BF16)
    return high, (value - high.astype(F32)).astype(BF16)


def request_kernel(table_ref, out_ref):
    outages = table_ref.shape[1]
    slots = table_ref.shape[0] - 4
    lines = out_ref.shape[0]
    table = table_ref[...]
    table = jnp.concatenate([table, table], axis=1)
    named = table[:slots]
    line_row = iota((lines, 128), 0)
    live = table[slots + 3 : slots + 4]
    names = jnp.zeros((lines, 128), F32)
    asks = jnp.zeros((lines, 128), F32)
    for s in range(slots):
        same = named[s : s + 1] == line_row
        names = jnp.where(same, 1.0, names)
        asks = jnp.where(same & (s < live), 1.0, asks)
    earlier = iota((128, 128), 0) < iota((128, 128), 1) % outages
    rank = lax.dot_general(
        names.astype(BF16), jnp.where(earlier, 1.0, 0.0).astype(BF16), NN, preferred_element_type=F32
    )
    rank = jnp.where(asks > 0.0, rank, -1.0)
    start = table[slots : slots + 1] + 1
    end = table[slots + 1 : slots + 2] + 1
    place = table[slots + 2 : slots + 3] + 1
    second = iota((1, 128), 1) // outages
    spot = iota((128, 128), 0)
    chosen, high, low = [], [], []
    for t in range(CAP // 2):
        turn = 2 * t + second
        chosen.append(jnp.where(rank == turn.astype(F32), 1.0, 0.0).astype(BF16))
        value = jnp.where(
            spot == turn, start, jnp.where(spot == 16 + turn, end, jnp.where(spot == 32 + turn, place, 0))
        )
        high.append((value >> 8).astype(F32).astype(BF16))
        low.append((value & 255).astype(F32).astype(BF16))
    chosen = jnp.concatenate(chosen, axis=1)
    high = lax.dot_general(chosen, jnp.concatenate(high, axis=1), NT, preferred_element_type=F32)
    low = lax.dot_general(chosen, jnp.concatenate(low, axis=1), NT, preferred_element_type=F32)
    out_ref[...] = 256.0 * high + low


def pick_kernel(
    req_ref,
    s_ref,
    inj_ref,
    out_ref,
    turn_ref,
    perm_ref,
    from_ref,
    to_ref,
    sum_ref,
    total_ref,
):
    lines = req_ref.shape[0]
    rows, width = s_ref.shape
    peers, _, entries = out_ref.shape
    packed = from_ref.shape[0]
    deep = rows // peers
    whole, rest = width // CHUNK, width % CHUNK

    bus = lax.axis_index("bus_x") * lax.axis_size("bus_z") + lax.axis_index("bus_z")
    base = (bus * width + 1).astype(F32)
    req = req_ref[...]
    lane = iota((lines, 128), 1)
    first = req - base
    second = pltpu.roll(req, 112, 1) - base
    has_first = (first >= 0.0) & (first < float(width))
    has_second = (second >= 0.0) & (second < float(width))
    used = (has_first | has_second) & (first != second) & (lane < CAP)
    mask = jnp.where(used, 1.0, 0.0)
    hits = mask.astype(BF16)
    above = jnp.where(iota((lines, lines), 1) < iota((lines, lines), 0), 1.0, 0.0).astype(BF16)
    ahead = jnp.where(iota((128, 128), 0) < iota((128, 128), 1), 1.0, 0.0).astype(BF16)
    ones = jnp.ones((lines, lines), BF16)
    in_lane = lax.dot_general(ones, hits, NN, preferred_element_type=F32)
    rank = lax.dot_general(above, hits, NN, preferred_element_type=F32) + lax.dot_general(
        in_lane.astype(BF16), ahead, NN, preferred_element_type=F32
    )
    rank = jnp.where(used, rank, -1.0)
    count = jnp.sum(mask).astype(jnp.int32)
    blocks = (count + (packed - 1)) // packed
    first = jnp.where(has_first & used, first + 1.0, 0.0)
    second = jnp.where(has_second & used, second + 1.0, 0.0)
    first_high = jnp.floor(first * (1.0 / 128.0))
    second_high = jnp.floor(second * (1.0 / 128.0))
    fields = (first_high, first - 128.0 * first_high, second_high, second - 128.0 * second_high, rank)
    mixed = pltpu.roll(req, 48, 1)
    for q in reversed(range(5)):
        field = pltpu.roll(fields[q], 16 * q, 1) if q else fields[q]
        mixed = jnp.where(lane < 16 * (q + 1), field, mixed) if q < 4 else jnp.where(lane < 80, field, mixed)
    turn_ref[...] = jnp.transpose(jnp.concatenate([mixed, jnp.zeros((128 - lines, 128), F32)], axis=0))
    pairs = []
    lane_row = iota((8, 128), 1)
    for t in range(CAP // 2):
        even = turn_ref[pl.ds(2 * t, 8, stride=16), :]
        odd = turn_ref[pl.ds(2 * t + 1, 8, stride=16), :]
        pairs.append(jnp.where(lane_row < lines, even, pltpu.roll(odd, lines, 1)))
    table = jnp.concatenate(pairs, axis=1)
    ranks = table[4:5].astype(jnp.int32)
    offs = table[5:6].astype(jnp.int32) - 1
    table_low = table.astype(BF16)
    one, minus, zero = jnp.asarray(1, BF16), jnp.asarray(-1, BF16), jnp.asarray(0, BF16)
    total_ref[...] = jnp.zeros_like(total_ref)

    def open_block(block):
        perm = jnp.where(iota((packed, entries), 0) + block * packed == ranks, 1.0, 0.0).astype(BF16)
        perm_ref[...] = perm
        ends = lax.dot_general(perm, table_low, NT, preferred_element_type=F32)
        start = (128.0 * ends[:, 0:1] + ends[:, 1:2] - 1.0).astype(jnp.int32)
        end = (128.0 * ends[:, 2:3] + ends[:, 3:4] - 1.0).astype(jnp.int32)
        from_ref[...] = jnp.broadcast_to(start, (packed, 128)).astype(jnp.int16)
        to_ref[...] = jnp.broadcast_to(end, (packed, 128)).astype(jnp.int16)
        sum_ref[...] = jnp.zeros_like(sum_ref)

    def hot(at, size):
        columns = []
        for t in range(size // 128):
            spot = (iota((16, 128), 1) + (at + t * 128)).astype(jnp.int16)
            spot = jnp.broadcast_to(spot[None], (packed // 16, 16, 128)).reshape(packed, 128)
            columns.append(
                jnp.where(from_ref[...] == spot, one, jnp.where(to_ref[...] == spot, minus, zero))
            )
        return jnp.concatenate(columns, axis=1)

    def multiply(left, at, size):
        both = jnp.concatenate(split2(s_ref[:, pl.ds(at, size)]), axis=0)
        return lax.dot_general(left, both, NT, preferred_element_type=F32)

    def close_block():
        turned = jnp.transpose(sum_ref[:packed, :rows] + sum_ref[:packed, rows:])
        both = lax.dot_general(
            jnp.concatenate(split2(turned), axis=0), perm_ref[...], NN, preferred_element_type=F32
        )
        total_ref[...] += both[:rows] + both[rows:]

    def step(at, size):
        left = jnp.concatenate((hot(at, size),) + split2(inj_ref[:, pl.ds(at, size)]), axis=0)
        sum_ref[...] += multiply(left, at, size)

    def pick(at, size):
        sum_ref[:packed] += multiply(hot(at, size), at, size)

    open_block(0)
    step(whole * CHUNK, rest)

    def first_block(q, carry):
        at = pl.multiple_of(q * CHUNK, CHUNK)
        step(at, CHUNK)
        return carry

    lax.fori_loop(0, whole, first_block, 0)
    flows = sum_ref[packed:]
    part = (
        flows[:HOURS, :rows] + (flows[:HOURS, rows:] + flows[HOURS:, :rows]) + flows[HOURS:, rows:]
    )
    close_block()

    def other_block(block, carry):
        open_block(block)
        pick(whole * CHUNK, rest)

        def piece(q, carry):
            pick(pl.multiple_of(q * CHUNK, CHUNK), CHUNK)
            return carry

        lax.fori_loop(0, whole, piece, 0)
        close_block()
        return carry

    lax.fori_loop(1, blocks, other_block, 0)
    total = total_ref[...]
    own = jnp.sum(jnp.where(iota((rows, entries), 0) == offs, total, 0.0), axis=0, keepdims=True)
    own = [own[:, 128 * t : 128 * t + 128] for t in range(CAP // 2)] + [jnp.zeros((2, 128), F32)]
    extra = jnp.concatenate(
        [part[8 * t : 8 * t + 8] for t in range(4)] + [jnp.concatenate(own, axis=0), jnp.zeros((8, 128), F32)],
        axis=1,
    )
    for b in range(peers):
        out_ref[b, :deep, :] = total[b * deep : (b + 1) * deep]
        out_ref[b, deep:, :] = extra


def reply_kernel(got_ref, req_ref, rate_ref, out_ref, rate_scratch):
    peers = got_ref.shape[0]
    lines = req_ref.shape[0]
    rows = rate_ref.shape[1]
    passes = out_ref.shape[0] // (lines * TILES)
    sub = (got_ref.shape[1] - 8) // passes
    place = lax.axis_index("bus_x") * passes
    total = got_ref[0]
    for b in range(1, peers):
        total = total + got_ref[b]
    sens, rest = total[: passes * sub], total[passes * sub :]
    flows = jnp.concatenate([rest[:, 128 * t : 128 * t + 128] for t in range(4)], axis=0)
    lane = iota((HOURS, 128), 1)
    hour = iota((HOURS, 128), 0)
    f_high, f_low = split2(flows)
    f_rest = (flows - f_high.astype(F32) - f_low.astype(F32)).astype(BF16)
    f_all = jnp.concatenate([f_high, f_low, f_rest], axis=0)
    req = req_ref[...]
    lane_line = iota((lines, 128), 1)
    hots = [
        jnp.where(lane_line == req[:, 32 + c : 33 + c].astype(jnp.int32) - 1, 1.0, 0.0).astype(BF16)
        for c in range(CAP)
    ]
    left = jnp.concatenate([jnp.concatenate(hots[4 * q : 4 * q + 4], axis=1) for q in range(3)], axis=0)

    def diagonal(block):
        blank = jnp.zeros_like(block)
        return jnp.concatenate(
            [jnp.concatenate([block if v == u else blank for v in range(4)], axis=1) for u in range(4)], axis=0
        )

    lost = lax.dot_general(
        left, diagonal(f_high), NT, preferred_element_type=F32
    ) + lax.dot_general(left, diagonal(f_low), NT, preferred_element_type=F32)
    rate_scratch[...] = 0.5 * jnp.transpose(jnp.broadcast_to(rate_ref[...], (rows, 128)))

    def wide(block):
        return jnp.concatenate([block, jnp.zeros((block.shape[0], 128 - lines), F32)], axis=1)

    def put(p, q, block):
        out_ref[pl.ds(p * TILES + q, lines, stride=passes * TILES), :] = block

    for p in range(passes):
        wanted = iota((128, 128), 0) == (place + p) * sub + iota((128, 128), 1) % sub
        spread = lax.dot_general(f_all, jnp.where(wanted, 1.0, 0.0).astype(BF16), NN, preferred_element_type=F32)
        spread = spread[:HOURS] + spread[HOURS : 2 * HOURS] + spread[2 * HOURS :]
        spread = jnp.where(lane // sub == hour % 8, spread, 0.0)
        for t in range(4):
            row = jnp.sum(spread[8 * t : 8 * t + 8], axis=0, keepdims=True)
            put(p, t, jnp.broadcast_to(row, (lines, 128)))
        for q in range(3):
            put(p, 4 + q, lost[q * lines : (q + 1) * lines])
        rate = rate_scratch[pl.ds(pl.multiple_of((place + p) * sub, sub), sub), :]
        part = sens[p * sub : (p + 1) * sub]
        blocks = [wide(part[:, c * lines : (c + 1) * lines]) for c in range(CAP)]
        one = jnp.concatenate(blocks[:8], axis=0)
        two = jnp.concatenate(
            blocks[8:]
            + [rest[:, 512:640], pltpu.roll(rest[:, 512:640], lines, 1), rate, jnp.zeros((32, 128), F32)],
            axis=0,
        )
        put(p, 7, jnp.transpose(one)[:lines])
        put(p, 8, jnp.transpose(two)[:lines])


def screen_kernel(got_ref, table_ref, out_ref):
    slots, sub, outages = out_ref.shape
    passes = lax.axis_size("bus_z")
    lines = got_ref.shape[0] // (passes * TILES)
    place = lax.axis_index("bus_x") * passes + lax.axis_index("bus_z")
    pieces = []
    for t in range(TILES):
        block = got_ref[pl.ds(t, lines, stride=passes * TILES), :]
        for p in range(1, passes):
            block = block + got_ref[pl.ds(p * TILES + t, lines, stride=passes * TILES), :]
        high = block.astype(BF16).astype(F32)
        low = (block - high).astype(BF16).astype(F32)
        pieces.append(jnp.transpose(jnp.concatenate([high, low], axis=0)).astype(BF16))
    shared = jnp.concatenate(pieces[:4] + pieces[7:], axis=0)
    own = jnp.concatenate(pieces[4:7] + pieces[8:], axis=0)
    table = jnp.concatenate([table_ref[...], table_ref[...]], axis=1)
    named = table[:slots]
    line_row = iota((lines, 128), 0)
    lane = iota((1, 128), 1)
    outage = lane % outages
    names = jnp.zeros((lines, 128), F32)
    for s in range(slots):
        names = jnp.where(named[s : s + 1] == line_row, 1.0, names)
    earlier = iota((128, 128), 0) < iota((128, 128), 1) % outages
    rank = lax.dot_general(
        names.astype(BF16),
        jnp.where(earlier, 1.0, 0.0).astype(BF16),
        (((1,), (0,)), ((), ())),
        preferred_element_type=F32,
    )

    def hot_of(target):
        hot = jnp.where(line_row == target, 1.0, 0.0)
        turn = jnp.sum(hot * rank, axis=0, keepdims=True)
        hot = hot.astype(BF16)
        return jnp.concatenate([hot, hot], axis=0), turn

    plain = (((1,), (0,)), ((), ()))
    hot_own, turn_own = hot_of(named[0:1])
    got_own = lax.dot_general(own, hot_own, plain, preferred_element_type=F32)
    lost = jnp.zeros((HOURS, 128), F32)
    self_sens = jnp.zeros((1, 128), F32)
    for c in range(CAP):
        mine = turn_own == float(c)
        lost = jnp.where(mine, got_own[HOURS * c : HOURS * c + HOURS], lost)
        at = 448 + 8 * (c % 2) + c // 2
        self_sens = jnp.where(mine, got_own[at : at + 1], self_sens)
    divisor = jnp.maximum(1.0 - self_sens, floor_value)
    off = table[slots + 2 : slots + 3]
    live = table[slots + 3 : slots + 4]
    lost_scaled = lost
    row = iota((sub, 128), 0)
    for t in range(slots // 2):
        target = jnp.where(lane < outages, named[2 * t : 2 * t + 1], named[2 * t + 1 : 2 * t + 2])
        hot, turn = hot_of(target)
        got = lax.dot_general(shared, hot, plain, preferred_element_type=F32)
        sens = jnp.zeros((sub, 128), F32)
        for c in range(CAP):
            sens = jnp.where(turn == float(c), got[512 + sub * c : 512 + sub * c + sub], sens)
        factor = sens / divisor
        worst = jnp.zeros((sub, 128), F32)
        for h in range(HOURS):
            worst = jnp.maximum(worst, jnp.abs(got[sub * h : sub * h + sub] + factor * lost_scaled[h : h + 1]))
        result = worst / got[720:736]
        slot = 2 * t + jnp.where(lane < outages, 0, 1)
        keep = slot < live
        if t == 0:
            keep = keep & ~((slot == 0) & (row == off - place * sub))
        result = jnp.where(keep, result, 0.0)
        out_ref[2 * t] = result[:, :outages]
        out_ref[2 * t + 1] = result[:, outages:]


def call(kernel, out_shape, in_specs, scratch=(), flops=0, moved=0, limit=16):
    return pl.pallas_call(
        kernel,
        out_shape=out_shape,
        in_specs=in_specs,
        out_specs=IN_VMEM,
        scratch_shapes=list(scratch),
        compiler_params=pltpu.CompilerParams(vmem_limit_bytes=limit * 1024 * 1024),
        cost_estimate=pl.CostEstimate(flops=flops, bytes_accessed=moved, transcendentals=0),
    )


def local(shift_factors, injection, rating, monitored, live_count, outage_offset, outage_ends):
    peers = lax.axis_size("bus_x")
    passes = lax.axis_size("bus_z")
    line_count = lax.axis_size("line")
    block_rows, bus_width = shift_factors.shape
    sub_rows = block_rows // (peers * passes)
    outages, slot_count = monitored.shape
    entries = CAP * line_count
    shape = jax.ShapeDtypeStruct
    rate_row = rating.reshape(1, block_rows)
    table = jnp.concatenate(
        [monitored.T, outage_ends.T, outage_offset.reshape(1, outages), live_count.reshape(1, outages)], axis=0
    )
    with jax.named_scope("requests"):
        requests = call(request_kernel, shape((line_count, 128), F32), [IN_VMEM], flops=10**10, moved=10**7)(
            table
        )
        asked = lax.all_to_all(requests, "line", split_axis=0, concat_axis=0, tiled=True)
    with jax.named_scope("picks"):
        partial_sens = call(
            pick_kernel,
            shape((peers, passes * sub_rows + 8, entries), F32),
            [IN_VMEM] * 3,
            scratch=(
                pltpu.VMEM((128, 128), F32),
                pltpu.VMEM((PACKED, entries), BF16),
                pltpu.VMEM((PACKED, 128), jnp.int16),
                pltpu.VMEM((PACKED, 128), jnp.int16),
                pltpu.VMEM((PACKED + 2 * HOURS, 2 * block_rows), F32),
                pltpu.VMEM((block_rows, entries), F32),
            ),
            flops=4 * entries * block_rows * bus_width,
            moved=4 * block_rows * bus_width,
            limit=24,
        )(asked, shift_factors, injection)
        half_sens = lax.all_to_all(partial_sens, "bus_x", split_axis=0, concat_axis=0, tiled=True)
    with jax.named_scope("reply"):
        reply = call(
            reply_kernel,
            shape((passes * line_count * TILES, 128), F32),
            [IN_VMEM] * 3,
            scratch=(pltpu.VMEM((block_rows, block_rows), F32),),
        )(half_sens, asked, rate_row)
        reply = reply.reshape(passes * line_count, TILES * 128)
        got = lax.all_to_all(reply, ("line", "bus_z"), split_axis=0, concat_axis=0, tiled=True)
    with jax.named_scope("screen"):
        loading = call(screen_kernel, shape((slot_count, sub_rows, outages), F32), [IN_VMEM] * 2)(
            got.reshape(-1, 128), table
        )
    return jnp.transpose(loading, (2, 0, 1))


def solution(mesh):
    lines, buses = mesh.devices.shape
    bus = ("bus_x", "bus_z")
    return jax.shard_map(
        local,
        mesh=jax.sharding.Mesh(mesh.devices.reshape(lines, buses // PASS, PASS), ("line",) + bus),
        in_specs=(
            P("line", bus),
            P(None, bus),
            P("line"),
            P("line", None),
            P("line"),
            P("line"),
            P("line", None),
        ),
        out_specs=P("line", None, bus),
        check_vma=False,
    )
```

```python
import jax
import jax.numpy as jnp
from jax import lax
from jax.experimental import pallas as pl
from jax.experimental.pallas import tpu as pltpu
from jax.sharding import PartitionSpec as P

floor_value = 0.25
F32 = jnp.float32
BF16 = jnp.bfloat16
NT = (((1,), (1,)), ((), ()))
NN = (((1,), (0,)), ((), ()))
HOURS = 32
CAP = 12
CHUNK = 3072
PASS = 2
TILES = 9
PACKED = 160
IN_VMEM = pl.BlockSpec(memory_space=pltpu.VMEM)


def iota(shape, axis):
    return lax.broadcasted_iota(jnp.int32, shape, axis)


def split2(value):
    high = value.astype(BF16)
    return high, (value - high.astype(F32)).astype(BF16)


def request_kernel(table_ref, out_ref):
    outages = table_ref.shape[1]
    slots = table_ref.shape[0] - 4
    lines = out_ref.shape[0]
    table = table_ref[...]
    table = jnp.concatenate([table, table], axis=1)
    named = table[:slots]
    line_row = iota((lines, 128), 0)
    live = table[slots + 3 : slots + 4]
    names = jnp.zeros((lines, 128), F32)
    asks = jnp.zeros((lines, 128), F32)
    for s in range(slots):
        same = named[s : s + 1] == line_row
        names = jnp.where(same, 1.0, names)
        asks = jnp.where(same & (s < live), 1.0, asks)
    earlier = iota((128, 128), 0) < iota((128, 128), 1) % outages
    rank = lax.dot_general(
        names.astype(BF16), jnp.where(earlier, 1.0, 0.0).astype(BF16), NN, preferred_element_type=F32
    )
    rank = jnp.where(asks > 0.0, rank, -1.0)
    start = table[slots : slots + 1] + 1
    end = table[slots + 1 : slots + 2] + 1
    place = table[slots + 2 : slots + 3] + 1
    second = iota((1, 128), 1) // outages
    spot = iota((128, 128), 0)
    chosen, high, low = [], [], []
    for t in range(CAP // 2):
        turn = 2 * t + second
        chosen.append(jnp.where(rank == turn.astype(F32), 1.0, 0.0).astype(BF16))
        value = jnp.where(
            spot == turn, start, jnp.where(spot == 16 + turn, end, jnp.where(spot == 32 + turn, place, 0))
        )
        high.append((value >> 8).astype(F32).astype(BF16))
        low.append((value & 255).astype(F32).astype(BF16))
    chosen = jnp.concatenate(chosen, axis=1)
    high = lax.dot_general(chosen, jnp.concatenate(high, axis=1), NT, preferred_element_type=F32)
    low = lax.dot_general(chosen, jnp.concatenate(low, axis=1), NT, preferred_element_type=F32)
    out_ref[...] = 256.0 * high + low


def pick_kernel(
    req_ref,
    s_ref,
    inj_ref,
    out_ref,
    turn_ref,
    perm_ref,
    from_ref,
    to_ref,
    sum_ref,
    total_ref,
):
    lines = req_ref.shape[0]
    rows, width = s_ref.shape
    peers, _, entries = out_ref.shape
    packed = from_ref.shape[0]
    deep = rows // peers
    whole, rest = width // CHUNK, width % CHUNK

    bus = lax.axis_index("bus_x") * lax.axis_size("bus_z") + lax.axis_index("bus_z")
    base = (bus * width + 1).astype(F32)
    req = req_ref[...]
    lane = iota((lines, 128), 1)
    first = req - base
    second = pltpu.roll(req, 112, 1) - base
    has_first = (first >= 0.0) & (first < float(width))
    has_second = (second >= 0.0) & (second < float(width))
    used = (has_first | has_second) & (first != second) & (lane < CAP)
    mask = jnp.where(used, 1.0, 0.0)
    hits = mask.astype(BF16)
    above = jnp.where(iota((lines, lines), 1) < iota((lines, lines), 0), 1.0, 0.0).astype(BF16)
    ahead = jnp.where(iota((128, 128), 0) < iota((128, 128), 1), 1.0, 0.0).astype(BF16)
    ones = jnp.ones((lines, lines), BF16)
    in_lane = lax.dot_general(ones, hits, NN, preferred_element_type=F32)
    rank = lax.dot_general(above, hits, NN, preferred_element_type=F32) + lax.dot_general(
        in_lane.astype(BF16), ahead, NN, preferred_element_type=F32
    )
    rank = jnp.where(used, rank, -1.0)
    count = jnp.sum(mask).astype(jnp.int32)
    blocks = (count + (packed - 1)) // packed
    first = jnp.where(has_first & used, first + 1.0, 0.0)
    second = jnp.where(has_second & used, second + 1.0, 0.0)
    first_high = jnp.floor(first * (1.0 / 128.0))
    second_high = jnp.floor(second * (1.0 / 128.0))
    fields = (first_high, first - 128.0 * first_high, second_high, second - 128.0 * second_high, rank)
    mixed = pltpu.roll(req, 48, 1)
    for q in reversed(range(5)):
        field = pltpu.roll(fields[q], 16 * q, 1) if q else fields[q]
        mixed = jnp.where(lane < 16 * (q + 1), field, mixed) if q < 4 else jnp.where(lane < 80, field, mixed)
    turn_ref[...] = jnp.transpose(jnp.concatenate([mixed, jnp.zeros((128 - lines, 128), F32)], axis=0))
    pairs = []
    lane_row = iota((8, 128), 1)
    for t in range(CAP // 2):
        even = turn_ref[pl.ds(2 * t, 8, stride=16), :]
        odd = turn_ref[pl.ds(2 * t + 1, 8, stride=16), :]
        pairs.append(jnp.where(lane_row < lines, even, pltpu.roll(odd, lines, 1)))
    table = jnp.concatenate(pairs, axis=1)
    ranks = table[4:5].astype(jnp.int32)
    offs = table[5:6].astype(jnp.int32) - 1
    table_low = table.astype(BF16)
    one, minus, zero = jnp.asarray(1, BF16), jnp.asarray(-1, BF16), jnp.asarray(0, BF16)
    total_ref[...] = jnp.zeros_like(total_ref)

    def open_block(block):
        perm = jnp.where(iota((packed, entries), 0) + block * packed == ranks, 1.0, 0.0).astype(BF16)
        perm_ref[...] = perm
        ends = lax.dot_general(perm, table_low, NT, preferred_element_type=F32)
        start = (128.0 * ends[:, 0:1] + ends[:, 1:2] - 1.0).astype(jnp.int32)
        end = (128.0 * ends[:, 2:3] + ends[:, 3:4] - 1.0).astype(jnp.int32)
        from_ref[...] = jnp.broadcast_to(start, (packed, 128)).astype(jnp.int16)
        to_ref[...] = jnp.broadcast_to(end, (packed, 128)).astype(jnp.int16)
        sum_ref[...] = jnp.zeros_like(sum_ref)

    def hot(at, size):
        columns = []
        for t in range(size // 128):
            spot = (iota((16, 128), 1) + (at + t * 128)).astype(jnp.int16)
            spot = jnp.broadcast_to(spot[None], (packed // 16, 16, 128)).reshape(packed, 128)
            columns.append(
                jnp.where(from_ref[...] == spot, one, jnp.where(to_ref[...] == spot, minus, zero))
            )
        return jnp.concatenate(columns, axis=1)

    def multiply(left, at, size):
        both = jnp.concatenate(split2(s_ref[:, pl.ds(at, size)]), axis=0)
        return lax.dot_general(left, both, NT, preferred_element_type=F32)

    def close_block():
        turned = jnp.transpose(sum_ref[:packed, :rows] + sum_ref[:packed, rows:])
        both = lax.dot_general(
            jnp.concatenate(split2(turned), axis=0), perm_ref[...], NN, preferred_element_type=F32
        )
        total_ref[...] += both[:rows] + both[rows:]

    def step(at, size):
        left = jnp.concatenate((hot(at, size),) + split2(inj_ref[:, pl.ds(at, size)]), axis=0)
        sum_ref[...] += multiply(left, at, size)

    def pick(at, size):
        sum_ref[:packed] += multiply(hot(at, size), at, size)

    open_block(0)
    step(whole * CHUNK, rest)

    def first_block(q, carry):
        at = pl.multiple_of(q * CHUNK, CHUNK)
        step(at, CHUNK)
        return carry

    lax.fori_loop(0, whole, first_block, 0)
    flows = sum_ref[packed:]
    part = (
        flows[:HOURS, :rows] + (flows[:HOURS, rows:] + flows[HOURS:, :rows]) + flows[HOURS:, rows:]
    )
    close_block()

    def other_block(block, carry):
        open_block(block)
        pick(whole * CHUNK, rest)

        def piece(q, carry):
            pick(pl.multiple_of(q * CHUNK, CHUNK), CHUNK)
            return carry

        lax.fori_loop(0, whole, piece, 0)
        close_block()
        return carry

    lax.fori_loop(1, blocks, other_block, 0)
    total = total_ref[...]
    own = jnp.sum(jnp.where(iota((rows, entries), 0) == offs, total, 0.0), axis=0, keepdims=True)
    own = [own[:, 128 * t : 128 * t + 128] for t in range(CAP // 2)] + [jnp.zeros((2, 128), F32)]
    extra = jnp.concatenate(
        [part[8 * t : 8 * t + 8] for t in range(4)] + [jnp.concatenate(own, axis=0), jnp.zeros((8, 128), F32)],
        axis=1,
    )
    for b in range(peers):
        out_ref[b, :deep, :] = total[b * deep : (b + 1) * deep]
        out_ref[b, deep:, :] = extra


def reply_kernel(got_ref, req_ref, rate_ref, out_ref, rate_scratch):
    peers = got_ref.shape[0]
    lines = req_ref.shape[0]
    rows = rate_ref.shape[1]
    passes = out_ref.shape[0] // (lines * TILES)
    sub = (got_ref.shape[1] - 8) // passes
    place = lax.axis_index("bus_x") * passes
    total = got_ref[0]
    for b in range(1, peers):
        total = total + got_ref[b]
    sens, rest = total[: passes * sub], total[passes * sub :]
    flows = jnp.concatenate([rest[:, 128 * t : 128 * t + 128] for t in range(4)], axis=0)
    lane = iota((HOURS, 128), 1)
    hour = iota((HOURS, 128), 0)
    f_high, f_low = split2(flows)
    f_rest = (flows - f_high.astype(F32) - f_low.astype(F32)).astype(BF16)
    f_all = jnp.concatenate([f_high, f_low, f_rest], axis=0)
    req = req_ref[...]
    lane_line = iota((lines, 128), 1)
    hots = [
        jnp.where(lane_line == req[:, 32 + c : 33 + c].astype(jnp.int32) - 1, 1.0, 0.0).astype(BF16)
        for c in range(CAP)
    ]
    left = jnp.concatenate([jnp.concatenate(hots[4 * q : 4 * q + 4], axis=1) for q in range(3)], axis=0)

    def diagonal(block):
        blank = jnp.zeros_like(block)
        return jnp.concatenate(
            [jnp.concatenate([block if v == u else blank for v in range(4)], axis=1) for u in range(4)], axis=0
        )

    lost = lax.dot_general(
        left, diagonal(f_high), NT, preferred_element_type=F32
    ) + lax.dot_general(left, diagonal(f_low), NT, preferred_element_type=F32)
    rate_scratch[...] = 0.5 * jnp.transpose(jnp.broadcast_to(rate_ref[...], (rows, 128)))

    def wide(block):
        return jnp.concatenate([block, jnp.zeros((block.shape[0], 128 - lines), F32)], axis=1)

    def put(p, q, block):
        out_ref[pl.ds(p * TILES + q, lines, stride=passes * TILES), :] = block

    for p in range(passes):
        wanted = iota((128, 128), 0) == (place + p) * sub + iota((128, 128), 1) % sub
        spread = lax.dot_general(f_all, jnp.where(wanted, 1.0, 0.0).astype(BF16), NN, preferred_element_type=F32)
        spread = spread[:HOURS] + spread[HOURS : 2 * HOURS] + spread[2 * HOURS :]
        spread = jnp.where(lane // sub == hour % 8, spread, 0.0)
        for t in range(4):
            row = jnp.sum(spread[8 * t : 8 * t + 8], axis=0, keepdims=True)
            put(p, t, jnp.broadcast_to(row, (lines, 128)))
        for q in range(3):
            put(p, 4 + q, lost[q * lines : (q + 1) * lines])
        rate = rate_scratch[pl.ds(pl.multiple_of((place + p) * sub, sub), sub), :]
        part = sens[p * sub : (p + 1) * sub]
        blocks = [wide(part[:, c * lines : (c + 1) * lines]) for c in range(CAP)]
        one = jnp.concatenate(blocks[:8], axis=0)
        two = jnp.concatenate(
            blocks[8:]
            + [rest[:, 512:640], pltpu.roll(rest[:, 512:640], lines, 1), rate, jnp.zeros((32, 128), F32)],
            axis=0,
        )
        put(p, 7, jnp.transpose(one)[:lines])
        put(p, 8, jnp.transpose(two)[:lines])


def screen_kernel(got_ref, table_ref, out_ref):
    slots, sub, outages = out_ref.shape
    passes = lax.axis_size("bus_z")
    lines = got_ref.shape[0] // (passes * TILES)
    place = lax.axis_index("bus_x") * passes + lax.axis_index("bus_z")
    pieces = []
    for t in range(TILES):
        block = got_ref[pl.ds(t, lines, stride=passes * TILES), :]
        for p in range(1, passes):
            block = block + got_ref[pl.ds(p * TILES + t, lines, stride=passes * TILES), :]
        high = block.astype(BF16).astype(F32)
        low = (block - high).astype(BF16).astype(F32)
        pieces.append(jnp.transpose(jnp.concatenate([high, low], axis=0)).astype(BF16))
    shared = jnp.concatenate(pieces[:4] + pieces[7:], axis=0)
    own = jnp.concatenate(pieces[4:7] + pieces[8:], axis=0)
    table = jnp.concatenate([table_ref[...], table_ref[...]], axis=1)
    named = table[:slots]
    line_row = iota((lines, 128), 0)
    lane = iota((1, 128), 1)
    outage = lane % outages
    names = jnp.zeros((lines, 128), F32)
    for s in range(slots):
        names = jnp.where(named[s : s + 1] == line_row, 1.0, names)
    earlier = iota((128, 128), 0) < iota((128, 128), 1) % outages
    rank = lax.dot_general(
        names.astype(BF16),
        jnp.where(earlier, 1.0, 0.0).astype(BF16),
        (((1,), (0,)), ((), ())),
        preferred_element_type=F32,
    )

    def hot_of(target):
        hot = jnp.where(line_row == target, 1.0, 0.0)
        turn = jnp.sum(hot * rank, axis=0, keepdims=True)
        hot = hot.astype(BF16)
        return jnp.concatenate([hot, hot], axis=0), turn

    plain = (((1,), (0,)), ((), ()))
    hot_own, turn_own = hot_of(named[0:1])
    got_own = lax.dot_general(own, hot_own, plain, preferred_element_type=F32)
    lost = jnp.zeros((HOURS, 128), F32)
    self_sens = jnp.zeros((1, 128), F32)
    for c in range(CAP):
        mine = turn_own == float(c)
        lost = jnp.where(mine, got_own[HOURS * c : HOURS * c + HOURS], lost)
        at = 448 + 8 * (c % 2) + c // 2
        self_sens = jnp.where(mine, got_own[at : at + 1], self_sens)
    divisor = jnp.maximum(1.0 - self_sens, floor_value)
    off = table[slots + 2 : slots + 3]
    live = table[slots + 3 : slots + 4]
    lost_scaled = lost
    row = iota((sub, 128), 0)
    for t in range(slots // 2):
        target = jnp.where(lane < outages, named[2 * t : 2 * t + 1], named[2 * t + 1 : 2 * t + 2])
        hot, turn = hot_of(target)
        got = lax.dot_general(shared, hot, plain, preferred_element_type=F32)
        sens = jnp.zeros((sub, 128), F32)
        for c in range(CAP):
            sens = jnp.where(turn == float(c), got[512 + sub * c : 512 + sub * c + sub], sens)
        factor = sens / divisor
        worst = jnp.zeros((sub, 128), F32)
        for h in range(HOURS):
            worst = jnp.maximum(worst, jnp.abs(got[sub * h : sub * h + sub] + factor * lost_scaled[h : h + 1]))
        result = worst / got[720:736]
        slot = 2 * t + jnp.where(lane < outages, 0, 1)
        keep = slot < live
        if t == 0:
            keep = keep & ~((slot == 0) & (row == off - place * sub))
        result = jnp.where(keep, result, 0.0)
        out_ref[2 * t] = result[:, :outages]
        out_ref[2 * t + 1] = result[:, outages:]


def call(kernel, out_shape, in_specs, scratch=(), flops=0, moved=0, limit=16):
    return pl.pallas_call(
        kernel,
        out_shape=out_shape,
        in_specs=in_specs,
        out_specs=IN_VMEM,
        scratch_shapes=list(scratch),
        compiler_params=pltpu.CompilerParams(vmem_limit_bytes=limit * 1024 * 1024),
        cost_estimate=pl.CostEstimate(flops=flops, bytes_accessed=moved, transcendentals=0),
    )


def local(shift_factors, injection, rating, monitored, live_count, outage_offset, outage_ends):
    peers = lax.axis_size("bus_x")
    passes = lax.axis_size("bus_z")
    line_count = lax.axis_size("line")
    block_rows, bus_width = shift_factors.shape
    sub_rows = block_rows // (peers * passes)
    outages, slot_count = monitored.shape
    entries = CAP * line_count
    shape = jax.ShapeDtypeStruct
    rate_row = rating.reshape(1, block_rows)
    table = jnp.concatenate(
        [monitored.T, outage_ends.T, outage_offset.reshape(1, outages), live_count.reshape(1, outages)], axis=0
    )
    with jax.named_scope("requests"):
        requests = call(request_kernel, shape((line_count, 128), F32), [IN_VMEM], flops=10**10, moved=10**7)(
            table
        )
        asked = lax.all_to_all(requests, "line", split_axis=0, concat_axis=0, tiled=True)
    with jax.named_scope("picks"):
        partial_sens = call(
            pick_kernel,
            shape((peers, passes * sub_rows + 8, entries), F32),
            [IN_VMEM] * 3,
            scratch=(
                pltpu.VMEM((128, 128), F32),
                pltpu.VMEM((PACKED, entries), BF16),
                pltpu.VMEM((PACKED, 128), jnp.int16),
                pltpu.VMEM((PACKED, 128), jnp.int16),
                pltpu.VMEM((PACKED + 2 * HOURS, 2 * block_rows), F32),
                pltpu.VMEM((block_rows, entries), F32),
            ),
            flops=4 * entries * block_rows * bus_width,
            moved=4 * block_rows * bus_width,
            limit=24,
        )(asked, shift_factors, injection)
        half_sens = lax.all_to_all(partial_sens, "bus_x", split_axis=0, concat_axis=0, tiled=True)
    with jax.named_scope("reply"):
        reply = call(
            reply_kernel,
            shape((passes * line_count * TILES, 128), F32),
            [IN_VMEM] * 3,
            scratch=(pltpu.VMEM((block_rows, block_rows), F32),),
        )(half_sens, asked, rate_row)
        reply = reply.reshape(passes * line_count, TILES * 128)
        got = lax.all_to_all(reply, ("line", "bus_z"), split_axis=0, concat_axis=0, tiled=True)
    with jax.named_scope("screen"):
        loading = call(screen_kernel, shape((slot_count, sub_rows, outages), F32), [IN_VMEM] * 2)(
            got.reshape(-1, 128), table
        )
    return jnp.transpose(loading, (2, 0, 1))


def solution(mesh):
    lines, buses = mesh.devices.shape
    bus = ("bus_x", "bus_z")
    return jax.shard_map(
        local,
        mesh=jax.sharding.Mesh(mesh.devices.reshape(lines, buses // PASS, PASS), ("line",) + bus),
        in_specs=(
            P("line", bus),
            P(None, bus),
            P("line"),
            P("line", None),
            P("line"),
            P("line"),
            P("line", None),
        ),
        out_specs=P("line", None, bus),
        check_vma=False,
    )
```

```python
import jax
import jax.numpy as jnp
from jax import lax
from jax.experimental import pallas as pl
from jax.experimental.pallas import tpu as pltpu
from jax.sharding import PartitionSpec as P

floor_value = 0.25
F32 = jnp.float32
BF16 = jnp.bfloat16
NT = (((1,), (1,)), ((), ()))
NN = (((1,), (0,)), ((), ()))
HOURS = 32
CAP = 12
CHUNK = 3072
PASS = 2
TILES = 6
PACKED = 160
IN_VMEM = pl.BlockSpec(memory_space=pltpu.VMEM)
IN_HBM = pl.BlockSpec(memory_space=pltpu.HBM)


def iota(shape, axis):
    return lax.broadcasted_iota(jnp.int32, shape, axis)


def split2(value):
    high = value.astype(BF16)
    return high, (value - high.astype(F32)).astype(BF16)


def request_kernel(table_ref, out_ref):
    outages = table_ref.shape[1]
    slots = table_ref.shape[0] - 4
    lines = out_ref.shape[0]
    table = table_ref[...]
    table = jnp.concatenate([table, table], axis=1)
    named = table[:slots]
    line_row = iota((lines, 128), 0)
    live = table[slots + 3 : slots + 4]
    names = jnp.zeros((lines, 128), F32)
    asks = jnp.zeros((lines, 128), F32)
    for s in range(slots):
        same = named[s : s + 1] == line_row
        names = jnp.where(same, 1.0, names)
        asks = jnp.where(same & (s < live), 1.0, asks)
    earlier = iota((128, 128), 0) < iota((128, 128), 1) % outages
    rank = lax.dot_general(
        names.astype(BF16), jnp.where(earlier, 1.0, 0.0).astype(BF16), NN, preferred_element_type=F32
    )
    rank = jnp.where(asks > 0.0, rank, -1.0)
    start = table[slots : slots + 1] + 1
    end = table[slots + 1 : slots + 2] + 1
    place = table[slots + 2 : slots + 3] + 1
    second = iota((1, 128), 1) // outages
    spot = iota((128, 128), 0)
    chosen, high, low = [], [], []
    for t in range(CAP // 2):
        turn = 2 * t + second
        chosen.append(jnp.where(rank == turn.astype(F32), 1.0, 0.0).astype(BF16))
        value = jnp.where(
            spot == turn, start, jnp.where(spot == 16 + turn, end, jnp.where(spot == 32 + turn, place, 0))
        )
        high.append((value >> 8).astype(F32).astype(BF16))
        low.append((value & 255).astype(F32).astype(BF16))
    chosen = jnp.concatenate(chosen, axis=1)
    high = lax.dot_general(chosen, jnp.concatenate(high, axis=1), NT, preferred_element_type=F32)
    low = lax.dot_general(chosen, jnp.concatenate(low, axis=1), NT, preferred_element_type=F32)
    out_ref[...] = 256.0 * high + low


def flow_kernel(s_ref, inj_ref, part_ref, flow_ref):
    rows, width = s_ref.shape
    whole, rest = width // CHUNK, width % CHUNK
    flow_ref[...] = jnp.zeros_like(flow_ref)

    def step(at, size):
        cols = pl.ds(at, size)
        flow_ref[...] += lax.dot_general(
            jnp.concatenate(split2(inj_ref[:, cols]), axis=0),
            jnp.concatenate(split2(s_ref[:, cols]), axis=0),
            NT,
            preferred_element_type=F32,
        )

    def body(q, carry):
        step(pl.multiple_of(q * CHUNK, CHUNK), CHUNK)
        return carry

    lax.fori_loop(0, whole, body, 0)
    step(whole * CHUNK, rest)
    part_ref[...] = (
        flow_ref[:HOURS, :rows]
        + (flow_ref[:HOURS, rows:] + flow_ref[HOURS:, :rows])
        + flow_ref[HOURS:, rows:]
    )


def pick_kernel(
    req_ref,
    s_hbm,
    out_ref,
    s_ref,
    turn_ref,
    perm_ref,
    from_ref,
    to_ref,
    sum_ref,
    total_ref,
    s_sems,
):
    lines = req_ref.shape[0]
    rows, width = s_ref.shape
    peers, _, entries = out_ref.shape
    packed = from_ref.shape[0]
    deep = rows // peers
    whole, rest = width // CHUNK, width % CHUNK


    def copy(at, size, q):
        cols = pl.ds(at, size)
        return pltpu.make_async_copy(s_hbm.at[:, cols], s_ref.at[:, cols], s_sems.at[q])

    copy(whole * CHUNK, rest, whole).start()
    for q in range(whole):
        copy(q * CHUNK, CHUNK, q).start()
    bus = lax.axis_index("bus_x") * lax.axis_size("bus_z") + lax.axis_index("bus_z")
    base = (bus * width + 1).astype(F32)
    req = req_ref[...]
    lane = iota((lines, 128), 1)
    first = req - base
    second = pltpu.roll(req, 112, 1) - base
    has_first = (first >= 0.0) & (first < float(width))
    has_second = (second >= 0.0) & (second < float(width))
    used = (has_first | has_second) & (first != second) & (lane < CAP)
    mask = jnp.where(used, 1.0, 0.0)
    hits = mask.astype(BF16)
    above = jnp.where(iota((lines, lines), 1) < iota((lines, lines), 0), 1.0, 0.0).astype(BF16)
    ahead = jnp.where(iota((128, 128), 0) < iota((128, 128), 1), 1.0, 0.0).astype(BF16)
    ones = jnp.ones((lines, lines), BF16)
    in_lane = lax.dot_general(ones, hits, NN, preferred_element_type=F32)
    rank = lax.dot_general(above, hits, NN, preferred_element_type=F32) + lax.dot_general(
        in_lane.astype(BF16), ahead, NN, preferred_element_type=F32
    )
    rank = jnp.where(used, rank, -1.0)
    count = jnp.sum(mask).astype(jnp.int32)
    blocks = (count + (packed - 1)) // packed
    first = jnp.where(has_first & used, first + 1.0, 0.0)
    second = jnp.where(has_second & used, second + 1.0, 0.0)
    first_high = jnp.floor(first * (1.0 / 128.0))
    second_high = jnp.floor(second * (1.0 / 128.0))
    fields = (first_high, first - 128.0 * first_high, second_high, second - 128.0 * second_high, rank)
    mixed = pltpu.roll(req, 48, 1)
    for q in reversed(range(5)):
        field = pltpu.roll(fields[q], 16 * q, 1) if q else fields[q]
        mixed = jnp.where(lane < 16 * (q + 1), field, mixed) if q < 4 else jnp.where(lane < 80, field, mixed)
    turn_ref[...] = jnp.transpose(jnp.concatenate([mixed, jnp.zeros((128 - lines, 128), F32)], axis=0))
    pairs = []
    lane_row = iota((8, 128), 1)
    for t in range(CAP // 2):
        even = turn_ref[pl.ds(2 * t, 8, stride=16), :]
        odd = turn_ref[pl.ds(2 * t + 1, 8, stride=16), :]
        pairs.append(jnp.where(lane_row < lines, even, pltpu.roll(odd, lines, 1)))
    table = jnp.concatenate(pairs, axis=1)
    ranks = table[4:5].astype(jnp.int32)
    offs = table[5:6].astype(jnp.int32) - 1
    table_low = table.astype(BF16)
    one, minus, zero = jnp.asarray(1, BF16), jnp.asarray(-1, BF16), jnp.asarray(0, BF16)
    total_ref[...] = jnp.zeros_like(total_ref)

    def open_block(block):
        perm = jnp.where(iota((packed, entries), 0) + block * packed == ranks, 1.0, 0.0).astype(BF16)
        perm_ref[...] = perm
        ends = lax.dot_general(perm, table_low, NT, preferred_element_type=F32)
        start = (128.0 * ends[:, 0:1] + ends[:, 1:2] - 1.0).astype(jnp.int32)
        end = (128.0 * ends[:, 2:3] + ends[:, 3:4] - 1.0).astype(jnp.int32)
        from_ref[...] = jnp.broadcast_to(start, (packed, 128)).astype(jnp.int16)
        to_ref[...] = jnp.broadcast_to(end, (packed, 128)).astype(jnp.int16)
        sum_ref[...] = jnp.zeros_like(sum_ref)

    def hot(at, size):
        columns = []
        for t in range(size // 128):
            spot = (iota((16, 128), 1) + (at + t * 128)).astype(jnp.int16)
            spot = jnp.broadcast_to(spot[None], (packed // 16, 16, 128)).reshape(packed, 128)
            columns.append(
                jnp.where(from_ref[...] == spot, one, jnp.where(to_ref[...] == spot, minus, zero))
            )
        return jnp.concatenate(columns, axis=1)

    def multiply(left, at, size):
        both = jnp.concatenate(split2(s_ref[:, pl.ds(at, size)]), axis=0)
        return lax.dot_general(left, both, NT, preferred_element_type=F32)

    def close_block():
        turned = jnp.transpose(sum_ref[:, :rows] + sum_ref[:, rows:])
        both = lax.dot_general(
            jnp.concatenate(split2(turned), axis=0), perm_ref[...], NN, preferred_element_type=F32
        )
        total_ref[...] += both[:rows] + both[rows:]

    def pick(at, size):
        sum_ref[...] += multiply(hot(at, size), at, size)

    open_block(0)
    copy(whole * CHUNK, rest, whole).wait()
    pick(whole * CHUNK, rest)

    def first_block(q, carry):
        at = pl.multiple_of(q * CHUNK, CHUNK)
        copy(at, CHUNK, q).wait()
        pick(at, CHUNK)
        return carry

    lax.fori_loop(0, whole, first_block, 0)
    close_block()

    def other_block(block, carry):
        open_block(block)
        pick(whole * CHUNK, rest)

        def piece(q, carry):
            pick(pl.multiple_of(q * CHUNK, CHUNK), CHUNK)
            return carry

        lax.fori_loop(0, whole, piece, 0)
        close_block()
        return carry

    lax.fori_loop(1, blocks, other_block, 0)
    total = total_ref[...]
    own = jnp.sum(jnp.where(iota((rows, entries), 0) == offs, total, 0.0), axis=0, keepdims=True)
    own = [own[:, 128 * t : 128 * t + 128] for t in range(CAP // 2)] + [jnp.zeros((2, 128), F32)]
    own = jnp.concatenate(own, axis=0)
    for b in range(peers):
        out_ref[b, :deep, :] = total[b * deep : (b + 1) * deep]
        out_ref[b, deep:, :512] = jnp.zeros((8, 512), F32)
        out_ref[b, deep:, 512:640] = own
        out_ref[b, deep:, 640:] = jnp.zeros((8, 128), F32)


def merge_kernel(message_ref, mine_ref, other_ref, out_ref):
    flows = mine_ref[...] + other_ref[...]
    flows = jnp.concatenate([flows[8 * t : 8 * t + 8] for t in range(4)], axis=1)
    deep = out_ref.shape[1] - 8
    for b in range(out_ref.shape[0]):
        out_ref[b, :deep, :] = message_ref[b, :deep, :]
        out_ref[b, deep:, :512] = flows
        out_ref[b, deep:, 512:] = message_ref[b, deep:, 512:]


def reply_kernel(got_ref, req_ref, rate_ref, out_ref, rate_scratch):
    peers = got_ref.shape[0]
    lines = req_ref.shape[0]
    rows = rate_ref.shape[1]
    passes = out_ref.shape[0] // (lines * TILES)
    sub = (got_ref.shape[1] - 8) // passes
    half = HOURS // passes
    place = lax.axis_index("bus_x") * passes
    total = got_ref[0]
    for b in range(1, peers):
        total = total + got_ref[b]
    sens, rest = total[: passes * sub], total[passes * sub :]
    flows = jnp.where(
        lax.axis_index("bus_z") == 0,
        jnp.concatenate([rest[:, 0:128], rest[:, 128:256]], axis=0),
        jnp.concatenate([rest[:, 256:384], rest[:, 384:512]], axis=0),
    )
    lane = iota((half, 128), 1)
    hour = iota((half, 128), 0)
    f_high, f_low = split2(flows)
    f_rest = (flows - f_high.astype(F32) - f_low.astype(F32)).astype(BF16)
    f_all = jnp.concatenate([f_high, f_low, f_rest], axis=0)
    req = req_ref[...]
    lane_line = iota((lines, 128), 1)
    hots = [
        jnp.where(lane_line == req[:, 32 + c : 33 + c].astype(jnp.int32) - 1, 1.0, 0.0).astype(BF16)
        for c in range(CAP)
    ] + [jnp.zeros((lines, 128), BF16)] * 4
    left = jnp.concatenate([jnp.concatenate(hots[8 * q : 8 * q + 8], axis=1) for q in range(2)], axis=0)

    def diagonal(block):
        blank = jnp.zeros_like(block)
        return jnp.concatenate(
            [jnp.concatenate([block if v == u else blank for v in range(8)], axis=1) for u in range(8)], axis=0
        )

    lost = lax.dot_general(
        left, diagonal(f_high), NT, preferred_element_type=F32
    ) + lax.dot_general(left, diagonal(f_low), NT, preferred_element_type=F32)
    rate_scratch[...] = 0.5 * jnp.transpose(jnp.broadcast_to(rate_ref[...], (rows, 128)))

    def wide(block):
        return jnp.concatenate([block, jnp.zeros((block.shape[0], 128 - lines), F32)], axis=1)

    def put(p, q, block):
        out_ref[pl.ds(p * lines * TILES + q, lines, stride=TILES), :] = block

    for p in range(passes):
        wanted = iota((128, 128), 0) == (place + p) * sub + iota((128, 128), 1) % sub
        spread = lax.dot_general(f_all, jnp.where(wanted, 1.0, 0.0).astype(BF16), NN, preferred_element_type=F32)
        spread = spread[:half] + spread[half : 2 * half] + spread[2 * half :]
        spread = jnp.where(lane // sub == hour % 8, spread, 0.0)
        for t in range(2):
            row = jnp.sum(spread[8 * t : 8 * t + 8], axis=0, keepdims=True)
            put(p, t, jnp.broadcast_to(row, (lines, 128)))
        rate = rate_scratch[pl.ds(pl.multiple_of((place + p) * sub, sub), sub), :]
        part = sens[p * sub : (p + 1) * sub]
        blocks = [wide(part[:, c * lines : (c + 1) * lines]) for c in range(CAP)]
        one = jnp.concatenate(blocks[:8], axis=0)
        two = jnp.concatenate([jnp.zeros((64, 128), F32)] + blocks[8:], axis=0)
        three = jnp.concatenate(
            [rest[:, 512:640], pltpu.roll(rest[:, 512:640], lines, 1), rate, jnp.zeros((96, 128), F32)], axis=0
        )
        put(p, 2, lost[:lines])
        put(p, 3, jnp.where(lane_line < 64, lost[lines:], jnp.transpose(two)[:lines]))
        put(p, 4, jnp.transpose(one)[:lines])
        put(p, 5, jnp.transpose(three)[:lines])


def screen_kernel(got_ref, table_ref, out_ref):
    slots, sub, outages = out_ref.shape
    passes = lax.axis_size("bus_z")
    lines = got_ref.shape[0] // (passes * TILES)
    place = lax.axis_index("bus_x") * passes + lax.axis_index("bus_z")
    half = HOURS // passes

    def tile(p, t):
        return got_ref[pl.ds(p * lines * TILES + t, lines, stride=TILES), :]

    def piece(block):
        high = block.astype(BF16).astype(F32)
        low = (block - high).astype(BF16).astype(F32)
        return jnp.transpose(jnp.concatenate([high, low], axis=0)).astype(BF16)

    sums = [piece(tile(0, t) + tile(1, t)) for t in (4, 3, 5)]
    shared = jnp.concatenate([piece(tile(p, t)) for p in range(passes) for t in range(2)] + sums, axis=0)
    own = jnp.concatenate([piece(tile(p, t)) for p in range(passes) for t in range(2, 4)] + sums[2:], axis=0)
    table = jnp.concatenate([table_ref[...], table_ref[...]], axis=1)
    named = table[:slots]
    line_row = iota((lines, 128), 0)
    lane = iota((1, 128), 1)
    outage = lane % outages
    names = jnp.zeros((lines, 128), F32)
    for s in range(slots):
        names = jnp.where(named[s : s + 1] == line_row, 1.0, names)
    earlier = iota((128, 128), 0) < iota((128, 128), 1) % outages
    rank = lax.dot_general(
        names.astype(BF16),
        jnp.where(earlier, 1.0, 0.0).astype(BF16),
        (((1,), (0,)), ((), ())),
        preferred_element_type=F32,
    )

    def hot_of(target):
        hot = jnp.where(line_row == target, 1.0, 0.0)
        turn = jnp.sum(hot * rank, axis=0, keepdims=True)
        hot = hot.astype(BF16)
        return jnp.concatenate([hot, hot], axis=0), turn

    plain = (((1,), (0,)), ((), ()))
    hot_own, turn_own = hot_of(named[0:1])
    got_own = lax.dot_general(own, hot_own, plain, preferred_element_type=F32)
    lost = [jnp.zeros((half, 128), F32)] * passes
    self_sens = jnp.zeros((1, 128), F32)
    for c in range(CAP):
        mine = turn_own == float(c)
        for p in range(passes):
            at = 256 * p + half * c
            lost[p] = jnp.where(mine, got_own[at : at + half], lost[p])
        at = 512 + 8 * (c % 2) + c // 2
        self_sens = jnp.where(mine, got_own[at : at + 1], self_sens)
    lost = jnp.concatenate(lost, axis=0)
    divisor = jnp.maximum(1.0 - self_sens, floor_value)
    off = table[slots + 2 : slots + 3]
    live = table[slots + 3 : slots + 4]
    row = iota((sub, 128), 0)
    for t in range(slots // 2):
        target = jnp.where(lane < outages, named[2 * t : 2 * t + 1], named[2 * t + 1 : 2 * t + 2])
        hot, turn = hot_of(target)
        got = lax.dot_general(shared, hot, plain, preferred_element_type=F32)
        sens = jnp.zeros((sub, 128), F32)
        for c in range(CAP):
            at = 512 + sub * c + (64 if c >= 8 else 0)
            sens = jnp.where(turn == float(c), got[at : at + sub], sens)
        factor = sens / divisor
        worst = jnp.zeros((sub, 128), F32)
        for h in range(HOURS):
            worst = jnp.maximum(worst, jnp.abs(got[sub * h : sub * h + sub] + factor * lost[h : h + 1]))
        result = worst / got[784:800]
        slot = 2 * t + jnp.where(lane < outages, 0, 1)
        keep = slot < live
        if t == 0:
            keep = keep & ~((slot == 0) & (row == off - place * sub))
        result = jnp.where(keep, result, 0.0)
        out_ref[2 * t] = result[:, :outages]
        out_ref[2 * t + 1] = result[:, outages:]


def call(kernel, out_shape, in_specs, scratch=(), flops=0, moved=0, limit=16):
    return pl.pallas_call(
        kernel,
        out_shape=out_shape,
        in_specs=in_specs,
        out_specs=IN_VMEM,
        scratch_shapes=list(scratch),
        compiler_params=pltpu.CompilerParams(vmem_limit_bytes=limit * 1024 * 1024),
        cost_estimate=pl.CostEstimate(flops=flops, bytes_accessed=moved, transcendentals=0),
    )


def local(shift_factors, injection, rating, monitored, live_count, outage_offset, outage_ends):
    peers = lax.axis_size("bus_x")
    passes = lax.axis_size("bus_z")
    line_count = lax.axis_size("line")
    block_rows, bus_width = shift_factors.shape
    sub_rows = block_rows // (peers * passes)
    outages, slot_count = monitored.shape
    entries = CAP * line_count
    shape = jax.ShapeDtypeStruct
    rate_row = rating.reshape(1, block_rows)
    table = jnp.concatenate(
        [monitored.T, outage_ends.T, outage_offset.reshape(1, outages), live_count.reshape(1, outages)], axis=0
    )
    with jax.named_scope("requests"):
        requests = call(request_kernel, shape((line_count, 128), F32), [IN_VMEM], flops=10**10, moved=10**7)(
            table
        )
        asked = lax.all_to_all(requests, "line", split_axis=0, concat_axis=0, tiled=True)
    with jax.named_scope("flows"):
        mine = call(
            flow_kernel,
            shape((HOURS, block_rows), F32),
            [IN_VMEM] * 2,
            scratch=(pltpu.VMEM((2 * HOURS, 2 * block_rows), F32),),
            flops=8 * HOURS * block_rows * bus_width,
            moved=4 * block_rows * bus_width,
        )(shift_factors, injection)
        other = lax.ppermute(mine, "bus_z", [(p, (p + 1) % passes) for p in range(passes)])
    with jax.named_scope("picks"):
        partial_sens = call(
            pick_kernel,
            shape((peers, passes * sub_rows + 8, entries), F32),
            [IN_VMEM, IN_HBM],
            scratch=(
                pltpu.VMEM((block_rows, bus_width), F32),
                pltpu.VMEM((128, 128), F32),
                pltpu.VMEM((PACKED, entries), BF16),
                pltpu.VMEM((PACKED, 128), jnp.int16),
                pltpu.VMEM((PACKED, 128), jnp.int16),
                pltpu.VMEM((PACKED, 2 * block_rows), F32),
                pltpu.VMEM((block_rows, entries), F32),
                pltpu.SemaphoreType.DMA((bus_width // CHUNK + 1,)),
            ),
            flops=4 * entries * block_rows * bus_width,
            moved=4 * block_rows * bus_width,
            limit=53,
        )(asked, shift_factors)
        partial_sens = call(merge_kernel, shape((peers, passes * sub_rows + 8, entries), F32), [IN_VMEM] * 3)(
            partial_sens, mine, other
        )
        half_sens = lax.all_to_all(partial_sens, "bus_x", split_axis=0, concat_axis=0, tiled=True)
    with jax.named_scope("reply"):
        reply = call(
            reply_kernel,
            shape((passes * line_count * TILES, 128), F32),
            [IN_VMEM] * 3,
            scratch=(pltpu.VMEM((block_rows, block_rows), F32),),
        )(half_sens, asked, rate_row)
        reply = reply.reshape(passes * line_count, TILES * 128)
        got = lax.all_to_all(reply, ("bus_z", "line"), split_axis=0, concat_axis=0, tiled=True)
    with jax.named_scope("screen"):
        loading = call(screen_kernel, shape((slot_count, sub_rows, outages), F32), [IN_VMEM] * 2)(
            got.reshape(-1, 128), table
        )
    return jnp.transpose(loading, (2, 0, 1))


def solution(mesh):
    lines, buses = mesh.devices.shape
    bus = ("bus_x", "bus_z")
    return jax.shard_map(
        local,
        mesh=jax.sharding.Mesh(mesh.devices.reshape(lines, buses // PASS, PASS), ("line",) + bus),
        in_specs=(
            P("line", bus),
            P(None, bus),
            P("line"),
            P("line", None),
            P("line"),
            P("line"),
            P("line", None),
        ),
        out_specs=P("line", None, bus),
        check_vma=False,
    )
```

```python
import jax
import jax.numpy as jnp
from jax import lax
from jax.experimental import pallas as pl
from jax.experimental.pallas import tpu as pltpu
from jax.sharding import PartitionSpec as P

floor_value = 0.25
F32 = jnp.float32
BF16 = jnp.bfloat16
NT = (((1,), (1,)), ((), ()))
NN = (((1,), (0,)), ((), ()))
HOURS = 32
CAP = 12
CHUNK = 3072
PASS = 2
TILES = 9
PACKED = 160
IN_VMEM = pl.BlockSpec(memory_space=pltpu.VMEM)


def iota(shape, axis):
    return lax.broadcasted_iota(jnp.int32, shape, axis)


def split2(value):
    high = value.astype(BF16)
    return high, (value - high.astype(F32)).astype(BF16)


def request_kernel(table_ref, out_ref):
    outages = table_ref.shape[1]
    slots = table_ref.shape[0] - 4
    lines = out_ref.shape[0]
    table = table_ref[...]
    table = jnp.concatenate([table, table], axis=1)
    named = table[:slots]
    line_row = iota((lines, 128), 0)
    live = table[slots + 3 : slots + 4]
    names = jnp.zeros((lines, 128), F32)
    asks = jnp.zeros((lines, 128), F32)
    for s in range(slots):
        same = named[s : s + 1] == line_row
        names = jnp.where(same, 1.0, names)
        asks = jnp.where(same & (s < live), 1.0, asks)
    earlier = iota((128, 128), 0) < iota((128, 128), 1) % outages
    rank = lax.dot_general(
        names.astype(BF16), jnp.where(earlier, 1.0, 0.0).astype(BF16), NN, preferred_element_type=F32
    )
    rank = jnp.where(asks > 0.0, rank, -1.0)
    start = table[slots : slots + 1] + 1
    end = table[slots + 1 : slots + 2] + 1
    place = table[slots + 2 : slots + 3] + 1
    second = iota((1, 128), 1) // outages
    spot = iota((128, 128), 0)
    chosen, high, low = [], [], []
    for t in range(CAP // 2):
        turn = 2 * t + second
        chosen.append(jnp.where(rank == turn.astype(F32), 1.0, 0.0).astype(BF16))
        value = jnp.where(
            spot == turn, start, jnp.where(spot == 16 + turn, end, jnp.where(spot == 32 + turn, place, 0))
        )
        high.append((value >> 8).astype(F32).astype(BF16))
        low.append((value & 255).astype(F32).astype(BF16))
    chosen = jnp.concatenate(chosen, axis=1)
    high = lax.dot_general(chosen, jnp.concatenate(high, axis=1), NT, preferred_element_type=F32)
    low = lax.dot_general(chosen, jnp.concatenate(low, axis=1), NT, preferred_element_type=F32)
    out_ref[...] = 256.0 * high + low


def pick_kernel(
    req_ref,
    s_ref,
    inj_ref,
    out_ref,
    turn_ref,
    perm_ref,
    from_ref,
    to_ref,
    sum_ref,
    total_ref,
):
    lines = req_ref.shape[0]
    rows, width = s_ref.shape
    peers, _, entries = out_ref.shape
    packed = from_ref.shape[0]
    deep = rows // peers
    whole, rest = width // CHUNK, width % CHUNK

    bus = lax.axis_index("bus_x") * lax.axis_size("bus_z") + lax.axis_index("bus_z")
    base = (bus * width + 1).astype(F32)
    req = req_ref[...]
    lane = iota((lines, 128), 1)
    first = req - base
    second = pltpu.roll(req, 112, 1) - base
    has_first = (first >= 0.0) & (first < float(width))
    has_second = (second >= 0.0) & (second < float(width))
    used = (has_first | has_second) & (first != second) & (lane < CAP)
    mask = jnp.where(used, 1.0, 0.0)
    hits = mask.astype(BF16)
    above = jnp.where(iota((lines, lines), 1) < iota((lines, lines), 0), 1.0, 0.0).astype(BF16)
    ahead = jnp.where(iota((128, 128), 0) < iota((128, 128), 1), 1.0, 0.0).astype(BF16)
    ones = jnp.ones((lines, lines), BF16)
    in_lane = lax.dot_general(ones, hits, NN, preferred_element_type=F32)
    rank = lax.dot_general(above, hits, NN, preferred_element_type=F32) + lax.dot_general(
        in_lane.astype(BF16), ahead, NN, preferred_element_type=F32
    )
    rank = jnp.where(used, rank, -1.0)
    count = jnp.sum(mask).astype(jnp.int32)
    blocks = (count + (packed - 1)) // packed
    first = jnp.where(has_first & used, first + 1.0, 0.0)
    second = jnp.where(has_second & used, second + 1.0, 0.0)
    first_high = jnp.floor(first * (1.0 / 128.0))
    second_high = jnp.floor(second * (1.0 / 128.0))
    fields = (first_high, first - 128.0 * first_high, second_high, second - 128.0 * second_high, rank)
    mixed = pltpu.roll(req, 48, 1)
    for q in reversed(range(5)):
        field = pltpu.roll(fields[q], 16 * q, 1) if q else fields[q]
        mixed = jnp.where(lane < 16 * (q + 1), field, mixed) if q < 4 else jnp.where(lane < 80, field, mixed)
    turn_ref[...] = jnp.transpose(jnp.concatenate([mixed, jnp.zeros((128 - lines, 128), F32)], axis=0))
    pairs = []
    lane_row = iota((8, 128), 1)
    for t in range(CAP // 2):
        even = turn_ref[pl.ds(2 * t, 8, stride=16), :]
        odd = turn_ref[pl.ds(2 * t + 1, 8, stride=16), :]
        pairs.append(jnp.where(lane_row < lines, even, pltpu.roll(odd, lines, 1)))
    table = jnp.concatenate(pairs, axis=1)
    ranks = table[4:5].astype(jnp.int32)
    offs = table[5:6].astype(jnp.int32) - 1
    table_low = table.astype(BF16)
    one, minus, zero = jnp.asarray(1, BF16), jnp.asarray(-1, BF16), jnp.asarray(0, BF16)

    def open_block(block):
        perm = jnp.where(iota((packed, entries), 0) + block * packed == ranks, 1.0, 0.0).astype(BF16)
        perm_ref[...] = perm
        ends = lax.dot_general(perm, table_low, NT, preferred_element_type=F32)
        start = (128.0 * ends[:, 0:1] + ends[:, 1:2] - 1.0).astype(jnp.int32)
        end = (128.0 * ends[:, 2:3] + ends[:, 3:4] - 1.0).astype(jnp.int32)
        from_ref[...] = jnp.broadcast_to(start, (packed, 128)).astype(jnp.int16)
        to_ref[...] = jnp.broadcast_to(end, (packed, 128)).astype(jnp.int16)

    def hot(at, size):
        columns = []
        for t in range(size // 128):
            spot = (iota((16, 128), 1) + (at + t * 128)).astype(jnp.int16)
            spot = jnp.broadcast_to(spot[None], (packed // 16, 16, 128)).reshape(packed, 128)
            columns.append(
                jnp.where(from_ref[...] == spot, one, jnp.where(to_ref[...] == spot, minus, zero))
            )
        return jnp.concatenate(columns, axis=1)

    def multiply(left, at, size):
        both = jnp.concatenate(split2(s_ref[:, pl.ds(at, size)]), axis=0)
        return lax.dot_general(left, both, NT, preferred_element_type=F32)

    def close_block():
        turned = jnp.transpose(sum_ref[:packed, :rows] + sum_ref[:packed, rows:])
        both = lax.dot_general(
            jnp.concatenate(split2(turned), axis=0), perm_ref[...], NN, preferred_element_type=F32
        )
        return both[:rows] + both[rows:]

    def step(at, size):
        left = jnp.concatenate((hot(at, size),) + split2(inj_ref[:, pl.ds(at, size)]), axis=0)
        return multiply(left, at, size)

    def pick(at, size):
        return multiply(hot(at, size), at, size)

    open_block(0)
    sum_ref[...] = step(whole * CHUNK, rest)

    def first_block(q, carry):
        at = pl.multiple_of(q * CHUNK, CHUNK)
        sum_ref[...] += step(at, CHUNK)
        return carry

    lax.fori_loop(0, whole, first_block, 0)
    flows = sum_ref[packed:]
    part = (
        flows[:HOURS, :rows] + (flows[:HOURS, rows:] + flows[HOURS:, :rows]) + flows[HOURS:, rows:]
    )
    total_ref[...] = close_block()

    def other_block(block, carry):
        open_block(block)
        sum_ref[:packed] = pick(whole * CHUNK, rest)

        def piece(q, carry):
            sum_ref[:packed] += pick(pl.multiple_of(q * CHUNK, CHUNK), CHUNK)
            return carry

        lax.fori_loop(0, whole, piece, 0)
        total_ref[...] += close_block()
        return carry

    lax.fori_loop(1, blocks, other_block, 0)
    total = total_ref[...]
    own = jnp.sum(jnp.where(iota((rows, entries), 0) == offs, total, 0.0), axis=0, keepdims=True)
    own = [own[:, 128 * t : 128 * t + 128] for t in range(CAP // 2)] + [jnp.zeros((2, 128), F32)]
    extra = jnp.concatenate(
        [part[8 * t : 8 * t + 8] for t in range(4)] + [jnp.concatenate(own, axis=0), jnp.zeros((8, 128), F32)],
        axis=1,
    )
    for b in range(peers):
        out_ref[b, :deep, :] = total[b * deep : (b + 1) * deep]
        out_ref[b, deep:, :] = extra


def reply_kernel(got_ref, req_ref, rate_ref, out_ref, rate_scratch):
    peers = got_ref.shape[0]
    lines = req_ref.shape[0]
    rows = rate_ref.shape[1]
    passes = out_ref.shape[0] // (lines * TILES)
    sub = (got_ref.shape[1] - 8) // passes
    place = lax.axis_index("bus_x") * passes
    total = got_ref[0]
    for b in range(1, peers):
        total = total + got_ref[b]
    sens, rest = total[: passes * sub], total[passes * sub :]
    flows = jnp.concatenate([rest[:, 128 * t : 128 * t + 128] for t in range(4)], axis=0)
    lane = iota((HOURS, 128), 1)
    hour = iota((HOURS, 128), 0)
    f_high, f_low = split2(flows)
    f_rest = (flows - f_high.astype(F32) - f_low.astype(F32)).astype(BF16)
    f_all = jnp.concatenate([f_high, f_low, f_rest], axis=0)
    req = req_ref[...]
    lane_line = iota((lines, 128), 1)
    hots = [
        jnp.where(lane_line == req[:, 32 + c : 33 + c].astype(jnp.int32) - 1, 1.0, 0.0).astype(BF16)
        for c in range(CAP)
    ]
    left = jnp.concatenate([jnp.concatenate(hots[4 * q : 4 * q + 4], axis=1) for q in range(3)], axis=0)

    def diagonal(block):
        blank = jnp.zeros_like(block)
        return jnp.concatenate(
            [jnp.concatenate([block if v == u else blank for v in range(4)], axis=1) for u in range(4)], axis=0
        )

    lost = lax.dot_general(
        left, diagonal(f_high), NT, preferred_element_type=F32
    ) + lax.dot_general(left, diagonal(f_low), NT, preferred_element_type=F32)
    rate_scratch[...] = 0.5 * jnp.transpose(jnp.broadcast_to(rate_ref[...], (rows, 128)))

    def wide(block):
        return jnp.concatenate([block, jnp.zeros((block.shape[0], 128 - lines), F32)], axis=1)

    def put(p, q, block):
        out_ref[pl.ds(p * TILES + q, lines, stride=passes * TILES), :] = block

    for p in range(passes):
        wanted = iota((128, 128), 0) == (place + p) * sub + iota((128, 128), 1) % sub
        spread = lax.dot_general(f_all, jnp.where(wanted, 1.0, 0.0).astype(BF16), NN, preferred_element_type=F32)
        spread = spread[:HOURS] + spread[HOURS : 2 * HOURS] + spread[2 * HOURS :]
        spread = jnp.where(lane // sub == hour % 8, spread, 0.0)
        for t in range(4):
            row = jnp.sum(spread[8 * t : 8 * t + 8], axis=0, keepdims=True)
            put(p, t, jnp.broadcast_to(row, (lines, 128)))
        for q in range(3):
            put(p, 4 + q, lost[q * lines : (q + 1) * lines])
        rate = rate_scratch[pl.ds(pl.multiple_of((place + p) * sub, sub), sub), :]
        part = sens[p * sub : (p + 1) * sub]
        blocks = [wide(part[:, c * lines : (c + 1) * lines]) for c in range(CAP)]
        one = jnp.concatenate(blocks[:8], axis=0)
        two = jnp.concatenate(
            blocks[8:]
            + [rest[:, 512:640], pltpu.roll(rest[:, 512:640], lines, 1), rate, jnp.zeros((32, 128), F32)],
            axis=0,
        )
        put(p, 7, jnp.transpose(one)[:lines])
        put(p, 8, jnp.transpose(two)[:lines])


def screen_kernel(got_ref, table_ref, out_ref):
    slots, sub, outages = out_ref.shape
    passes = lax.axis_size("bus_z")
    lines = got_ref.shape[0] // (passes * TILES)
    place = lax.axis_index("bus_x") * passes + lax.axis_index("bus_z")
    pieces = []
    for t in range(TILES):
        block = got_ref[pl.ds(t, lines, stride=passes * TILES), :]
        for p in range(1, passes):
            block = block + got_ref[pl.ds(p * TILES + t, lines, stride=passes * TILES), :]
        high = block.astype(BF16).astype(F32)
        low = (block - high).astype(BF16).astype(F32)
        pieces.append(jnp.transpose(jnp.concatenate([high, low], axis=0)).astype(BF16))
    shared = jnp.concatenate(pieces[:4] + pieces[7:], axis=0)
    own = jnp.concatenate(pieces[4:7] + pieces[8:], axis=0)
    table = jnp.concatenate([table_ref[...], table_ref[...]], axis=1)
    named = table[:slots]
    line_row = iota((lines, 128), 0)
    lane = iota((1, 128), 1)
    outage = lane % outages
    names = jnp.zeros((lines, 128), F32)
    for s in range(slots):
        names = jnp.where(named[s : s + 1] == line_row, 1.0, names)
    earlier = iota((128, 128), 0) < iota((128, 128), 1) % outages
    rank = lax.dot_general(
        names.astype(BF16),
        jnp.where(earlier, 1.0, 0.0).astype(BF16),
        (((1,), (0,)), ((), ())),
        preferred_element_type=F32,
    )

    def hot_of(target):
        hot = jnp.where(line_row == target, 1.0, 0.0)
        turn = jnp.sum(hot * rank, axis=0, keepdims=True)
        hot = hot.astype(BF16)
        return jnp.concatenate([hot, hot], axis=0), turn

    plain = (((1,), (0,)), ((), ()))
    hot_own, turn_own = hot_of(named[0:1])
    got_own = lax.dot_general(own, hot_own, plain, preferred_element_type=F32)
    lost = jnp.zeros((HOURS, 128), F32)
    self_sens = jnp.zeros((1, 128), F32)
    for c in range(CAP):
        mine = turn_own == float(c)
        lost = jnp.where(mine, got_own[HOURS * c : HOURS * c + HOURS], lost)
        at = 448 + 8 * (c % 2) + c // 2
        self_sens = jnp.where(mine, got_own[at : at + 1], self_sens)
    divisor = jnp.maximum(1.0 - self_sens, floor_value)
    off = table[slots + 2 : slots + 3]
    live = table[slots + 3 : slots + 4]
    lost_scaled = lost
    row = iota((sub, 128), 0)
    for t in range(slots // 2):
        target = jnp.where(lane < outages, named[2 * t : 2 * t + 1], named[2 * t + 1 : 2 * t + 2])
        hot, turn = hot_of(target)
        got = lax.dot_general(shared, hot, plain, preferred_element_type=F32)
        sens = jnp.zeros((sub, 128), F32)
        for c in range(CAP):
            sens = jnp.where(turn == float(c), got[512 + sub * c : 512 + sub * c + sub], sens)
        factor = sens / divisor
        worst = jnp.zeros((sub, 128), F32)
        for h in range(HOURS):
            worst = jnp.maximum(worst, jnp.abs(got[sub * h : sub * h + sub] + factor * lost_scaled[h : h + 1]))
        result = worst / got[720:736]
        slot = 2 * t + jnp.where(lane < outages, 0, 1)
        keep = slot < live
        if t == 0:
            keep = keep & ~((slot == 0) & (row == off - place * sub))
        result = jnp.where(keep, result, 0.0)
        out_ref[2 * t] = result[:, :outages]
        out_ref[2 * t + 1] = result[:, outages:]


def call(kernel, out_shape, in_specs, scratch=(), flops=0, moved=0, limit=16):
    return pl.pallas_call(
        kernel,
        out_shape=out_shape,
        in_specs=in_specs,
        out_specs=IN_VMEM,
        scratch_shapes=list(scratch),
        compiler_params=pltpu.CompilerParams(vmem_limit_bytes=limit * 1024 * 1024),
        cost_estimate=pl.CostEstimate(flops=flops, bytes_accessed=moved, transcendentals=0),
    )


def local(shift_factors, injection, rating, monitored, live_count, outage_offset, outage_ends):
    peers = lax.axis_size("bus_x")
    passes = lax.axis_size("bus_z")
    line_count = lax.axis_size("line")
    block_rows, bus_width = shift_factors.shape
    sub_rows = block_rows // (peers * passes)
    outages, slot_count = monitored.shape
    entries = CAP * line_count
    shape = jax.ShapeDtypeStruct
    rate_row = rating.reshape(1, block_rows)
    table = jnp.concatenate(
        [monitored.T, outage_ends.T, outage_offset.reshape(1, outages), live_count.reshape(1, outages)], axis=0
    )
    with jax.named_scope("requests"):
        requests = call(request_kernel, shape((line_count, 128), F32), [IN_VMEM], flops=10**10, moved=10**7)(
            table
        )
        asked = lax.all_to_all(requests, "line", split_axis=0, concat_axis=0, tiled=True)
    with jax.named_scope("picks"):
        partial_sens = call(
            pick_kernel,
            shape((peers, passes * sub_rows + 8, entries), F32),
            [IN_VMEM] * 3,
            scratch=(
                pltpu.VMEM((128, 128), F32),
                pltpu.VMEM((PACKED, entries), BF16),
                pltpu.VMEM((PACKED, 128), jnp.int16),
                pltpu.VMEM((PACKED, 128), jnp.int16),
                pltpu.VMEM((PACKED + 2 * HOURS, 2 * block_rows), F32),
                pltpu.VMEM((block_rows, entries), F32),
            ),
            flops=4 * entries * block_rows * bus_width,
            moved=4 * block_rows * bus_width,
            limit=24,
        )(asked, shift_factors, injection)
        half_sens = lax.all_to_all(partial_sens, "bus_x", split_axis=0, concat_axis=0, tiled=True)
    with jax.named_scope("reply"):
        reply = call(
            reply_kernel,
            shape((passes * line_count * TILES, 128), F32),
            [IN_VMEM] * 3,
            scratch=(pltpu.VMEM((block_rows, block_rows), F32),),
        )(half_sens, asked, rate_row)
        reply = reply.reshape(passes * line_count, TILES * 128)
        got = lax.all_to_all(reply, ("line", "bus_z"), split_axis=0, concat_axis=0, tiled=True)
    with jax.named_scope("screen"):
        loading = call(screen_kernel, shape((slot_count, sub_rows, outages), F32), [IN_VMEM] * 2)(
            got.reshape(-1, 128), table
        )
    return jnp.transpose(loading, (2, 0, 1))


def solution(mesh):
    lines, buses = mesh.devices.shape
    bus = ("bus_x", "bus_z")
    return jax.shard_map(
        local,
        mesh=jax.sharding.Mesh(mesh.devices.reshape(lines, buses // PASS, PASS), ("line",) + bus),
        in_specs=(
            P("line", bus),
            P(None, bus),
            P("line"),
            P("line", None),
            P("line"),
            P("line"),
            P("line", None),
        ),
        out_specs=P("line", None, bus),
        check_vma=False,
    )
```

```python
import jax
import jax.numpy as jnp
from jax import lax
from jax.experimental import pallas as pl
from jax.experimental.pallas import tpu as pltpu
from jax.sharding import PartitionSpec as P

floor_value = 0.25
F32 = jnp.float32
BF16 = jnp.bfloat16
NT = (((1,), (1,)), ((), ()))
NN = (((1,), (0,)), ((), ()))
HOURS = 32
CAP = 12
CHUNK = 3072
PASS = 2
TILES = 9
PACKED = 160
IN_VMEM = pl.BlockSpec(memory_space=pltpu.VMEM)


def iota(shape, axis):
    return lax.broadcasted_iota(jnp.int32, shape, axis)


def split2(value):
    high = value.astype(BF16)
    return high, (value - high.astype(F32)).astype(BF16)


def request_kernel(table_ref, out_ref):
    outages = table_ref.shape[1]
    slots = table_ref.shape[0] - 4
    lines = out_ref.shape[0]
    table = table_ref[...]
    table = jnp.concatenate([table, table], axis=1)
    named = table[:slots]
    line_row = iota((lines, 128), 0)
    live = table[slots + 3 : slots + 4]
    names = jnp.zeros((lines, 128), F32)
    asks = jnp.zeros((lines, 128), F32)
    for s in range(slots):
        same = named[s : s + 1] == line_row
        names = jnp.where(same, 1.0, names)
        asks = jnp.where(same & (s < live), 1.0, asks)
    earlier = iota((128, 128), 0) < iota((128, 128), 1) % outages
    rank = lax.dot_general(
        names.astype(BF16), jnp.where(earlier, 1.0, 0.0).astype(BF16), NN, preferred_element_type=F32
    )
    rank = jnp.where(asks > 0.0, rank, -1.0)
    start = table[slots : slots + 1] + 1
    end = table[slots + 1 : slots + 2] + 1
    place = table[slots + 2 : slots + 3] + 1
    second = iota((1, 128), 1) // outages
    spot = iota((128, 128), 0)
    chosen, high, low = [], [], []
    for t in range(CAP // 2):
        turn = 2 * t + second
        chosen.append(jnp.where(rank == turn.astype(F32), 1.0, 0.0).astype(BF16))
        value = jnp.where(
            spot == turn, start, jnp.where(spot == 16 + turn, end, jnp.where(spot == 32 + turn, place, 0))
        )
        high.append((value >> 8).astype(F32).astype(BF16))
        low.append((value & 255).astype(F32).astype(BF16))
    chosen = jnp.concatenate(chosen, axis=1)
    high = lax.dot_general(chosen, jnp.concatenate(high, axis=1), NT, preferred_element_type=F32)
    low = lax.dot_general(chosen, jnp.concatenate(low, axis=1), NT, preferred_element_type=F32)
    out_ref[...] = 256.0 * high + low


def pick_kernel(
    req_ref,
    s_ref,
    inj_ref,
    out_ref,
    turn_ref,
    perm_ref,
    from_ref,
    to_ref,
    sum_ref,
    total_ref,
):
    lines = req_ref.shape[0]
    rows, width = s_ref.shape
    peers, _, entries = out_ref.shape
    packed = from_ref.shape[0]
    deep = rows // peers
    whole, rest = width // CHUNK, width % CHUNK

    bus = lax.axis_index("bus_x") * lax.axis_size("bus_z") + lax.axis_index("bus_z")
    base = (bus * width + 1).astype(F32)
    req = req_ref[...]
    lane = iota((lines, 128), 1)
    first = req - base
    second = pltpu.roll(req, 112, 1) - base
    has_first = (first >= 0.0) & (first < float(width))
    has_second = (second >= 0.0) & (second < float(width))
    used = (has_first | has_second) & (first != second) & (lane < CAP)
    mask = jnp.where(used, 1.0, 0.0)
    hits = mask.astype(BF16)
    above = jnp.where(iota((lines, lines), 1) < iota((lines, lines), 0), 1.0, 0.0).astype(BF16)
    ahead = jnp.where(iota((128, 128), 0) < iota((128, 128), 1), 1.0, 0.0).astype(BF16)
    ones = jnp.ones((lines, lines), BF16)
    in_lane = lax.dot_general(ones, hits, NN, preferred_element_type=F32)
    rank = lax.dot_general(above, hits, NN, preferred_element_type=F32) + lax.dot_general(
        in_lane.astype(BF16), ahead, NN, preferred_element_type=F32
    )
    rank = jnp.where(used, rank, -1.0)
    count = jnp.sum(mask).astype(jnp.int32)
    blocks = (count + (packed - 1)) // packed
    first = jnp.where(has_first & used, first + 1.0, 0.0)
    second = jnp.where(has_second & used, second + 1.0, 0.0)
    first_high = jnp.floor(first * (1.0 / 128.0))
    second_high = jnp.floor(second * (1.0 / 128.0))
    fields = (first_high, first - 128.0 * first_high, second_high, second - 128.0 * second_high, rank)
    mixed = pltpu.roll(req, 48, 1)
    for q in reversed(range(5)):
        field = pltpu.roll(fields[q], 16 * q, 1) if q else fields[q]
        mixed = jnp.where(lane < 16 * (q + 1), field, mixed) if q < 4 else jnp.where(lane < 80, field, mixed)
    turn_ref[...] = jnp.transpose(jnp.concatenate([mixed, jnp.zeros((128 - lines, 128), F32)], axis=0))
    pairs = []
    lane_row = iota((8, 128), 1)
    for t in range(CAP // 2):
        even = turn_ref[pl.ds(2 * t, 8, stride=16), :]
        odd = turn_ref[pl.ds(2 * t + 1, 8, stride=16), :]
        pairs.append(jnp.where(lane_row < lines, even, pltpu.roll(odd, lines, 1)))
    table = jnp.concatenate(pairs, axis=1)
    ranks = table[4:5].astype(jnp.int32)
    offs = table[5:6].astype(jnp.int32) - 1
    table_low = table.astype(BF16)
    one, minus, zero = jnp.asarray(1, BF16), jnp.asarray(-1, BF16), jnp.asarray(0, BF16)

    def open_block(block):
        perm = jnp.where(iota((packed, entries), 0) + block * packed == ranks, 1.0, 0.0).astype(BF16)
        perm_ref[...] = perm
        ends = lax.dot_general(perm, table_low, NT, preferred_element_type=F32)
        start = (128.0 * ends[:, 0:1] + ends[:, 1:2] - 1.0).astype(jnp.int32)
        end = (128.0 * ends[:, 2:3] + ends[:, 3:4] - 1.0).astype(jnp.int32)
        from_ref[...] = jnp.broadcast_to(start, (packed, 128)).astype(jnp.int16)
        to_ref[...] = jnp.broadcast_to(end, (packed, 128)).astype(jnp.int16)

    def hot(at, size):
        columns = []
        for t in range(size // 128):
            spot = (iota((16, 128), 1) + (at + t * 128)).astype(jnp.int16)
            spot = jnp.broadcast_to(spot[None], (packed // 16, 16, 128)).reshape(packed, 128)
            columns.append(
                jnp.where(from_ref[...] == spot, one, jnp.where(to_ref[...] == spot, minus, zero))
            )
        return jnp.concatenate(columns, axis=1)

    def multiply(left, at, size):
        both = jnp.concatenate(split2(s_ref[:, pl.ds(at, size)]), axis=0)
        return lax.dot_general(left, both, NT, preferred_element_type=F32)

    def close_block():
        turned = jnp.transpose(sum_ref[:packed, :rows] + sum_ref[:packed, rows:])
        both = lax.dot_general(
            jnp.concatenate(split2(turned), axis=0), perm_ref[...], NN, preferred_element_type=F32
        )
        return both[:rows] + both[rows:]

    def step(at, size):
        left = jnp.concatenate((hot(at, size),) + split2(inj_ref[:, pl.ds(at, size)]), axis=0)
        return multiply(left, at, size)

    def pick(at, size):
        return multiply(hot(at, size), at, size)

    open_block(0)
    sum_ref[...] = step(whole * CHUNK, rest)

    def first_block(q, carry):
        at = pl.multiple_of(q * CHUNK, CHUNK)
        sum_ref[...] += step(at, CHUNK)
        return carry

    lax.fori_loop(0, whole, first_block, 0)
    flows = sum_ref[packed:]
    part = (
        flows[:HOURS, :rows] + (flows[:HOURS, rows:] + flows[HOURS:, :rows]) + flows[HOURS:, rows:]
    )
    total_ref[...] = close_block()

    def other_block(block, carry):
        open_block(block)
        sum_ref[:packed] = pick(whole * CHUNK, rest)

        def piece(q, carry):
            sum_ref[:packed] += pick(pl.multiple_of(q * CHUNK, CHUNK), CHUNK)
            return carry

        lax.fori_loop(0, whole, piece, 0)
        total_ref[...] += close_block()
        return carry

    lax.fori_loop(1, blocks, other_block, 0)
    total = total_ref[...]
    own = jnp.sum(jnp.where(iota((rows, entries), 0) == offs, total, 0.0), axis=0, keepdims=True)
    own = [own[:, 128 * t : 128 * t + 128] for t in range(CAP // 2)] + [jnp.zeros((2, 128), F32)]
    extra = jnp.concatenate(
        [part[8 * t : 8 * t + 8] for t in range(4)] + [jnp.concatenate(own, axis=0), jnp.zeros((8, 128), F32)],
        axis=1,
    )
    for b in range(peers):
        out_ref[b, :deep, :] = total[b * deep : (b + 1) * deep]
        out_ref[b, deep:, :] = extra


def reply_kernel(got_ref, req_ref, rate_ref, out_ref, rate_scratch):
    peers = got_ref.shape[0]
    lines = req_ref.shape[0]
    rows = rate_ref.shape[1]
    passes = out_ref.shape[0] // (lines * TILES)
    sub = (got_ref.shape[1] - 8) // passes
    place = lax.axis_index("bus_x") * passes
    total = got_ref[0]
    for b in range(1, peers):
        total = total + got_ref[b]
    sens, rest = total[: passes * sub], total[passes * sub :]
    flows = jnp.concatenate([rest[:, 128 * t : 128 * t + 128] for t in range(4)], axis=0)
    lane = iota((HOURS, 128), 1)
    hour = iota((HOURS, 128), 0)
    f_high, f_low = split2(flows)
    f_all = jnp.concatenate([f_high, f_low], axis=0)
    req = req_ref[...]
    lane_line = iota((lines, 128), 1)
    hots = [
        jnp.where(lane_line == req[:, 32 + c : 33 + c].astype(jnp.int32) - 1, 1.0, 0.0).astype(BF16)
        for c in range(CAP)
    ]
    left = jnp.concatenate([jnp.concatenate(hots[4 * q : 4 * q + 4], axis=1) for q in range(3)], axis=0)

    def diagonal(block):
        blank = jnp.zeros_like(block)
        return jnp.concatenate(
            [jnp.concatenate([block if v == u else blank for v in range(4)], axis=1) for u in range(4)], axis=0
        )

    lost = lax.dot_general(
        left, diagonal(f_high), NT, preferred_element_type=F32
    ) + lax.dot_general(left, diagonal(f_low), NT, preferred_element_type=F32)
    rate_scratch[...] = 0.5 * jnp.transpose(jnp.broadcast_to(rate_ref[...], (rows, 128)))

    def wide(block):
        return jnp.concatenate([block, jnp.zeros((block.shape[0], 128 - lines), F32)], axis=1)

    def put(p, q, block):
        out_ref[pl.ds(p * TILES + q, lines, stride=passes * TILES), :] = block

    for p in range(passes):
        wanted = iota((128, 128), 0) == (place + p) * sub + iota((128, 128), 1) % sub
        spread = lax.dot_general(f_all, jnp.where(wanted, 1.0, 0.0).astype(BF16), NN, preferred_element_type=F32)
        spread = spread[:HOURS] + spread[HOURS:]
        spread = jnp.where(lane // sub == hour % 8, spread, 0.0)
        for t in range(4):
            row = jnp.sum(spread[8 * t : 8 * t + 8], axis=0, keepdims=True)
            put(p, t, jnp.broadcast_to(row, (lines, 128)))
        for q in range(3):
            put(p, 4 + q, lost[q * lines : (q + 1) * lines])
        rate = rate_scratch[pl.ds(pl.multiple_of((place + p) * sub, sub), sub), :]
        part = sens[p * sub : (p + 1) * sub]
        blocks = [wide(part[:, c * lines : (c + 1) * lines]) for c in range(CAP)]
        one = jnp.concatenate(blocks[:8], axis=0)
        two = jnp.concatenate(
            blocks[8:]
            + [rest[:, 512:640], pltpu.roll(rest[:, 512:640], lines, 1), rate, jnp.zeros((32, 128), F32)],
            axis=0,
        )
        put(p, 7, jnp.transpose(one)[:lines])
        put(p, 8, jnp.transpose(two)[:lines])


def screen_kernel(got_ref, table_ref, out_ref):
    slots, sub, outages = out_ref.shape
    passes = lax.axis_size("bus_z")
    lines = got_ref.shape[0] // (passes * TILES)
    place = lax.axis_index("bus_x") * passes + lax.axis_index("bus_z")
    pieces = []
    for t in range(TILES):
        block = got_ref[pl.ds(t, lines, stride=passes * TILES), :]
        for p in range(1, passes):
            block = block + got_ref[pl.ds(p * TILES + t, lines, stride=passes * TILES), :]
        high = block.astype(BF16).astype(F32)
        low = (block - high).astype(BF16).astype(F32)
        pieces.append(jnp.transpose(jnp.concatenate([high, low], axis=0)).astype(BF16))
    shared = jnp.concatenate(pieces[:4] + pieces[7:], axis=0)
    own = jnp.concatenate(pieces[4:7] + pieces[8:], axis=0)
    table = jnp.concatenate([table_ref[...], table_ref[...]], axis=1)
    named = table[:slots]
    line_row = iota((lines, 128), 0)
    lane = iota((1, 128), 1)
    outage = lane % outages
    names = jnp.zeros((lines, 128), F32)
    for s in range(slots):
        names = jnp.where(named[s : s + 1] == line_row, 1.0, names)
    earlier = iota((128, 128), 0) < iota((128, 128), 1) % outages
    rank = lax.dot_general(
        names.astype(BF16),
        jnp.where(earlier, 1.0, 0.0).astype(BF16),
        (((1,), (0,)), ((), ())),
        preferred_element_type=F32,
    )

    def hot_of(target):
        hot = jnp.where(line_row == target, 1.0, 0.0)
        turn = jnp.sum(hot * rank, axis=0, keepdims=True)
        hot = hot.astype(BF16)
        return jnp.concatenate([hot, hot], axis=0), turn

    plain = (((1,), (0,)), ((), ()))
    hot_own, turn_own = hot_of(named[0:1])
    got_own = lax.dot_general(own, hot_own, plain, preferred_element_type=F32)
    lost = jnp.zeros((HOURS, 128), F32)
    self_sens = jnp.zeros((1, 128), F32)
    for c in range(CAP):
        mine = turn_own == float(c)
        lost = jnp.where(mine, got_own[HOURS * c : HOURS * c + HOURS], lost)
        at = 448 + 8 * (c % 2) + c // 2
        self_sens = jnp.where(mine, got_own[at : at + 1], self_sens)
    divisor = jnp.maximum(1.0 - self_sens, floor_value)
    off = table[slots + 2 : slots + 3]
    live = table[slots + 3 : slots + 4]
    lost_scaled = lost
    row = iota((sub, 128), 0)
    for t in range(slots // 2):
        target = jnp.where(lane < outages, named[2 * t : 2 * t + 1], named[2 * t + 1 : 2 * t + 2])
        hot, turn = hot_of(target)
        got = lax.dot_general(shared, hot, plain, preferred_element_type=F32)
        sens = jnp.zeros((sub, 128), F32)
        for c in range(CAP):
            sens = jnp.where(turn == float(c), got[512 + sub * c : 512 + sub * c + sub], sens)
        factor = sens / divisor
        worst = jnp.zeros((sub, 128), F32)
        for h in range(HOURS):
            worst = jnp.maximum(worst, jnp.abs(got[sub * h : sub * h + sub] + factor * lost_scaled[h : h + 1]))
        result = worst / got[720:736]
        slot = 2 * t + jnp.where(lane < outages, 0, 1)
        keep = slot < live
        if t == 0:
            keep = keep & ~((slot == 0) & (row == off - place * sub))
        result = jnp.where(keep, result, 0.0)
        out_ref[2 * t] = result[:, :outages]
        out_ref[2 * t + 1] = result[:, outages:]


def call(kernel, out_shape, in_specs, scratch=(), flops=0, moved=0, limit=16):
    return pl.pallas_call(
        kernel,
        out_shape=out_shape,
        in_specs=in_specs,
        out_specs=IN_VMEM,
        scratch_shapes=list(scratch),
        compiler_params=pltpu.CompilerParams(vmem_limit_bytes=limit * 1024 * 1024),
        cost_estimate=pl.CostEstimate(flops=flops, bytes_accessed=moved, transcendentals=0),
    )


def local(shift_factors, injection, rating, monitored, live_count, outage_offset, outage_ends):
    peers = lax.axis_size("bus_x")
    passes = lax.axis_size("bus_z")
    line_count = lax.axis_size("line")
    block_rows, bus_width = shift_factors.shape
    sub_rows = block_rows // (peers * passes)
    outages, slot_count = monitored.shape
    entries = CAP * line_count
    shape = jax.ShapeDtypeStruct
    rate_row = rating.reshape(1, block_rows)
    table = jnp.concatenate(
        [monitored.T, outage_ends.T, outage_offset.reshape(1, outages), live_count.reshape(1, outages)], axis=0
    )
    with jax.named_scope("requests"):
        requests = call(request_kernel, shape((line_count, 128), F32), [IN_VMEM], flops=10**10, moved=10**7)(
            table
        )
        asked = lax.all_to_all(requests, "line", split_axis=0, concat_axis=0, tiled=True)
    with jax.named_scope("picks"):
        partial_sens = call(
            pick_kernel,
            shape((peers, passes * sub_rows + 8, entries), F32),
            [IN_VMEM] * 3,
            scratch=(
                pltpu.VMEM((128, 128), F32),
                pltpu.VMEM((PACKED, entries), BF16),
                pltpu.VMEM((PACKED, 128), jnp.int16),
                pltpu.VMEM((PACKED, 128), jnp.int16),
                pltpu.VMEM((PACKED + 2 * HOURS, 2 * block_rows), F32),
                pltpu.VMEM((block_rows, entries), F32),
            ),
            flops=4 * entries * block_rows * bus_width,
            moved=4 * block_rows * bus_width,
            limit=24,
        )(asked, shift_factors, injection)
        half_sens = lax.all_to_all(partial_sens, "bus_x", split_axis=0, concat_axis=0, tiled=True)
    with jax.named_scope("reply"):
        reply = call(
            reply_kernel,
            shape((passes * line_count * TILES, 128), F32),
            [IN_VMEM] * 3,
            scratch=(pltpu.VMEM((block_rows, block_rows), F32),),
        )(half_sens, asked, rate_row)
        reply = reply.reshape(passes * line_count, TILES * 128)
        got = lax.all_to_all(reply, ("line", "bus_z"), split_axis=0, concat_axis=0, tiled=True)
    with jax.named_scope("screen"):
        loading = call(screen_kernel, shape((slot_count, sub_rows, outages), F32), [IN_VMEM] * 2)(
            got.reshape(-1, 128), table
        )
    return jnp.transpose(loading, (2, 0, 1))


def solution(mesh):
    lines, buses = mesh.devices.shape
    bus = ("bus_x", "bus_z")
    return jax.shard_map(
        local,
        mesh=jax.sharding.Mesh(mesh.devices.reshape(lines, buses // PASS, PASS), ("line",) + bus),
        in_specs=(
            P("line", bus),
            P(None, bus),
            P("line"),
            P("line", None),
            P("line"),
            P("line"),
            P("line", None),
        ),
        out_specs=P("line", None, bus),
        check_vma=False,
    )
```
